128 devices in a mesh: dp: 16 (over y_lo, x, core), head: 8 (over z, y_hi).
Axes of the slice: x: 4, y: 4 (y_hi: 2, y_lo: 2; y = y_hi * 2 + y_lo), z: 4, core: 2. Of those that a mesh axis runs over, the one named last changes fastest.
Arguments:
- tokens: bfloat16 [16384, 1024], P(('dp', 'head')), may hold values from -6 to 6
- w_project: bfloat16 [1024, 3072], P(None, ('dp', 'head')), may hold values from -0.1875 to 0.1875
- w_attend: bfloat16 [1024, 1024], P(None, ('dp', 'head')), may hold values from -1 to 1
- first_gain: bfloat16 [1024], P(('dp', 'head')), may hold values from 0.099609375 to 1.8984375
- first_shift: bfloat16 [1024], P(('dp', 'head')), may hold values from -3 to 3
- w_expand: bfloat16 [1024, 4096], P(None, ('dp', 'head')), may hold values from -0.1875 to 0.1875
- w_reduce: bfloat16 [4096, 1024], P(None, ('dp', 'head')), may hold values from -0.09375 to 0.09375
- second_gain: bfloat16 [1024], P(('dp', 'head')), may hold values from 0.099609375 to 1.8984375
- second_shift: bfloat16 [1024], P(('dp', 'head')), may hold values from -3 to 3
- position_table: bfloat16 [512, 1024], P(None, ('dp', 'head')), may hold values from -6 to 6
- w_query: bfloat16 [1024, 1024], P('dp', 'head'), may hold values from -0.1875 to 0.1875
- w_key: bfloat16 [1024, 1024], P('dp', 'head'), may hold values from -0.1875 to 0.1875
- lengths: int32 [32], P('dp'), may hold values from 64 to 512, as said below
- cotangent: bfloat16 [16384, 1024], P(('dp', 'head')), may hold values from -24 to 24
Outputs:
- layer_output: bfloat16 [16384, 1024], P(('dp', 'head'))
- tokens_grad: bfloat16 [16384, 1024], P(('dp', 'head'))
- grad_project: float32 [1024, 3072], P(None, ('dp', 'head'))
- grad_attend: float32 [1024, 1024], P(None, ('dp', 'head'))
- grad_first_gain: float32 [1024], P(('dp', 'head'))
- grad_first_shift: float32 [1024], P(('dp', 'head'))
- grad_expand: float32 [1024, 4096], P(None, ('dp', 'head'))
- grad_reduce: float32 [4096, 1024], P(None, ('dp', 'head'))
- grad_second_gain: float32 [1024], P(('dp', 'head'))
- grad_second_shift: float32 [1024], P(('dp', 'head'))
- grad_table: float32 [512, 1024], P(None, ('dp', 'head'))
- grad_query: float32 [1024, 1024], P('dp', 'head')
- grad_key: float32 [1024, 1024], P('dp', 'head')
The draws below stay inside these ranges and needn't reach their ends.
Inputs may be any that keep to these rules, and one draw needn't show every extreme that they name: `lengths`: in each aligned block of 2 rows, one row has length 512.
All inputs are finite; a program needn't handle non-finite values.
Results may differ from the reference program's by a relative error of at most 0.02.
Values may be sent and summed in bfloat16 or wider, within the bound.
No kernel may reach another device: no remote copies, remote signals or barrier semaphores. Data moves between devices by JAX's collectives and lax.ppermute only.
A program may use at most 192 MiB of HBM per device.

```python
import math
from functools import partial
import jax
import jax.numpy as jnp
import numpy as np
from jax import lax

D = 1024
HEADS = 16
HEAD_DIM = 64
FF = 4096
SPAN = 256
SEQ = 512
MIN_LEN = 64
ROWS_GRP = 2
ROWS = 32
TOKENS = 16384


def draw_lengths(key, part):
    key = jax.random.fold_in(key, 11)
    pick_key, force_key = jax.random.split(key)
    extent = SEQ - MIN_LEN
    uniform_pick = jax.random.randint(pick_key, (ROWS,), 0, extent + 1)
    drawn = MIN_LEN + uniform_pick * (uniform_pick + 2 * extent) // (3 * extent)
    chosen = jax.random.randint(force_key, (ROWS // ROWS_GRP,), 0, ROWS_GRP)
    row_index = jnp.arange(ROWS)
    return jnp.where(row_index % ROWS_GRP == chosen[row_index // ROWS_GRP], SEQ, drawn).astype(jnp.int32)


def with_spikes(values, own_key, source, target, parts, factor):
    def block_of(axis_at):
        return (jnp.arange(values.shape[axis_at]) // (values.shape[axis_at] // parts)).reshape((-1,) + (1,) * (values.ndim - 1 - axis_at))

    near = jax.random.permutation(own_key, parts)[block_of(target)]
    far = (block_of(target) + parts // 2) % parts
    return jnp.where((block_of(source) == near) | (block_of(source) == far), factor * values, values)


def levels(own_key, shape, cuts, smallest, top_value):
    loudness, own = 1.0, jax.random.fold_in(own_key, 6)
    for dim, parts in cuts:
        steps = jnp.exp(jax.random.uniform(jax.random.fold_in(own, dim), (parts,), jnp.float32, smallest / len(cuts), top_value / len(cuts)))
        loudness = loudness * jnp.repeat(steps, shape[dim] // parts).reshape([-1 if axis == dim else 1 for axis in range(len(shape))])
    return loudness


def centred(rng, dims, spread, reach, shards=(), kind=jnp.bfloat16):
    values = spread * jax.random.normal(rng, dims, jnp.float32)
    if shards:
        values = values * levels(rng, dims, shards, -0.22, 0.18)
    return jnp.clip(values, -reach, reach).astype(kind)


def noise_with(key, shape, deviation, bound, cuts, heavy, dtype=jnp.bfloat16):
    values = deviation * jax.random.normal(key, shape, jnp.float32)
    if cuts:
        values = values * levels(key, shape, cuts, -0.22, 0.18)
    return jnp.clip(with_spikes(values, jax.random.fold_in(key, 3), *heavy), -bound, bound).astype(dtype)


def setup_inputs(seed: int = 0) -> dict:
    key_list = jax.random.split(jax.random.key(seed), 15)
    return {
        "tokens": centred(key_list[0], (TOKENS, D), 1.0, 6.0, ((0, 128),)),
        "w_project": centred(key_list[1], (D, 3 * D), D ** -0.5, 0.1875, ((1, 128),)),
        "w_attend": centred(key_list[2], (D, D), (D // 32) ** -0.5, 1.0, ((1, 128),)),
        "first_gain": jnp.clip(1.0 + 0.18 * jax.random.normal(key_list[3], (D,), jnp.float32), 0.099609375, 1.8984375).astype(jnp.bfloat16),
        "first_shift": centred(key_list[4], (D,), 0.5, 3.0, ((0, 128),)),
        "w_expand": centred(key_list[5], (D, FF), D ** -0.5, 0.1875, ((1, 128),)),
        "w_reduce": centred(key_list[6], (FF, D), FF ** -0.5, 0.09375, ((1, 128),)),
        "second_gain": jnp.clip(1.0 + 0.18 * jax.random.normal(key_list[7], (D,), jnp.float32), 0.099609375, 1.8984375).astype(jnp.bfloat16),
        "second_shift": centred(key_list[8], (D,), 0.5, 3.0, ((0, 128),)),
        "position_table": centred(key_list[9], (2 * SPAN, D), 1.0, 6.0, ((1, 128),)),
        "w_query": centred(key_list[10], (D, D), D ** -0.5, 0.1875, ((0, 16), (1, 8))),
        "w_key": centred(key_list[11], (D, D), D ** -0.5, 0.1875, ((0, 16), (1, 8))),
        "lengths": draw_lengths(jax.random.fold_in(key_list[14], 71), 0),
        "cotangent": noise_with(key_list[13], (TOKENS, D), 1.0, 24.0, ((0, 128),), (0, 1, 128, 5.5)),
    }


@jax.custom_vjp
def low(v):
    return lax.optimization_barrier(v.astype(jnp.bfloat16)).astype(jnp.float32)

@jax.custom_vjp
def low_back(v):
    return v

def low_keep(v):
    return (low(v), None)

def low_pass(kept, grad):
    return (grad,)

def back_keep(v):
    return (v, None)

def back_low(kept, grad):
    return (low(grad),)
low.defvjp(low_keep, low_pass)
low_back.defvjp(back_keep, back_low)
EPS = 1e-07
MASKED = -1e+30

def bucket_table(length, span):
    offset = np.arange(length)[:, None] - np.arange(length)[None, :]
    middle = span // 2
    absolute = np.where((offset < middle) & (offset > -middle), middle - 1, np.abs(offset))
    log_place = np.ceil(np.log(absolute / middle) / np.log((2 * span - 1) / middle) * (middle - 1)) + middle
    buckets = np.where(absolute <= middle, offset, log_place * np.sign(offset)).astype(np.int64)
    return np.clip(buckets + span, 0, 2 * span - 1).astype(np.int32)

def product(left, right):
    return jnp.dot(left, right, precision=lax.Precision.HIGHEST, preferred_element_type=jnp.float32)

def normalize(value, gain, shift):
    center = value - lax.optimization_barrier(jnp.mean(value, axis=-1, keepdims=True))
    inverse = lax.rsqrt(lax.optimization_barrier(jnp.mean(center * center, axis=-1, keepdims=True)) + EPS)
    return center * inverse * gain + shift

def attend_sequence(rel_keys, rel_queries, offset_table, pieces):
    query_rows, key_rows, values, length = pieces
    highest = lax.Precision.HIGHEST
    score_scale = 1.0 / math.sqrt(3 * HEAD_DIM)
    direct = low_back(jnp.einsum('ihd,jhd->hij', query_rows, key_rows, precision=highest))
    key_position_scores = low_back(jnp.einsum('ihd,rhd->hir', query_rows, rel_keys, precision=highest))
    query_position_scores = low_back(jnp.einsum('jhd,rhd->hjr', key_rows, rel_queries, precision=highest))
    spread_index = jnp.broadcast_to(offset_table[None], (query_rows.shape[1],) + offset_table.shape)
    gathered_key = jnp.take_along_axis(key_position_scores, spread_index, axis=2)
    gathered_query = jnp.take_along_axis(query_position_scores, spread_index, axis=2)
    logits = (direct + gathered_key + jnp.swapaxes(gathered_query, 1, 2)) * score_scale
    valid = jnp.arange(key_rows.shape[0]) < length
    logits = jnp.where(valid[None, None, :], logits, MASKED)
    weighting = low(jax.nn.softmax(logits, axis=-1))
    return low(low_back(jnp.einsum('hij,jhd->ihd', weighting, values, precision=highest)))

def forward(lengths, tokens, w_project, w_attend, first_gain, first_shift, w_expand, w_reduce, second_gain, second_shift, position_table, w_query, w_key):
    total_tok = tokens.shape[0]
    sequences = total_tok // SEQ
    offset_table = jnp.asarray(bucket_table(SEQ, SPAN))
    packed = low(low_back(product(tokens, w_project)))
    packed = packed.reshape(sequences, SEQ, 3, HEADS, HEAD_DIM)
    rel_keys = low(product(position_table, w_key)).reshape(2 * SPAN, HEADS, HEAD_DIM)
    rel_queries = low(product(position_table, w_query)).reshape(2 * SPAN, HEADS, HEAD_DIM)
    step_fn = jax.checkpoint(partial(attend_sequence, rel_keys, rel_queries, offset_table))
    context = lax.map(step_fn, (packed[:, :, 0], packed[:, :, 1], packed[:, :, 2], lengths))
    context = context.reshape(total_tok, D)
    attended = low_back(product(context, w_attend))
    first_norm = normalize(tokens + attended, first_gain, first_shift)
    inner = low_back(product(low(first_norm), w_expand))
    activ = low(jax.nn.gelu(inner, approximate=False))
    ffn = low_back(product(activ, w_reduce))
    return normalize(first_norm + ffn, second_gain, second_shift)

def reference(tokens, w_project, w_attend, first_gain, first_shift, w_expand, w_reduce, second_gain, second_shift, position_table, w_query, w_key, lengths, cotangent):
    floats = [array.astype(jnp.float32) for array in (tokens, w_project, w_attend, first_gain, first_shift, w_expand, w_reduce, second_gain, second_shift, position_table, w_query, w_key)]
    output, pullback = jax.vjp(partial(forward, lengths), *floats)
    grads = pullback(cotangent.astype(jnp.float32))
    return (output.astype(jnp.bfloat16), grads[0].astype(jnp.bfloat16), grads[1], grads[2], grads[3], grads[4], grads[5], grads[6], grads[7], grads[8], grads[9], grads[10], grads[11])
```

```python
import math

import jax
import jax.numpy as jnp
import numpy as np
from jax import lax
from jax.sharding import Mesh
from jax.sharding import PartitionSpec as P

D = 1024
HEADS = 16
HEAD_DIM = 64
FF = 4096
SPAN = 256
SEQ = 512

EPS = 1e-07
MASKED = -1e30

DP = ("yl", "x", "core")
GROUP = ("z", "yh")
COLUMN = ("yl", "x")
EVERY = DP + GROUP
CHIPS = ("z", "yh", "yl", "x")
DEVICES = ("core",) + CHIPS
bf16 = jnp.bfloat16
f32 = jnp.float32


def bucket_values(offset, span):
    middle = span // 2
    absolute = np.where((offset < middle) & (offset > -middle), middle - 1, np.abs(offset))
    log_place = (
        np.ceil(np.log(absolute / middle) / np.log((2 * span - 1) / middle) * (middle - 1)) + middle
    )
    buckets = np.where(absolute <= middle, offset, log_place * np.sign(offset)).astype(np.int64)
    return np.clip(buckets + span, 0, 2 * span - 1).astype(np.int32)


def dot_nn(left, right):
    return lax.dot_general(left, right, (((1,), (0,)), ((), ())), preferred_element_type=f32)


def dot_nt(left, right):
    return lax.dot_general(left, right, (((1,), (1,)), ((), ())), preferred_element_type=f32)


def dot_tn(left, right, precision=None):
    return lax.dot_general(
        left, right, (((0,), (0,)), ((), ())), precision=precision, preferred_element_type=f32
    )


def normalize(value, gain, shift):
    center = value - jnp.mean(value, axis=-1, keepdims=True)
    inverse = lax.rsqrt(jnp.mean(center * center, axis=-1, keepdims=True) + EPS)
    scaled = center * inverse
    return (scaled * gain + shift, scaled, inverse)


def normalize_back(incoming, scaled, inverse, gain):
    grad_scaled = incoming * gain
    middle = (
        grad_scaled
        - jnp.mean(grad_scaled, axis=-1, keepdims=True)
        - scaled * jnp.mean(grad_scaled * scaled, axis=-1, keepdims=True)
    )
    return (inverse * middle, jnp.sum(incoming * scaled, axis=0), jnp.sum(incoming, axis=0))


def smooth_gate(value):
    return jax.nn.gelu(value, approximate=False)


def skew_grid(values):
    count = values.shape[-2]
    padded = jnp.pad(values, ((0, 0), (0, 0), (0, 1)))
    flat = padded.reshape(values.shape[0], count * 2 * count)
    flat = flat[:, count - 1 : count - 1 + count * (2 * count - 1)]
    return flat.reshape(values.shape[0], count, 2 * count - 1)[:, :, :count]


def unskew_grid(values):
    count = values.shape[-1]
    padded = jnp.pad(values, ((0, 0), (0, 0), (0, count - 1)))
    flat = padded.reshape(values.shape[0], count * (2 * count - 1))
    flat = jnp.pad(flat, ((0, 0), (count - 1, 1)))
    return flat.reshape(values.shape[0], count, 2 * count)[:, :, : 2 * count - 1]


def split_sum(columns, selector):
    upper = columns.astype(bf16)
    lower = (columns - upper.astype(f32)).astype(bf16)
    return jnp.einsum("him,mr->hir", upper, selector, preferred_element_type=f32) + jnp.einsum(
        "him,mr->hir", lower, selector, preferred_element_type=f32
    )


def bucket_sums(grid, leftmost_distance, far_right):
    count = grid.shape[-1]
    middle = SPAN // 2
    columns = unskew_grid(grid)
    near_part = columns[:, :, count - 1 - middle : count + middle][:, :, ::-1]
    high_part = split_sum(columns[:, :, : count - 1 - middle], leftmost_distance)
    low_part = split_sum(columns[:, :, count + middle :], far_right)
    return jnp.concatenate([low_part, near_part, high_part], axis=-1)


def attention_logits(query, key, relative_key_rows, relative_query_rows, lengths, scale):
    direct = jnp.einsum("bid,bjd->bij", query, key, preferred_element_type=f32)
    by_key = jnp.einsum("bid,fd->bif", query, relative_key_rows, preferred_element_type=f32)
    by_query = jnp.einsum("bjd,fd->bjf", key, relative_query_rows, preferred_element_type=f32)
    logits = (direct + skew_grid(by_key) + jnp.swapaxes(skew_grid(by_query), 1, 2)) * scale
    valid = jnp.arange(SEQ)[None, :] < lengths[:, None]
    return jnp.where(valid[:, None, :], logits, MASKED)


def swap(value):
    return lax.ppermute(value, "core", [(0, 1), (1, 0)])


def exchange(value, axes):
    return lax.all_to_all(value, axes, 0, 0, tiled=True)


def per_device(
    tokens,
    w_project,
    w_attend,
    first_gain,
    first_shift,
    w_expand,
    w_reduce,
    second_gain,
    second_shift,
    position_table,
    w_query,
    w_key,
    lengths,
    cotangent,
):
    core = lax.axis_index("core")
    group = lax.axis_index(GROUP)
    column = lax.axis_index(COLUMN)
    local = tokens.shape[0]
    pair = 2 * local
    scale = 1.0 / math.sqrt(3 * HEAD_DIM)
    highest = lax.Precision.HIGHEST
    middle = SPAN // 2
    column_bucket = bucket_values(SEQ - 1 - np.arange(2 * SEQ - 1), SPAN)
    column_ids = jnp.asarray(column_bucket)
    leftmost_distance = jnp.asarray(
        (
            column_bucket[: SEQ - 1 - middle][:, None]
            == np.arange(SPAN + middle + 1, 2 * SPAN)[None, :]
        ).astype(np.float32)
    ).astype(bf16)
    far_right = jnp.asarray(
        (column_bucket[SEQ + middle :][:, None] == np.arange(0, SPAN - middle)[None, :]).astype(
            np.float32
        )
    ).astype(bf16)

    def by_core(zero, one):
        return jnp.where(core == 0, zero, one)

    def both(value):
        return jnp.concatenate([value, swap(value)], axis=0)

    def give_halves(value):
        mine = by_core(value[0], value[1])
        theirs = by_core(value[1], value[0])
        got = swap(theirs)
        return mine, got

    def sum_pair(partial):
        return partial[:local] + swap(partial[local:])

    project_rows = w_project.T
    vectors = jnp.stack([first_gain, first_shift, second_gain, second_shift])
    packet = jnp.concatenate(
        [
            project_rows[:, :512],
            project_rows[:, 512:],
            position_table.T,
            jnp.pad(vectors, ((0, 4), (0, 504))),
        ],
        axis=0,
    )
    gathered = lax.all_gather(packet, DEVICES, axis=0, tiled=False)
    gathered = gathered.reshape(2, 4, 2, 2, 4, 64, 512)
    project_all = (
        gathered[..., :48, :]
        .reshape(2, 4, 2, 2, 4, 2, 24, 512)
        .transpose(3, 4, 0, 1, 2, 6, 5, 7)
        .reshape(3, 8, 2, HEAD_DIM, D)
    )
    w_heads = lax.dynamic_index_in_dim(project_all, core, axis=2, keepdims=False).reshape(1536, D)
    table_cols = gathered[..., 48:56, :].transpose(3, 4, 0, 1, 2, 5, 6).reshape(D, 2 * SPAN)
    vec = (
        gathered[..., 56:60, :8].transpose(5, 3, 4, 0, 1, 2, 6).reshape(4, D).astype(f32)
    )
    gain_one, shift_one, gain_two, shift_two = vec[0], vec[1], vec[2], vec[3]

    position_weights = lax.all_gather(
        jnp.concatenate([w_key, w_query], axis=1), DP, axis=0, tiled=True
    )
    position_weights = lax.dynamic_index_in_dim(
        position_weights.reshape(D, 2, 2, HEAD_DIM), core, axis=2, keepdims=False
    ).reshape(D, 2 * HEAD_DIM)

    reduce_rows = w_reduce.T.reshape(8, 8, 2, 256)
    mine, got = give_halves(jnp.moveaxis(reduce_rows, 2, 0).reshape(2, 8, 2048))
    reduce_rows = jnp.concatenate([by_core(mine, got), by_core(got, mine)], axis=0)
    attend_rows = w_attend.T.reshape(8, 8, 2, HEAD_DIM)
    mine, got = give_halves(jnp.moveaxis(attend_rows, 2, 0).reshape(2, 8, 512))
    attend_rows = jnp.concatenate([by_core(mine, got), by_core(got, mine)], axis=0)
    packet = jnp.concatenate(
        [w_expand.T, reduce_rows.reshape(32, D), attend_rows.reshape(8, D)], axis=0
    )
    gathered = lax.all_gather(packet, CHIPS, axis=0, tiled=False).reshape(4, 2, 2, 4, 72, D)
    expand_t = gathered[..., :32, :].transpose(2, 3, 0, 1, 4, 5).reshape(2048, D)
    reduce_t = (
        gathered[..., 32:64, :]
        .reshape(4, 2, 2, 4, 2, 8, 2048)
        .transpose(2, 3, 4, 0, 1, 5, 6)
        .reshape(D, 2048)
    )
    attend_t = (
        gathered[..., 64:, :]
        .reshape(4, 2, 2, 4, 2, 8, 512)
        .transpose(2, 3, 4, 0, 1, 5, 6)
        .reshape(D, 512)
    )

    tokens_two = both(tokens)
    packed = dot_nt(tokens_two, w_heads).astype(bf16)
    packed = packed.reshape(pair, 3, 8, HEAD_DIM).transpose(2, 0, 1, 3).reshape(8, pair, 192)
    heads_in = exchange(packed, GROUP)
    heads_in = heads_in.reshape(8, 2, local, 3, HEAD_DIM).transpose(3, 1, 0, 2, 4)
    query, key, values = heads_in.reshape(3, 4, SEQ, HEAD_DIM)
    lengths_four = jnp.concatenate([lengths, swap(lengths)], axis=0)
    rel = dot_tn(table_cols, position_weights).astype(bf16)
    rel_keys, rel_queries = rel[:, :HEAD_DIM], rel[:, HEAD_DIM:]
    relative_key_rows = rel_keys[column_ids]
    relative_query_rows = rel_queries[column_ids]
    logits = attention_logits(
        query, key, relative_key_rows, relative_query_rows, lengths_four, scale
    )
    maximum = jnp.max(logits, axis=-1, keepdims=True)
    exponent = jnp.exp(logits - maximum)
    totals = jnp.sum(exponent, axis=-1, keepdims=True)
    weighting = (exponent / totals).astype(bf16)
    context = jnp.einsum("bij,bjd->bid", weighting, values, preferred_element_type=f32).astype(bf16)
    lse = maximum + jnp.log(totals)

    context = context.reshape(2, 8, local, HEAD_DIM).transpose(1, 0, 2, 3)
    context = exchange(context.reshape(8, pair, HEAD_DIM), GROUP)
    context_two = context.transpose(1, 0, 2).reshape(pair, 512)

    attended = sum_pair(dot_nt(context_two, attend_t))
    first_norm, scaled_one, inverse_one = normalize(
        tokens.astype(f32) + attended, gain_one, shift_one
    )
    first_two = both(first_norm.astype(bf16))
    inner = dot_nt(first_two, expand_t)
    activ = smooth_gate(inner).astype(bf16)
    ffn = sum_pair(dot_nt(activ, reduce_t))
    output, scaled_two, inverse_two = normalize(first_norm + ffn, gain_two, shift_two)
    grad_resid2, grad_gain2, grad_shift2 = normalize_back(
        cotangent.astype(f32), scaled_two, inverse_two, gain_two
    )
    grad_ffn = both(grad_resid2.astype(bf16))
    grad_reduce_t = dot_tn(grad_ffn, activ).astype(bf16)
    grad_activ = dot_nn(grad_ffn, reduce_t)
    gate_value, gate_pull = jax.vjp(smooth_gate, inner)
    grad_inner = gate_pull(grad_activ)[0].astype(bf16)
    grad_expand_t = dot_tn(grad_inner, first_two).astype(bf16)
    grad_first = grad_resid2 + sum_pair(dot_nn(grad_inner, expand_t))
    grad_resid1, grad_gain1, grad_shift1 = normalize_back(
        grad_first, scaled_one, inverse_one, gain_one
    )
    grad_attended = both(grad_resid1.astype(bf16))
    grad_attend_t = dot_tn(grad_attended, context_two).astype(bf16)
    grad_context = dot_nn(grad_attended, attend_t).astype(bf16)

    grad_context = grad_context.reshape(pair, 8, HEAD_DIM).transpose(1, 0, 2)
    grad_ctx = exchange(grad_context, GROUP)
    grad_ctx = grad_ctx.reshape(8, 2, local, HEAD_DIM).transpose(1, 0, 2, 3)
    grad_ctx = grad_ctx.reshape(4, SEQ, HEAD_DIM)
    logits = attention_logits(
        query, key, relative_key_rows, relative_query_rows, lengths_four, scale
    )
    weighting = jnp.exp(logits - lse)
    grad_values = jnp.einsum(
        "bij,bid->bjd", weighting.astype(bf16), grad_ctx, preferred_element_type=f32
    )
    grad_weights = jnp.einsum("bid,bjd->bij", grad_ctx, values, preferred_element_type=f32)
    grad_logits = (
        weighting
        * (grad_weights - jnp.sum(weighting * grad_weights, axis=-1, keepdims=True))
        * scale
    )
    direct_grad = grad_logits.astype(bf16)
    by_key_grad = bucket_sums(grad_logits, leftmost_distance, far_right).astype(bf16)
    by_query_grad = bucket_sums(
        jnp.swapaxes(grad_logits, 1, 2), leftmost_distance, far_right
    ).astype(bf16)
    grad_queries = jnp.einsum(
        "bij,bjd->bid", direct_grad, key, preferred_element_type=f32
    ) + jnp.einsum("bir,rd->bid", by_key_grad, rel_keys, preferred_element_type=f32)
    grad_keys = jnp.einsum(
        "bij,bid->bjd", direct_grad, query, preferred_element_type=f32
    ) + jnp.einsum("bjr,rd->bjd", by_query_grad, rel_queries, preferred_element_type=f32)
    key_acc = jnp.einsum("bir,bid->rd", by_key_grad, query, preferred_element_type=f32)
    query_acc = jnp.einsum("bjr,bjd->rd", by_query_grad, key, preferred_element_type=f32)
    grad_stack = jnp.stack([grad_queries, grad_keys, grad_values], axis=2).astype(bf16)

    grad_stack = grad_stack.reshape(2, 8, local, 192).transpose(1, 0, 2, 3)
    grad_packed = exchange(grad_stack.reshape(8, pair, 192), GROUP)
    grad_packed = grad_packed.reshape(8, pair, 3, HEAD_DIM).transpose(1, 2, 0, 3)
    grad_packed = grad_packed.reshape(pair, 1536)
    tokens_grad = grad_resid1 + sum_pair(dot_nn(grad_packed, w_heads))

    def scatter(blocks):
        received = exchange(blocks, CHIPS)
        return jnp.sum(received.astype(f32), axis=0)

    def owners(rows, count):
        return jnp.swapaxes(rows, 0, 1).reshape(64, count, D)

    expand_blocks = owners(grad_expand_t.reshape(8, 8, 32 * D), 32)
    reduce_blocks = owners(
        grad_reduce_t.reshape(8, 2, 8, 8 * 2048).transpose(0, 2, 1, 3), 32
    )
    attend_blocks = owners(grad_attend_t.reshape(8, 2, 8, 8 * 512).transpose(0, 2, 1, 3), 8)
    summed = scatter(jnp.concatenate([expand_blocks, reduce_blocks, attend_blocks], axis=1))
    grad_expand = summed[:32].T
    mine, got = give_halves(summed[32:64].reshape(2, 8, 2048))
    grad_reduce = jnp.stack(
        [by_core(mine, got).reshape(8, 8, 256), by_core(got, mine).reshape(8, 8, 256)], axis=2
    )
    grad_reduce = grad_reduce.reshape(8, FF).T
    mine, got = give_halves(summed[64:].reshape(2, 8, 512))
    grad_attend = jnp.stack(
        [by_core(mine, got).reshape(8, 8, HEAD_DIM), by_core(got, mine).reshape(8, 8, HEAD_DIM)],
        axis=2,
    )
    grad_attend = grad_attend.reshape(8, D).T

    triples = grad_packed.reshape(pair, 8, 3, HEAD_DIM)
    triples = by_core(triples[:, :, (0, 2, 1)], triples[:, :, (1, 0, 2)])
    grad_project_t = dot_tn(triples.reshape(pair, 1536), tokens_two).astype(bf16)
    project_sum = scatter(owners(grad_project_t.reshape(8, 8, 24 * D), 24))
    from_partner = swap(project_sum)
    unit = (3 * group + np.arange(24) // 8) // 8
    grad_project = jnp.where((unit % 2 == 0)[:, None], project_sum, from_partner).T

    vectors = jnp.stack([grad_gain1, grad_shift1, grad_gain2, grad_shift2])
    vectors = vectors.reshape(4, 128, 8).transpose(1, 0, 2).reshape(128, 1, 32)
    vectors = jnp.sum(exchange(vectors, EVERY), axis=0).reshape(4, 8)

    rel_grad = jnp.concatenate([key_acc, query_acc], axis=1).astype(bf16)
    rel_grad = exchange(jnp.broadcast_to(rel_grad[None], (8, 2 * SPAN, 2 * HEAD_DIM)), COLUMN)
    rel_grad = jnp.sum(rel_grad.astype(f32), axis=0)
    other = swap(rel_grad)
    first, second = by_core(rel_grad, other), by_core(other, rel_grad)
    table_own = lax.dynamic_slice_in_dim(table_cols, 64 * (2 * column + core), 64, axis=0)
    table_own = table_own.astype(f32)
    grad_key = jnp.dot(
        table_own,
        jnp.concatenate([first[:, :HEAD_DIM], second[:, :HEAD_DIM]], axis=1),
        precision=highest,
    )
    grad_query = jnp.dot(
        table_own,
        jnp.concatenate([first[:, HEAD_DIM:], second[:, HEAD_DIM:]], axis=1),
        precision=highest,
    )
    weights_own = lax.dynamic_slice_in_dim(position_weights, 128 * column, 128, axis=0)
    table_part = lax.dot_general(
        weights_own.astype(f32), rel_grad, (((1,), (1,)), ((), ())), precision=highest
    ).astype(bf16)
    table_part = table_part.reshape(2, 8, 8, 2 * SPAN).transpose(1, 0, 2, 3)
    table_part = jnp.sum(exchange(table_part, GROUP).astype(f32), axis=0)
    mine, got = give_halves(table_part)
    grad_table = (mine + got).T

    return (
        output.astype(bf16),
        tokens_grad.astype(bf16),
        grad_project,
        grad_attend,
        vectors[0],
        vectors[1],
        grad_expand,
        grad_reduce,
        vectors[2],
        vectors[3],
        grad_table,
        grad_query,
        grad_key,
    )


def solution(mesh):
    parts = Mesh(mesh.devices.reshape(2, 4, 2, 4, 2), EVERY)
    in_specs = (
        P(EVERY, None),
        P(None, EVERY),
        P(None, EVERY),
        P(EVERY),
        P(EVERY),
        P(None, EVERY),
        P(None, EVERY),
        P(EVERY),
        P(EVERY),
        P(None, EVERY),
        P(DP, GROUP),
        P(DP, GROUP),
        P(DP),
        P(EVERY, None),
    )
    out_specs = (
        P(EVERY, None),
        P(EVERY, None),
        P(None, EVERY),
        P(None, EVERY),
        P(EVERY),
        P(EVERY),
        P(None, EVERY),
        P(None, EVERY),
        P(EVERY),
        P(EVERY),
        P(None, EVERY),
        P(DP, GROUP),
        P(DP, GROUP),
    )
    return jax.shard_map(
        per_device, mesh=parts, in_specs=in_specs, out_specs=out_specs, check_vma=False
    )
```

```python
import math

import jax
import jax.numpy as jnp
import numpy as np
from jax import lax
from jax.experimental import pallas as pl
from jax.experimental.pallas import tpu as pltpu
from jax.sharding import Mesh
from jax.sharding import PartitionSpec as P

D = 1024
HEADS = 16
HEAD_DIM = 64
FF = 4096
SPAN = 256
SEQ = 512
BLOCK = 128
WINDOW = SEQ + BLOCK

EPS = 1e-07
MASKED = -1e30

DP = ("yl", "x", "core")
GROUP = ("z", "yh")
COLUMN = ("yl", "x")
EVERY = DP + GROUP
CHIPS = ("z", "yh", "yl", "x")
DEVICES = ("core",) + CHIPS
bf16 = jnp.bfloat16
f32 = jnp.float32


def bucket_values(offset, span):
    middle = span // 2
    absolute = np.where((offset < middle) & (offset > -middle), middle - 1, np.abs(offset))
    log_place = (
        np.ceil(np.log(absolute / middle) / np.log((2 * span - 1) / middle) * (middle - 1)) + middle
    )
    buckets = np.where(absolute <= middle, offset, log_place * np.sign(offset)).astype(np.int64)
    return np.clip(buckets + span, 0, 2 * span - 1).astype(np.int32)


def normalize(value, gain, shift):
    center = value - jnp.mean(value, axis=-1, keepdims=True)
    inverse = lax.rsqrt(jnp.mean(center * center, axis=-1, keepdims=True) + EPS)
    scaled = center * inverse
    return (scaled * gain + shift, scaled, inverse)


def normalize_back(incoming, scaled, inverse, gain):
    grad_scaled = incoming * gain
    middle = (
        grad_scaled
        - jnp.mean(grad_scaled, axis=-1, keepdims=True)
        - scaled * jnp.mean(grad_scaled * scaled, axis=-1, keepdims=True)
    )
    return inverse * middle


def smooth_gate(value):
    return jax.nn.gelu(value, approximate=False)


def dot_nn(left, right):
    return lax.dot_general(left, right, (((1,), (0,)), ((), ())), preferred_element_type=f32)


def dot_nt(left, right):
    return lax.dot_general(left, right, (((1,), (1,)), ((), ())), preferred_element_type=f32)


def dot_tn(left, right):
    return lax.dot_general(left, right, (((0,), (0,)), ((), ())), preferred_element_type=f32)


def window(block):
    start = SEQ - BLOCK - BLOCK * block
    return slice(start, start + WINDOW)


def rows(block):
    return slice(BLOCK * block, BLOCK * (block + 1))


def skew(values):
    return pltpu.roll(values, SEQ + 1, 1, stride=1, stride_axis=0)[:, :SEQ]


def unskew(values):
    wide = jnp.concatenate([values, jnp.zeros((BLOCK, BLOCK), f32)], axis=1)
    return pltpu.roll(wide, 0, 1, stride=1, stride_axis=0)


def one_head(value, head):
    lane = lax.broadcasted_iota(jnp.int32, value.shape, 1)
    return jnp.where(lane // HEAD_DIM == head, value, jnp.zeros_like(value))


def query_bias(key, rel_queries, bias):
    for block in range(SEQ // BLOCK):
        by_offset = dot_nt(key[rows(block)], rel_queries[window(block)])
        bias[:, rows(block)] = skew(by_offset).T


def probabilities(query, key, rel_keys, bias, block, length):
    part = query[rows(block)]
    logits = dot_nt(part, key) + skew(dot_nt(part, rel_keys[window(block)])) + bias[rows(block)]
    logits = logits * (1.0 / math.sqrt(3 * HEAD_DIM))
    column = lax.broadcasted_iota(jnp.int32, logits.shape, 1)
    logits = jnp.where(column < length, logits, MASKED)
    exponent = jnp.exp(logits - jnp.max(logits, axis=1, keepdims=True))
    return exponent / jnp.sum(exponent, axis=1, keepdims=True)


def attend_kernel(lengths, heads_in, rel, context, bias):
    length = lengths[pl.program_id(0)]
    query, key, values = (heads_in[:, part].reshape(SEQ, 128) for part in range(3))
    rel_keys, rel_queries = rel[:, :128], rel[:, 128:]
    total = [jnp.zeros((BLOCK, 128), f32) for _ in range(SEQ // BLOCK)]
    for head in range(2):
        query_h, key_h, values_h = (one_head(part, head) for part in (query, key, values))
        query_bias(key_h, rel_queries, bias)
        for block in range(SEQ // BLOCK):
            probs = probabilities(query_h, key, rel_keys, bias, block, length)
            total[block] = total[block] + dot_nn(probs.astype(bf16), values_h)
    for block in range(SEQ // BLOCK):
        context[block] = total[block].astype(bf16)


def attend_back_kernel(lengths, heads_in, rel, grad_context, grads, grad_rel, bias, probs_ref, grad_ref):
    length = lengths[pl.program_id(0)]
    query, key, values = (heads_in[:, part].reshape(SEQ, 128) for part in range(3))
    grad_ctx = grad_context[...].reshape(SEQ, 128)
    rel_keys, rel_queries = rel[:, :128], rel[:, 128:]
    blocks = SEQ // BLOCK
    first = lax.broadcasted_iota(jnp.int32, (BLOCK, BLOCK), 0)
    second = lax.broadcasted_iota(jnp.int32, (BLOCK, BLOCK), 1)
    mirror = jnp.where(first + second == BLOCK - 1, 1.0, 0.0).astype(bf16)

    @pl.when(pl.program_id(0) == 0)
    def _():
        grad_rel[...] = jnp.zeros_like(grad_rel)

    grad_q, grad_k, grad_v = ([0.0] * blocks for _ in range(3))
    for head in range(2):
        query_h, key_h, ctx_h = (one_head(part, head) for part in (query, key, grad_ctx))
        rel_keys_h, rel_queries_h = one_head(rel_keys, head), one_head(rel_queries, head)
        query_bias(key_h, rel_queries, bias)
        for block in range(blocks):
            probs = probabilities(query_h, key, rel_keys, bias, block, length)
            probs_ref[rows(block)] = probs.astype(bf16)
            grad_probs = dot_nt(ctx_h[rows(block)], values)
            inner = jnp.sum(probs * grad_probs, axis=1, keepdims=True)
            grad = (probs * (grad_probs - inner) * (1.0 / math.sqrt(3 * HEAD_DIM))).astype(bf16)
            grad_ref[rows(block)] = grad
            by_offset = unskew(dot_nn(mirror, grad)).astype(bf16)
            by_offset = dot_nn(mirror, by_offset).astype(bf16)
            grad_q[block] += dot_nn(grad, key_h) + dot_nn(by_offset, rel_keys_h[window(block)])
            grad_rel[window(block), :128] += dot_tn(by_offset, query_h[rows(block)])
        for block in range(blocks):
            grad = grad_ref[:, rows(block)]
            by_offset = unskew(dot_nt(mirror, grad)).astype(bf16)
            by_offset = dot_nn(mirror, by_offset).astype(bf16)
            grad_k[block] += dot_tn(grad, query_h) + dot_nn(by_offset, rel_queries_h[window(block)])
            grad_v[block] += dot_tn(probs_ref[:, rows(block)], ctx_h)
            grad_rel[window(block), 128:] += dot_tn(by_offset, key_h[rows(block)])
    for block in range(blocks):
        grads[block, 0] = grad_q[block].astype(bf16)
        grads[block, 1] = grad_k[block].astype(bf16)
        grads[block, 2] = grad_v[block].astype(bf16)


def attend(lengths, heads_in, rel):
    return pl.pallas_call(
        attend_kernel,
        grid=(2,),
        in_specs=[
            pl.BlockSpec(memory_space=pltpu.SMEM),
            pl.BlockSpec((4, 3, 128, 128), lambda row: (row, 0, 0, 0)),
            pl.BlockSpec((2 * SEQ, 256), lambda row: (0, 0)),
        ],
        out_specs=pl.BlockSpec((4, 128, 128), lambda row: (row, 0, 0)),
        out_shape=jax.ShapeDtypeStruct((8, 128, 128), bf16),
        scratch_shapes=[pltpu.VMEM((SEQ, SEQ), f32)],
        compiler_params=pltpu.CompilerParams(vmem_limit_bytes=48 * 2**20),
        name="attend",
    )(lengths, heads_in, rel)


def attend_back(lengths, heads_in, rel, grad_context):
    return pl.pallas_call(
        attend_back_kernel,
        grid=(2,),
        in_specs=[
            pl.BlockSpec(memory_space=pltpu.SMEM),
            pl.BlockSpec((4, 3, 128, 128), lambda row: (row, 0, 0, 0)),
            pl.BlockSpec((2 * SEQ, 256), lambda row: (0, 0)),
            pl.BlockSpec((4, 128, 128), lambda row: (row, 0, 0)),
        ],
        out_specs=[
            pl.BlockSpec((4, 3, 128, 128), lambda row: (row, 0, 0, 0)),
            pl.BlockSpec((2 * SEQ, 256), lambda row: (0, 0)),
        ],
        out_shape=[
            jax.ShapeDtypeStruct((8, 3, 128, 128), bf16),
            jax.ShapeDtypeStruct((2 * SEQ, 256), f32),
        ],
        scratch_shapes=[
            pltpu.VMEM((SEQ, SEQ), f32),
            pltpu.VMEM((SEQ, SEQ), bf16),
            pltpu.VMEM((SEQ, SEQ), bf16),
        ],
        compiler_params=pltpu.CompilerParams(vmem_limit_bytes=48 * 2**20),
        name="attend_back",
    )(lengths, heads_in, rel, grad_context)


def swap(value):
    return lax.ppermute(value, "core", [(0, 1), (1, 0)])


def exchange(value, axes):
    return lax.all_to_all(value, axes, 0, 0, tiled=True)


def per_device(
    tokens,
    w_project,
    w_attend,
    first_gain,
    first_shift,
    w_expand,
    w_reduce,
    second_gain,
    second_shift,
    position_table,
    w_query,
    w_key,
    lengths,
    cotangent,
):
    core = lax.axis_index("core")
    column = lax.axis_index(COLUMN)
    local = tokens.shape[0]
    pair = 2 * local
    highest = lax.Precision.HIGHEST
    column_bucket = bucket_values(SEQ - 1 - np.arange(2 * SEQ - 1), SPAN)
    column_ids = jnp.asarray(np.append(column_bucket, 0))
    fold = np.append(column_bucket, -1)[None, :] == np.arange(2 * SPAN)[:, None]
    fold = jnp.asarray(fold.astype(np.float32)).astype(bf16)

    def by_core(zero, one):
        return jnp.where(core == 0, zero, one)

    def in_order(mine, theirs):
        return by_core(mine, theirs), by_core(theirs, mine)

    def both(value):
        return jnp.concatenate([value, swap(value)], axis=0)

    def sum_pair(partial):
        got = swap(partial)
        return partial + jnp.concatenate([got[local:], got[:local]], axis=0)

    vectors = jnp.stack([first_gain, first_shift, second_gain, second_shift])
    packet = jnp.concatenate(
        [
            w_project.T,
            position_table.T.reshape(4, D),
            jnp.pad(vectors, ((0, 0), (0, D - 8))),
        ],
        axis=0,
    )
    gathered = lax.all_gather(packet, DEVICES, axis=0, tiled=False).reshape(2, 8, 8, 32, D)
    project_t = gathered[..., :24, :].transpose(2, 0, 1, 3, 4).reshape(3 * D, D)
    table_t = gathered[..., 24:28, :].transpose(2, 0, 1, 3, 4).reshape(D, 2 * SPAN)
    vec = gathered[..., 28:, :8].transpose(3, 2, 0, 1, 4).reshape(4, D).astype(f32)
    gain_one, shift_one, gain_two, shift_two = vec[0], vec[1], vec[2], vec[3]

    position_weights = lax.all_gather(
        jnp.concatenate([w_key, w_query], axis=1), DP, axis=0, tiled=True
    )

    reduce_rows = jnp.moveaxis(w_reduce.T.reshape(8, 8, 2, 256), 2, 0).reshape(2, 8, 2048)
    mine, theirs = in_order(reduce_rows[0], reduce_rows[1])
    reduce_rows = jnp.concatenate(in_order(mine, swap(theirs)), axis=0)
    attend_rows = w_attend.T
    attend_rows = jnp.concatenate(in_order(attend_rows, swap(attend_rows)), axis=0)
    packet = jnp.concatenate(
        [w_expand.T, reduce_rows[:, :D], reduce_rows[:, D:], attend_rows], axis=0
    )
    gathered = lax.all_gather(packet, CHIPS, axis=0, tiled=False).reshape(8, 8, 80, D)
    expand_t = gathered[..., :32, :].transpose(1, 0, 2, 3).reshape(2048, D)
    reduce_t = (
        gathered[..., 32:64, :]
        .reshape(8, 8, 2, 2, 8, D)
        .transpose(1, 3, 0, 4, 2, 5)
        .reshape(D, 2048)
    )
    attend_t = (
        gathered[..., 64:, :].reshape(8, 8, 2, 8, D).transpose(1, 2, 0, 3, 4).reshape(D, D)
    )

    packed = dot_nt(tokens, project_t).astype(bf16)
    heads_in = exchange(packed.reshape(local, 3, 8, 128).transpose(2, 1, 0, 3), GROUP)
    rel = dot_tn(table_t, position_weights).astype(bf16)[column_ids]
    context = exchange(attend(lengths, heads_in, rel), GROUP)
    context = context.transpose(1, 0, 2).reshape(local, D)
    halves = in_order(context[:, :512], context[:, 512:])
    context_half = jnp.concatenate([halves[0], swap(halves[1])], axis=0)
    tokens_two = both(tokens)
    cotangent_two = both(cotangent).astype(f32)

    resid1 = both(tokens.astype(f32) + dot_nt(context, attend_t))
    first_norm, scaled_one, inverse_one = normalize(resid1, gain_one, shift_one)
    first_two = first_norm.astype(bf16)
    inner = dot_nt(first_two, expand_t)
    activ = smooth_gate(inner).astype(bf16)
    ffn = sum_pair(dot_nt(activ, reduce_t))
    output, scaled_two, inverse_two = normalize(first_norm + ffn, gain_two, shift_two)
    grad_resid2 = normalize_back(cotangent_two, scaled_two, inverse_two, gain_two)
    grad_gain2 = jnp.sum((cotangent_two * scaled_two)[:local], axis=0)
    grad_shift2 = jnp.sum(cotangent_two[:local], axis=0)
    grad_ffn = grad_resid2.astype(bf16)
    grad_reduce_t = dot_tn(grad_ffn, activ).astype(bf16)
    grad_activ = dot_nn(grad_ffn, reduce_t)
    gate_value, gate_pull = jax.vjp(smooth_gate, inner)
    grad_inner = gate_pull(grad_activ)[0].astype(bf16)
    grad_expand_t = dot_tn(grad_inner, first_two).astype(bf16)
    grad_first = grad_resid2 + sum_pair(dot_nn(grad_inner, expand_t))
    grad_resid1 = normalize_back(grad_first, scaled_one, inverse_one, gain_one)
    grad_gain1 = jnp.sum((grad_first * scaled_one)[:local], axis=0)
    grad_shift1 = jnp.sum(grad_first[:local], axis=0)
    grad_attended = grad_resid1.astype(bf16)
    grad_attend_t = dot_tn(grad_attended, context_half).astype(bf16)
    grad_context = dot_nn(grad_attended[:local], attend_t).astype(bf16)

    def scatter(blocks):
        received = exchange(blocks, COLUMN + GROUP)
        return jnp.sum(received.astype(f32), axis=0)

    grad_ctx = exchange(grad_context.reshape(local, 8, 128).transpose(1, 0, 2), GROUP)
    expand_sum = scatter(grad_expand_t.reshape(64, 32, D))
    reduce_blocks = grad_reduce_t.reshape(8, 2, 8, 8, 2048).transpose(0, 2, 1, 3, 4)
    reduce_sum = scatter(reduce_blocks.reshape(64, 16, 2048))
    attend_blocks = grad_attend_t.reshape(8, 2, 8, 8, 512).transpose(0, 2, 1, 3, 4)
    attend_sum = scatter(attend_blocks.reshape(64, 16, 512))

    grads, rel_grad = attend_back(lengths, heads_in, rel, grad_ctx)
    grad_packed = exchange(grads, GROUP).transpose(2, 1, 0, 3).reshape(local, 3 * D)
    tokens_grad = grad_resid1[:local] + dot_nn(grad_packed, project_t)
    grad_own = lax.dynamic_index_in_dim(
        both(grad_packed).reshape(pair, 8, 2, 192), core, axis=2, keepdims=False
    )
    grad_project_t = dot_tn(grad_own.reshape(pair, 1536), tokens_two).astype(bf16)
    grad_project = scatter(grad_project_t.reshape(64, 24, D)).T

    grad_expand = expand_sum.T
    mine, theirs = in_order(reduce_sum[:8], reduce_sum[8:])
    parts = in_order(mine, swap(theirs))
    grad_reduce = jnp.stack([part.reshape(8, 8, 256) for part in parts], axis=2)
    grad_reduce = grad_reduce.reshape(8, FF).T
    mine, theirs = in_order(attend_sum[:8], attend_sum[8:])
    grad_attend = jnp.concatenate(in_order(mine, swap(theirs)), axis=1).T

    vectors = jnp.stack([grad_gain1, grad_shift1, grad_gain2, grad_shift2])
    vectors = vectors.reshape(4, 128, 8).transpose(1, 0, 2).reshape(128, 1, 32)
    vectors = jnp.sum(exchange(vectors, EVERY), axis=0).reshape(4, 8)

    upper = rel_grad.astype(bf16)
    lower = (rel_grad - upper.astype(f32)).astype(bf16)
    rel_grad = dot_nn(fold, upper) + dot_nn(fold, lower)
    rel_grad = rel_grad + swap(rel_grad)
    rel_grad = by_core(rel_grad[:, :128], rel_grad[:, 128:]).astype(bf16)
    rel_grad = exchange(jnp.broadcast_to(rel_grad[None], (8, 2 * SPAN, 128)), COLUMN)
    rel_grad = jnp.sum(rel_grad.astype(f32), axis=0)
    rel_key_grad, rel_query_grad = in_order(rel_grad, swap(rel_grad))
    own = 64 * (2 * column + core)
    table_own = lax.dynamic_slice_in_dim(table_t, own, 64, axis=0).astype(f32)
    grad_key = jnp.dot(table_own, rel_key_grad, precision=highest)
    grad_query = jnp.dot(table_own, rel_query_grad, precision=highest)
    weights_own = lax.dynamic_slice_in_dim(position_weights, own, 64, axis=0).astype(f32)
    table_part = lax.dot_general(
        weights_own,
        jnp.concatenate([rel_key_grad, rel_query_grad], axis=1),
        (((1,), (1,)), ((), ())),
        precision=highest,
    )
    grad_table = jnp.sum(exchange(table_part.reshape(8, 8, 2 * SPAN), GROUP), axis=0).T

    return (
        output[:local].astype(bf16),
        tokens_grad.astype(bf16),
        grad_project,
        grad_attend,
        vectors[0],
        vectors[1],
        grad_expand,
        grad_reduce,
        vectors[2],
        vectors[3],
        grad_table,
        grad_query,
        grad_key,
    )


def solution(mesh):
    parts = Mesh(mesh.devices.reshape(2, 4, 2, 4, 2), EVERY)
    in_specs = (
        P(EVERY, None),
        P(None, EVERY),
        P(None, EVERY),
        P(EVERY),
        P(EVERY),
        P(None, EVERY),
        P(None, EVERY),
        P(EVERY),
        P(EVERY),
        P(None, EVERY),
        P(DP, GROUP),
        P(DP, GROUP),
        P(DP),
        P(EVERY, None),
    )
    out_specs = (
        P(EVERY, None),
        P(EVERY, None),
        P(None, EVERY),
        P(None, EVERY),
        P(EVERY),
        P(EVERY),
        P(None, EVERY),
        P(None, EVERY),
        P(EVERY),
        P(EVERY),
        P(None, EVERY),
        P(DP, GROUP),
        P(DP, GROUP),
    )
    return jax.shard_map(
        per_device, mesh=parts, in_specs=in_specs, out_specs=out_specs, check_vma=False
    )
```

```python
import math

import jax
import jax.numpy as jnp
import numpy as np
from jax import lax
from jax.experimental import pallas as pl
from jax.experimental.pallas import tpu as pltpu
from jax.sharding import Mesh
from jax.sharding import PartitionSpec as P

D = 1024
HEADS = 16
HEAD_DIM = 64
FF = 4096
SPAN = 256
SEQ = 512
BLOCK = 128
WINDOW = SEQ + BLOCK

EPS = 1e-07
MASKED = -1e30

DP = ("yl", "x", "core")
GROUP = ("z", "yh")
COLUMN = ("yl", "x")
EVERY = DP + GROUP
CHIPS = ("z", "yh", "yl", "x")
DEVICES = ("core",) + CHIPS
bf16 = jnp.bfloat16
f32 = jnp.float32


def bucket_values(offset, span):
    middle = span // 2
    absolute = np.where((offset < middle) & (offset > -middle), middle - 1, np.abs(offset))
    log_place = (
        np.ceil(np.log(absolute / middle) / np.log((2 * span - 1) / middle) * (middle - 1)) + middle
    )
    buckets = np.where(absolute <= middle, offset, log_place * np.sign(offset)).astype(np.int64)
    return np.clip(buckets + span, 0, 2 * span - 1).astype(np.int32)


def normalize(value, gain, shift):
    center = value - jnp.mean(value, axis=-1, keepdims=True)
    inverse = lax.rsqrt(jnp.mean(center * center, axis=-1, keepdims=True) + EPS)
    scaled = center * inverse
    return (scaled * gain + shift, scaled, inverse)


def normalize_back(incoming, scaled, inverse, gain):
    grad_scaled = incoming * gain
    middle = (
        grad_scaled
        - jnp.mean(grad_scaled, axis=-1, keepdims=True)
        - scaled * jnp.mean(grad_scaled * scaled, axis=-1, keepdims=True)
    )
    return inverse * middle


def dot_nn(left, right):
    return lax.dot_general(left, right, (((1,), (0,)), ((), ())), preferred_element_type=f32)


def dot_nt(left, right):
    return lax.dot_general(left, right, (((1,), (1,)), ((), ())), preferred_element_type=f32)


def dot_tn(left, right):
    return lax.dot_general(left, right, (((0,), (0,)), ((), ())), preferred_element_type=f32)


def window(block):
    start = SEQ - BLOCK - BLOCK * block
    return slice(start, start + WINDOW)


def rows(block):
    return slice(BLOCK * block, BLOCK * (block + 1))


def skew(values):
    return pltpu.roll(values, SEQ + 1, 1, stride=1, stride_axis=0)[:, :SEQ]


def unskew(values):
    wide = jnp.concatenate([values, jnp.zeros((BLOCK, BLOCK), f32)], axis=1)
    return pltpu.roll(wide, 0, 1, stride=1, stride_axis=0)


def one_head(value, head):
    lane = lax.broadcasted_iota(jnp.int32, value.shape, 1)
    return jnp.where(lane // HEAD_DIM == head, value, jnp.zeros_like(value))


def query_bias(key, rel_queries, bias):
    for block in range(SEQ // BLOCK):
        by_offset = dot_nt(key[rows(block)], rel_queries[window(block)])
        bias[:, rows(block)] = skew(by_offset).T


def probabilities(query, key, rel_keys, bias, block, length):
    part = query[rows(block)]
    logits = dot_nt(part, key) + skew(dot_nt(part, rel_keys[window(block)])) + bias[rows(block)]
    logits = logits * (1.0 / math.sqrt(3 * HEAD_DIM))
    column = lax.broadcasted_iota(jnp.int32, logits.shape, 1)
    logits = jnp.where(column < length, logits, MASKED)
    exponent = jnp.exp(logits - jnp.max(logits, axis=1, keepdims=True))
    return exponent / jnp.sum(exponent, axis=1, keepdims=True)


def attend_kernel(lengths, heads_in, rel, context, bias):
    length = lengths[pl.program_id(0)]
    query, key, values = (heads_in[:, part].reshape(SEQ, 128) for part in range(3))
    rel_keys, rel_queries = rel[:, :128], rel[:, 128:]
    total = [jnp.zeros((BLOCK, 128), f32) for _ in range(SEQ // BLOCK)]
    for head in range(2):
        query_h, key_h, values_h = (one_head(part, head) for part in (query, key, values))
        query_bias(key_h, rel_queries, bias)
        for block in range(SEQ // BLOCK):
            probs = probabilities(query_h, key, rel_keys, bias, block, length)
            total[block] = total[block] + dot_nn(probs.astype(bf16), values_h)
    for block in range(SEQ // BLOCK):
        context[block] = total[block].astype(bf16)


def attend_back_kernel(lengths, heads_in, rel, grad_context, grads, grad_rel, bias, probs_ref, grad_ref):
    length = lengths[pl.program_id(0)]
    query, key, values = (heads_in[:, part].reshape(SEQ, 128) for part in range(3))
    grad_ctx = grad_context[...].reshape(SEQ, 128)
    rel_keys, rel_queries = rel[:, :128], rel[:, 128:]
    blocks = SEQ // BLOCK
    first = lax.broadcasted_iota(jnp.int32, (BLOCK, BLOCK), 0)
    second = lax.broadcasted_iota(jnp.int32, (BLOCK, BLOCK), 1)
    mirror = jnp.where(first + second == BLOCK - 1, 1.0, 0.0).astype(bf16)

    @pl.when(pl.program_id(0) == 0)
    def _():
        grad_rel[...] = jnp.zeros_like(grad_rel)

    grad_q, grad_k, grad_v = ([0.0] * blocks for _ in range(3))
    for head in range(2):
        query_h, key_h, ctx_h = (one_head(part, head) for part in (query, key, grad_ctx))
        rel_keys_h, rel_queries_h = one_head(rel_keys, head), one_head(rel_queries, head)
        query_bias(key_h, rel_queries, bias)
        for block in range(blocks):
            probs = probabilities(query_h, key, rel_keys, bias, block, length)
            probs_ref[rows(block)] = probs.astype(bf16)
            grad_probs = dot_nt(ctx_h[rows(block)], values)
            inner = jnp.sum(probs * grad_probs, axis=1, keepdims=True)
            grad = (probs * (grad_probs - inner) * (1.0 / math.sqrt(3 * HEAD_DIM))).astype(bf16)
            grad_ref[rows(block)] = grad
            by_offset = unskew(dot_nn(mirror, grad)).astype(bf16)
            by_offset = dot_nn(mirror, by_offset).astype(bf16)
            grad_q[block] += dot_nn(grad, key_h) + dot_nn(by_offset, rel_keys_h[window(block)])
            grad_rel[window(block), :128] += dot_tn(by_offset, query_h[rows(block)])
        for block in range(blocks):
            grad = grad_ref[:, rows(block)]
            by_offset = unskew(dot_nt(mirror, grad)).astype(bf16)
            by_offset = dot_nn(mirror, by_offset).astype(bf16)
            grad_k[block] += dot_tn(grad, query_h) + dot_nn(by_offset, rel_queries_h[window(block)])
            grad_v[block] += dot_tn(probs_ref[:, rows(block)], ctx_h)
            grad_rel[window(block), 128:] += dot_tn(by_offset, key_h[rows(block)])
    for block in range(blocks):
        grads[block, 0] = grad_q[block].astype(bf16)
        grads[block, 1] = grad_k[block].astype(bf16)
        grads[block, 2] = grad_v[block].astype(bf16)


def attend(lengths, heads_in, rel):
    return pl.pallas_call(
        attend_kernel,
        grid=(2,),
        in_specs=[
            pl.BlockSpec(memory_space=pltpu.SMEM),
            pl.BlockSpec((4, 3, 128, 128), lambda row: (row, 0, 0, 0)),
            pl.BlockSpec((2 * SEQ, 256), lambda row: (0, 0)),
        ],
        out_specs=pl.BlockSpec((4, 128, 128), lambda row: (row, 0, 0)),
        out_shape=jax.ShapeDtypeStruct((8, 128, 128), bf16),
        scratch_shapes=[pltpu.VMEM((SEQ, SEQ), f32)],
        compiler_params=pltpu.CompilerParams(vmem_limit_bytes=48 * 2**20),
        name="attend",
    )(lengths, heads_in, rel)


def attend_back(lengths, heads_in, rel, grad_context):
    return pl.pallas_call(
        attend_back_kernel,
        grid=(2,),
        in_specs=[
            pl.BlockSpec(memory_space=pltpu.SMEM),
            pl.BlockSpec((4, 3, 128, 128), lambda row: (row, 0, 0, 0)),
            pl.BlockSpec((2 * SEQ, 256), lambda row: (0, 0)),
            pl.BlockSpec((4, 128, 128), lambda row: (row, 0, 0)),
        ],
        out_specs=[
            pl.BlockSpec((4, 3, 128, 128), lambda row: (row, 0, 0, 0)),
            pl.BlockSpec((2 * SEQ, 256), lambda row: (0, 0)),
        ],
        out_shape=[
            jax.ShapeDtypeStruct((8, 3, 128, 128), bf16),
            jax.ShapeDtypeStruct((2 * SEQ, 256), f32),
        ],
        scratch_shapes=[
            pltpu.VMEM((SEQ, SEQ), f32),
            pltpu.VMEM((SEQ, SEQ), bf16),
            pltpu.VMEM((SEQ, SEQ), bf16),
        ],
        compiler_params=pltpu.CompilerParams(vmem_limit_bytes=48 * 2**20),
        name="attend_back",
    )(lengths, heads_in, rel, grad_context)


def owner_rows(block):
    wide = block.astype(f32).reshape(8, 2, 8, block.shape[-1])
    return jnp.swapaxes(wide, 0, 1).reshape(128, block.shape[-1]).astype(bf16)


def owner_blocks(rows128):
    wide = rows128.reshape(2, 8, 8, rows128.shape[-1])
    return jnp.swapaxes(wide, 0, 1)


def project_back_kernel(context, tokens, weights, resid):
    rows_in = jnp.concatenate([context[group] for group in range(8)], axis=1)
    resid[...] = tokens[...].astype(f32) + dot_nt(rows_in, owner_rows(weights[:, 0]))


def project_back(context, tokens, gathered):
    return pl.pallas_call(
        project_back_kernel,
        grid=(8,),
        in_specs=[
            pl.BlockSpec((8, 128, 128), lambda k: (0, 0, 0)),
            pl.BlockSpec((128, 128), lambda k: (0, k)),
            pl.BlockSpec((8, 1, 16, D), lambda k: (0, k, 4, 0)),
        ],
        out_specs=pl.BlockSpec((128, 128), lambda k: (0, k)),
        out_shape=jax.ShapeDtypeStruct((128, D), f32),
        compiler_params=pltpu.CompilerParams(vmem_limit_bytes=48 * 2**20),
        name="project_back",
    )(context, tokens, gathered)


def ffn_kernel(mine, theirs, vec, expand, reduce, act, slope, partial, low):
    phase, k = pl.program_id(0), pl.program_id(1)

    @pl.when((phase == 0) & (k == 0))
    def _():
        for half, resid in enumerate((mine, theirs)):
            first_norm, scaled, inverse = normalize(resid[...], vec[0:1], vec[1:2])
            low[128 * half : 128 * (half + 1)] = first_norm.astype(bf16)

    @pl.when(phase == 0)
    def _():
        inner = dot_nt(low[...], expand[:, 0].reshape(256, D))
        spread = 0.5 + 0.5 * lax.erf(inner * math.sqrt(0.5))
        act[k] = (inner * spread).astype(bf16)
        density = jnp.exp(-0.5 * inner * inner) * (1.0 / math.sqrt(2.0 * math.pi))
        slope[0] = spread + inner * density

    @pl.when(phase == 1)
    def _():
        total = jnp.zeros((256, 128), f32)
        for half in range(2):
            rows_in = jnp.concatenate([act[4 * half + part] for part in range(4)], axis=1)
            weights = owner_rows(reduce[:, 0, 16 * half : 16 * (half + 1)])
            total = total + dot_nt(rows_in, weights)
        partial[...] = total


def ffn_forward(mine, theirs, vec, gathered):
    whole = lambda phase, k: (0, 0)
    return pl.pallas_call(
        ffn_kernel,
        grid=(2, 8),
        in_specs=[
            pl.BlockSpec((128, D), whole),
            pl.BlockSpec((128, D), whole),
            pl.BlockSpec((4, D), whole),
            pl.BlockSpec((8, 1, 32, D), lambda phase, k: (0, jnp.where(phase == 0, k, 7), 0, 0)),
            pl.BlockSpec((8, 1, 32, D), lambda phase, k: (0, jnp.where(phase == 0, 0, k), 1, 0)),
        ],
        out_specs=[
            pl.BlockSpec((8, 256, 256), lambda phase, k: (0, 0, 0)),
            pl.BlockSpec((1, 256, 256), lambda phase, k: (jnp.where(phase == 0, k, 7), 0, 0)),
            pl.BlockSpec((256, 128), lambda phase, k: (0, jnp.where(phase == 0, 0, k))),
        ],
        out_shape=[
            jax.ShapeDtypeStruct((8, 256, 256), bf16),
            jax.ShapeDtypeStruct((8, 256, 256), f32),
            jax.ShapeDtypeStruct((256, D), f32),
        ],
        scratch_shapes=[pltpu.VMEM((256, D), bf16)],
        compiler_params=pltpu.CompilerParams(vmem_limit_bytes=48 * 2**20),
        name="ffn_forward",
    )(mine, theirs, vec, gathered, gathered)


def ffn_back_kernel(
    mine,
    theirs,
    vec,
    ffn_own,
    ffn_got,
    cot_own,
    cot_got,
    act,
    slope,
    expand,
    reduce,
    output,
    blocks,
    partial,
    sums,
    low,
    grad_ffn,
    grad_act,
):
    phase, k = pl.program_id(0), pl.program_id(1)

    @pl.when((phase == 0) & (k == 0))
    def _():
        sums[...] = jnp.zeros_like(sums)
        for half, (resid, cot) in enumerate(((mine, cot_own), (theirs, cot_got))):
            span = slice(128 * half, 128 * (half + 1))
            cross = slice(128 * (1 - half), 128 * (2 - half))
            first_norm, scaled, inverse = normalize(resid[...], vec[0:1], vec[1:2])
            low[span] = first_norm.astype(bf16)
            resid2 = first_norm + (ffn_own[span] + ffn_got[cross])
            normed, scaled, inverse = normalize(resid2, vec[2:3], vec[3:4])
            grad = cot[...].astype(f32)
            if half == 0:
                output[...] = normed.astype(bf16)
                sums[2:3] = jnp.sum(grad * scaled, axis=0, keepdims=True)
                sums[3:4] = jnp.sum(grad, axis=0, keepdims=True)
            grad = normalize_back(grad, scaled, inverse, vec[2:3])
            partial[span] = 0.5 * grad
            grad = grad.astype(bf16)
            for chunk in range(8):
                grad_ffn[chunk, span] = grad[:, 128 * chunk : 128 * (chunk + 1)]
        grad_act[...] = jnp.zeros_like(grad_act)

    @pl.when(phase == 0)
    def _():
        grad = grad_ffn[k]
        for half in range(2):
            weights = owner_rows(reduce[:, 0, 16 * half : 16 * (half + 1)])
            made = []
            for part in range(4):
                chunk = 4 * half + part
                grad_act[chunk] += dot_nn(grad, weights[:, 256 * part : 256 * (part + 1)])
                made.append(dot_tn(grad, act[chunk]))
            made = owner_blocks(jnp.concatenate(made, axis=1)).reshape(4, 2, 16, D)
            blocks[0, :, 0, :, 16 * half : 16 * (half + 1)] = made.astype(bf16)

    @pl.when(phase == 1)
    def _():
        weights = expand[:, 0].reshape(256, D)
        grad = (slope[0] * grad_act[k]).astype(bf16)
        blocks[0, :, 0] = dot_tn(grad, low[...]).astype(bf16).reshape(4, 2, 32, D)
        partial[...] += dot_nn(grad, weights)


def ffn_backward(mine, theirs, vec, ffn_own, ffn_got, cot_own, cot_got, act, slope, gathered):
    whole = lambda phase, k: (0, 0)
    return pl.pallas_call(
        ffn_back_kernel,
        grid=(2, 8),
        in_specs=[
            pl.BlockSpec((128, D), whole),
            pl.BlockSpec((128, D), whole),
            pl.BlockSpec((4, D), whole),
            pl.BlockSpec((256, D), whole),
            pl.BlockSpec((256, D), whole),
            pl.BlockSpec((128, D), whole),
            pl.BlockSpec((128, D), whole),
            pl.BlockSpec((8, 256, 256), lambda phase, k: (0, 0, 0)),
            pl.BlockSpec((1, 256, 256), lambda phase, k: (jnp.where(phase == 0, 0, k), 0, 0)),
            pl.BlockSpec((8, 1, 32, D), lambda phase, k: (0, jnp.where(phase == 0, 0, k), 0, 0)),
            pl.BlockSpec((8, 1, 32, D), lambda phase, k: (0, jnp.where(phase == 0, k, 7), 1, 0)),
        ],
        out_specs=[
            pl.BlockSpec((128, D), whole),
            pl.BlockSpec(
                (1, 4, 1, 2, 32, D), lambda phase, k: (k % 4, 0, k // 4, 0, 1 - phase, 0)
            ),
            pl.BlockSpec((256, D), whole),
            pl.BlockSpec((8, D), whole),
        ],
        out_shape=[
            jax.ShapeDtypeStruct((128, D), bf16),
            jax.ShapeDtypeStruct((4, 4, 2, 2, 80, D), bf16),
            jax.ShapeDtypeStruct((256, D), f32),
            jax.ShapeDtypeStruct((8, D), f32),
        ],
        scratch_shapes=[
            pltpu.VMEM((256, D), bf16),
            pltpu.VMEM((8, 256, 128), bf16),
            pltpu.VMEM((8, 256, 256), f32),
        ],
        compiler_params=pltpu.CompilerParams(vmem_limit_bytes=56 * 2**20),
        name="ffn_backward",
    )(mine, theirs, vec, ffn_own, ffn_got, cot_own, cot_got, act, slope, gathered, gathered)


def first_back_kernel(
    mine,
    theirs,
    vec,
    grad_own,
    grad_got,
    ctx_own,
    ctx_got,
    sums,
    weights,
    held,
    grad_resid,
    grad_context,
    blocks,
    grad_low,
    total,
    vec_sums,
):
    k = pl.program_id(0)

    @pl.when(k == 0)
    def _():
        for half, resid in enumerate((mine, theirs)):
            span = slice(128 * half, 128 * (half + 1))
            cross = slice(128 * (1 - half), 128 * (2 - half))
            normed, scaled, inverse = normalize(resid[...], vec[0:1], vec[1:2])
            grad = grad_own[span] + grad_got[cross]
            if half == 0:
                both_sums = jnp.concatenate(
                    [
                        jnp.sum(grad * scaled, axis=0, keepdims=True),
                        jnp.sum(grad, axis=0, keepdims=True),
                        sums[2:],
                    ],
                    axis=0,
                )
                for chunk in range(8):
                    vec_sums[chunk] = both_sums[:, 128 * chunk : 128 * (chunk + 1)]
            grad = normalize_back(grad, scaled, inverse, vec[0:1])
            if half == 0:
                grad_resid[...] = grad
            grad = grad.astype(bf16)
            for chunk in range(8):
                grad_low[chunk, span] = grad[:, 128 * chunk : 128 * (chunk + 1)]
        total[...] = jnp.zeros_like(total)

    grad = grad_low[k]
    total[...] += dot_nn(grad[:128], owner_rows(weights[:, 0]))
    ctx_half = jnp.concatenate([ctx_own[...], ctx_got[...]], axis=0)
    made = owner_blocks(dot_tn(grad, ctx_half))
    made = jnp.concatenate([made[:, 0], made[:, 1]], axis=-1)
    row = jnp.concatenate([vec_sums[k], jnp.zeros((8, D - 128), f32)], axis=1)
    row = jnp.broadcast_to(row[None], (8, 8, D))
    made = jnp.concatenate([made, row], axis=1).astype(bf16)
    blocks[0, :, 0] = made.reshape(4, 2, 16, D)

    @pl.when(k == 7)
    def _():
        for group in range(8):
            grad_context[group] = total[:, 128 * group : 128 * (group + 1)].astype(bf16)


def first_backward(mine, theirs, vec, grad_own, grad_got, ctx_own, ctx_got, sums, gathered, blocks):
    whole = lambda k: (0, 0)
    return pl.pallas_call(
        first_back_kernel,
        grid=(8,),
        in_specs=[
            pl.BlockSpec((128, D), whole),
            pl.BlockSpec((128, D), whole),
            pl.BlockSpec((4, D), whole),
            pl.BlockSpec((256, D), whole),
            pl.BlockSpec((256, D), whole),
            pl.BlockSpec((128, 512), whole),
            pl.BlockSpec((128, 512), whole),
            pl.BlockSpec((8, D), whole),
            pl.BlockSpec((8, 1, 16, D), lambda k: (0, k, 4, 0)),
            pl.BlockSpec(memory_space=pl.ANY),
        ],
        out_specs=[
            pl.BlockSpec((128, D), whole),
            pl.BlockSpec((8, 128, 128), lambda k: (0, 0, 0)),
            pl.BlockSpec((1, 4, 1, 2, 16, D), lambda k: (k % 4, 0, k // 4, 0, 4, 0)),
        ],
        out_shape=[
            jax.ShapeDtypeStruct((128, D), f32),
            jax.ShapeDtypeStruct((8, 128, 128), bf16),
            jax.ShapeDtypeStruct((4, 4, 2, 2, 80, D), bf16),
        ],
        scratch_shapes=[
            pltpu.VMEM((8, 256, 128), bf16),
            pltpu.VMEM((128, D), f32),
            pltpu.VMEM((8, 8, 128), f32),
        ],
        input_output_aliases={9: 2},
        compiler_params=pltpu.CompilerParams(vmem_limit_bytes=56 * 2**20),
        name="first_backward",
    )(mine, theirs, vec, grad_own, grad_got, ctx_own, ctx_got, sums, gathered, blocks)


def swap(value):
    return lax.ppermute(value, "core", [(0, 1), (1, 0)])


def exchange(value, axes):
    return lax.all_to_all(value, axes, 0, 0, tiled=True)


def shifted(value, axis, size, step):
    return lax.ppermute(value, axis, [(i, (i + step) % size) for i in range(size)])


def ring_gather(value, axis, size):
    place = lax.axis_index(axis)
    blocks = jnp.stack([value] + [shifted(value, axis, size, step) for step in range(1, size)])
    return jnp.take(blocks, (place - jnp.arange(size)) % size, axis=0)


def ring_scatter(blocks, axis, size, dtype=f32):
    place = lax.axis_index(axis)
    total = lax.dynamic_index_in_dim(blocks, place, 0, keepdims=False).astype(f32)
    for step in range(1, size):
        sent = lax.dynamic_index_in_dim(blocks, (place + step) % size, 0, keepdims=False)
        total = total + shifted(sent, axis, size, step).astype(f32)
    return total.astype(dtype)


def ring_sum(value, axis, size):
    total = value
    for step in range(1, size):
        total = total + shifted(value, axis, size, step)
    return total


def arrange_kernel(core, mine, theirs, heads):
    for column in range(8):
        span = slice(192 * column, 192 * (column + 1))
        own, other = mine[:, span].astype(f32), theirs[:, span].astype(f32)
        first = core[0] == 0
        joined = jnp.concatenate(
            [jnp.where(first, own, other), jnp.where(first, other, own)], axis=1
        )
        for place in range(3):
            chunk = 3 * column + place
            heads[chunk % 8, chunk // 8] = joined[:, 128 * place : 128 * (place + 1)].astype(bf16)


def arrange(core, mine, theirs):
    return pl.pallas_call(
        arrange_kernel,
        in_specs=[
            pl.BlockSpec(memory_space=pltpu.SMEM),
            pl.BlockSpec(memory_space=pltpu.VMEM),
            pl.BlockSpec(memory_space=pltpu.VMEM),
        ],
        out_specs=pl.BlockSpec(memory_space=pltpu.VMEM),
        out_shape=jax.ShapeDtypeStruct((8, 3, 128, 128), bf16),
        compiler_params=pltpu.CompilerParams(vmem_limit_bytes=32 * 2**20),
        name="arrange",
    )(core, mine, theirs)


def split_kernel(core, heads, keep, give):
    for column in range(8):
        chunks = [3 * column + place for place in range(3)]
        joined = jnp.concatenate(
            [heads[chunk % 8, chunk // 8].astype(f32) for chunk in chunks], axis=1
        )
        first = core[0] == 0
        zero, one = joined[:, :192], joined[:, 192:]
        span = slice(192 * column, 192 * (column + 1))
        keep[:, span] = jnp.where(first, zero, one).astype(bf16)
        give[:, span] = jnp.where(first, one, zero).astype(bf16)


def split(core, heads):
    return pl.pallas_call(
        split_kernel,
        in_specs=[
            pl.BlockSpec(memory_space=pltpu.SMEM),
            pl.BlockSpec(memory_space=pltpu.VMEM),
        ],
        out_specs=[pl.BlockSpec(memory_space=pltpu.VMEM)] * 2,
        out_shape=[jax.ShapeDtypeStruct((128, 1536), bf16)] * 2,
        compiler_params=pltpu.CompilerParams(vmem_limit_bytes=32 * 2**20),
        name="split",
    )(core, heads)


def per_device(
    tokens,
    w_project,
    w_attend,
    first_gain,
    first_shift,
    w_expand,
    w_reduce,
    second_gain,
    second_shift,
    position_table,
    w_query,
    w_key,
    lengths,
    cotangent,
):
    core = lax.axis_index("core")
    column = lax.axis_index(COLUMN)
    group = lax.axis_index(GROUP)
    local = tokens.shape[0]
    pair = 2 * local
    highest = lax.Precision.HIGHEST
    column_bucket = bucket_values(SEQ - 1 - np.arange(2 * SEQ - 1), SPAN)
    column_ids = jnp.asarray(np.append(column_bucket, 0))
    fold = np.append(column_bucket, -1)[None, :] == np.arange(2 * SPAN)[:, None]
    fold = jnp.asarray(fold.astype(np.float32)).astype(bf16)

    def by_core(zero, one):
        return jnp.where(core == 0, zero, one)

    def in_order(mine, theirs):
        return by_core(mine, theirs), by_core(theirs, mine)

    def both(value):
        return jnp.concatenate([value, swap(value)], axis=0)

    tokens_two = both(tokens)
    cotangent_got = swap(cotangent)
    project_t = exchange(
        jnp.broadcast_to(w_project.T[None], (64, 24, D)), COLUMN + GROUP
    ).reshape(1536, D)
    table = ring_gather(ring_gather(position_table.T, "yh", 2), "z", 4).reshape(64, 2 * SPAN)
    table = jnp.concatenate([table, w_key, w_query], axis=1)
    for axis, size in (("core", 2), ("x", 4), ("yl", 2)):
        table = ring_gather(table, axis, size)
    table = table.reshape(D, 2 * SPAN + 256)
    table_t, position_weights = table[:, : 2 * SPAN], table[:, 2 * SPAN :]

    vectors = jnp.stack([first_gain, first_shift, second_gain, second_shift])
    vectors = jnp.pad(vectors, ((0, 0), (0, D - 8)))
    vectors = jnp.concatenate(in_order(vectors, swap(vectors)), axis=0)
    reduce_rows = jnp.moveaxis(w_reduce.T.reshape(8, 8, 2, 256), 2, 0).reshape(2, 8, 2048)
    mine, theirs = in_order(reduce_rows[0], reduce_rows[1])
    reduce_rows = jnp.concatenate(in_order(mine, swap(theirs)), axis=0)
    attend_rows = w_attend.T
    attend_rows = jnp.concatenate(in_order(attend_rows, swap(attend_rows)), axis=0)
    packet = jnp.concatenate(
        [w_expand.T, reduce_rows[:, :D], reduce_rows[:, D:], attend_rows, vectors], axis=0
    )
    gathered = lax.all_gather(packet, CHIPS, axis=0, tiled=False).reshape(8, 8, 88, D)
    vec = gathered[..., 80:, :8].reshape(8, 8, 2, 4, 8).transpose(3, 1, 2, 0, 4)
    vec = vec.reshape(4, D).astype(f32)
    gain_one, shift_one, gain_two, shift_two = vec[0], vec[1], vec[2], vec[3]

    packed = dot_nt(tokens_two, project_t).astype(bf16)
    core_id = core.reshape(1)
    heads_in = exchange(arrange(core_id, packed[:local], swap(packed[local:])), GROUP)
    rel = dot_tn(table_t, position_weights).astype(bf16)[column_ids]
    context = exchange(attend(lengths, heads_in, rel), GROUP)
    flat = context.transpose(1, 0, 2).reshape(local, D)
    context_own, context_theirs = in_order(flat[:, :512], flat[:, 512:])
    context_got = swap(context_theirs)

    resid_own = project_back(context, tokens, gathered)
    resid_got = swap(resid_own)
    activ, slope, ffn_own = ffn_forward(resid_own, resid_got, vec, gathered)
    output, blocks, grad_own, sums = ffn_backward(
        resid_own,
        resid_got,
        vec,
        ffn_own,
        swap(ffn_own),
        cotangent,
        cotangent_got,
        activ,
        slope,
        gathered,
    )
    grad_resid1, grad_context, blocks = first_backward(
        resid_own,
        resid_got,
        vec,
        grad_own,
        swap(grad_own),
        context_own,
        context_got,
        sums,
        gathered,
        blocks,
    )

    grad_ctx = exchange(grad_context, GROUP)
    summed = lax.psum_scatter(
        blocks.reshape(16, 4 * 80, D), ("x", "z"), scatter_dimension=0, tiled=True
    )
    summed = ring_scatter(summed.reshape(2, 2 * 80, D), "yl", 2, bf16)
    summed = ring_scatter(summed.reshape(2, 80, D), "yh", 2)
    expand_sum = summed[:32]
    reduce_sum = jnp.concatenate([summed[32:48], summed[48:64]], axis=1)
    attend_sum = summed[64:72].reshape(8, 2, 512)
    vector_sum = summed[72:76, :128].reshape(4, 2, 8, 8)
    vector_sum = lax.dynamic_index_in_dim(vector_sum, group, axis=2, keepdims=False)

    grads, rel_grad = attend_back(lengths, heads_in, rel, grad_ctx)
    keep, give = split(core_id, exchange(grads, GROUP))
    grad_packed = jnp.concatenate([keep, swap(give)], axis=0)
    grad_project_t = dot_tn(grad_packed, tokens_two).astype(bf16)
    grad_project = exchange(grad_project_t.reshape(64, 24, D), COLUMN + GROUP)
    grad_project = jnp.sum(grad_project.astype(f32), axis=0).T
    tokens_part = dot_nn(grad_packed, project_t)
    tokens_grad = grad_resid1 + (tokens_part[:local] + swap(tokens_part[local:]))

    grad_expand = expand_sum.T
    mine, theirs = in_order(reduce_sum[:8], reduce_sum[8:])
    parts = in_order(mine, swap(theirs))
    grad_reduce = jnp.stack([part.reshape(8, 8, 256) for part in parts], axis=2)
    grad_reduce = grad_reduce.reshape(8, FF).T
    mine, theirs = in_order(attend_sum[:, 0], attend_sum[:, 1])
    grad_attend = jnp.concatenate(in_order(mine, swap(theirs)), axis=1).T

    mine, theirs = in_order(vector_sum[:, 0], vector_sum[:, 1])
    vectors = mine + swap(theirs)

    upper = rel_grad.astype(bf16)
    lower = (rel_grad - upper.astype(f32)).astype(bf16)
    rel_grad = dot_nn(fold, upper) + dot_nn(fold, lower)
    rel_grad = rel_grad + swap(rel_grad)
    rel_grad = by_core(rel_grad[:, :128], rel_grad[:, 128:])
    rel_grad = ring_sum(ring_sum(rel_grad, "x", 4), "yl", 2)
    rel_key_grad, rel_query_grad = in_order(rel_grad, swap(rel_grad))
    own = 64 * (2 * column + core)
    table_own = lax.dynamic_slice_in_dim(table_t, own, 64, axis=0).astype(f32)
    grad_key = jnp.dot(table_own, rel_key_grad, precision=highest)
    grad_query = jnp.dot(table_own, rel_query_grad, precision=highest)
    weights_own = lax.dynamic_slice_in_dim(position_weights, own, 64, axis=0).astype(f32)
    table_part = lax.dot_general(
        weights_own,
        jnp.concatenate([rel_key_grad, rel_query_grad], axis=1),
        (((1,), (1,)), ((), ())),
        precision=highest,
    )
    table_part = ring_scatter(table_part.reshape(4, 2, 8, 2 * SPAN), "z", 4)
    grad_table = ring_scatter(table_part, "yh", 2).T

    return (
        output,
        tokens_grad.astype(bf16),
        grad_project,
        grad_attend,
        vectors[0],
        vectors[1],
        grad_expand,
        grad_reduce,
        vectors[2],
        vectors[3],
        grad_table,
        grad_query,
        grad_key,
    )


def solution(mesh):
    parts = Mesh(mesh.devices.reshape(2, 4, 2, 4, 2), EVERY)
    in_specs = (
        P(EVERY, None),
        P(None, EVERY),
        P(None, EVERY),
        P(EVERY),
        P(EVERY),
        P(None, EVERY),
        P(None, EVERY),
        P(EVERY),
        P(EVERY),
        P(None, EVERY),
        P(DP, GROUP),
        P(DP, GROUP),
        P(DP),
        P(EVERY, None),
    )
    out_specs = (
        P(EVERY, None),
        P(EVERY, None),
        P(None, EVERY),
        P(None, EVERY),
        P(EVERY),
        P(EVERY),
        P(None, EVERY),
        P(None, EVERY),
        P(EVERY),
        P(EVERY),
        P(None, EVERY),
        P(DP, GROUP),
        P(DP, GROUP),
    )
    return jax.shard_map(
        per_device, mesh=parts, in_specs=in_specs, out_specs=out_specs, check_vma=False
    )
```

```python
import math

import jax
import jax.numpy as jnp
import numpy as np
from jax import lax
from jax.experimental import pallas as pl
from jax.experimental.pallas import tpu as pltpu
from jax.sharding import Mesh
from jax.sharding import PartitionSpec as P

D = 1024
HEADS = 16
HEAD_DIM = 64
FF = 4096
SPAN = 256
SEQ = 512
BLOCK = 128
WINDOW = SEQ + BLOCK
STEP = 4

EPS = 1e-07
MASKED = -1e30

DP = ("yl", "x", "core")
GROUP = ("z", "yh")
COLUMN = ("yl", "x")
EVERY = DP + GROUP
CHIPS = ("z", "yh", "yl", "x")
DEVICES = ("core",) + CHIPS
bf16 = jnp.bfloat16
f32 = jnp.float32


def bucket_values(offset, span):
    middle = span // 2
    absolute = np.where((offset < middle) & (offset > -middle), middle - 1, np.abs(offset))
    log_place = (
        np.ceil(np.log(absolute / middle) / np.log((2 * span - 1) / middle) * (middle - 1)) + middle
    )
    buckets = np.where(absolute <= middle, offset, log_place * np.sign(offset)).astype(np.int64)
    return np.clip(buckets + span, 0, 2 * span - 1).astype(np.int32)


def normalize(value, gain, shift):
    center = value - jnp.mean(value, axis=-1, keepdims=True)
    inverse = lax.rsqrt(jnp.mean(center * center, axis=-1, keepdims=True) + EPS)
    scaled = center * inverse
    return (scaled * gain + shift, scaled, inverse)


def normalize_back(incoming, scaled, inverse, gain):
    grad_scaled = incoming * gain
    middle = (
        grad_scaled
        - jnp.mean(grad_scaled, axis=-1, keepdims=True)
        - scaled * jnp.mean(grad_scaled * scaled, axis=-1, keepdims=True)
    )
    return inverse * middle


def dot_nn(left, right):
    return lax.dot_general(left, right, (((1,), (0,)), ((), ())), preferred_element_type=f32)


def dot_nt(left, right):
    return lax.dot_general(left, right, (((1,), (1,)), ((), ())), preferred_element_type=f32)


def dot_tn(left, right):
    return lax.dot_general(left, right, (((0,), (0,)), ((), ())), preferred_element_type=f32)


def window(block):
    start = SEQ - BLOCK - BLOCK * block
    return slice(start, start + WINDOW)


def rows(block):
    return slice(BLOCK * block, BLOCK * (block + 1))


def skew(values):
    return pltpu.roll(values, SEQ + 1, 1, stride=1, stride_axis=0)[:, :SEQ]


def unskew(values):
    wide = jnp.concatenate([values, jnp.zeros((BLOCK, BLOCK), f32)], axis=1)
    return pltpu.roll(wide, 0, 1, stride=1, stride_axis=0)


def turn(mirror, values):
    upper = values.astype(bf16)
    return dot_nn(mirror, upper) + dot_nn(mirror, (values - upper.astype(f32)).astype(bf16))


def one_head(value, head):
    lane = lax.broadcasted_iota(jnp.int32, value.shape, 1)
    return jnp.where(lane // HEAD_DIM == head, value, jnp.zeros_like(value))


def query_bias(key, rel_queries, bias):
    for block in range(SEQ // BLOCK):
        by_offset = dot_nt(key[rows(block)], rel_queries[window(block)])
        bias[:, rows(block)] = skew(by_offset).T


def probabilities(query, key, rel_keys, bias, block, length):
    part = query[rows(block)]
    logits = dot_nt(part, key) + skew(dot_nt(part, rel_keys[window(block)])) + bias[rows(block)]
    logits = logits * (1.0 / math.sqrt(3 * HEAD_DIM))
    column = lax.broadcasted_iota(jnp.int32, logits.shape, 1)
    logits = jnp.where(column < length, logits, MASKED)
    exponent = jnp.exp(logits - jnp.max(logits, axis=1, keepdims=True))
    return exponent * (1.0 / jnp.sum(exponent, axis=1, keepdims=True))


def attend_kernel(lengths, heads_in, rel, context, bias):
    length = lengths[pl.program_id(0)]
    query, key, values = (heads_in[:, part].reshape(SEQ, 128) for part in range(3))
    rel_keys, rel_queries = rel[:, :128], rel[:, 128:]
    total = [jnp.zeros((BLOCK, 128), f32) for _ in range(SEQ // BLOCK)]
    for head in range(2):
        query_h, key_h, values_h = (one_head(part, head) for part in (query, key, values))
        query_bias(key_h, rel_queries, bias)
        for block in range(SEQ // BLOCK):
            probs = probabilities(query_h, key, rel_keys, bias, block, length)
            total[block] = total[block] + dot_nn(probs.astype(bf16), values_h)
    for block in range(SEQ // BLOCK):
        context[block] = total[block].astype(bf16)


def attend_back_kernel(
    lengths, heads_in, rel, grad_context, grads, grad_rel, bias, probs_ref, grad_ref
):
    length = lengths[pl.program_id(0)]
    query, key, values = (heads_in[:, part].reshape(SEQ, 128) for part in range(3))
    grad_ctx = grad_context[...].reshape(SEQ, 128)
    rel_keys, rel_queries = rel[:, :128], rel[:, 128:]
    blocks = SEQ // BLOCK
    first = lax.broadcasted_iota(jnp.int32, (BLOCK, BLOCK), 0)
    second = lax.broadcasted_iota(jnp.int32, (BLOCK, BLOCK), 1)
    mirror = jnp.where(first + second == BLOCK - 1, 1.0, 0.0).astype(bf16)

    @pl.when(pl.program_id(0) == 0)
    def _():
        grad_rel[...] = jnp.zeros_like(grad_rel)

    queries, keys, ctxs = (
        [one_head(part, head) for head in range(2)] for part in (query, key, grad_ctx)
    )
    rel_keys_of = [one_head(rel_keys, head) for head in range(2)]
    rel_queries_of = [one_head(rel_queries, head) for head in range(2)]
    for head in range(2):
        query_bias(keys[head], rel_queries, bias.at[head])
    for block in range(blocks):
        grad_q, turned, rel_part = 0.0, 0.0, 0.0
        for head in range(2):
            probs = probabilities(queries[head], key, rel_keys, bias.at[head], block, length)
            probs_ref[head, rows(block)] = probs.astype(bf16)
            grad_probs = dot_nt(ctxs[head][rows(block)], values)
            inner = jnp.sum(probs * grad_probs, axis=1, keepdims=True)
            grad = (probs * (grad_probs - inner) * (1.0 / math.sqrt(3 * HEAD_DIM))).astype(bf16)
            grad_ref[head, rows(block)] = grad
            by_offset = unskew(dot_nn(mirror, grad)).astype(bf16)
            grad_q = grad_q + dot_nn(grad, keys[head])
            turned = turned + dot_nn(by_offset, rel_keys_of[head][window(block)])
            mirrored = dot_nn(mirror, queries[head][rows(block)]).astype(bf16)
            rel_part = rel_part + dot_tn(by_offset, mirrored)
        grad_rel[window(block), :128] += rel_part
        grads[block, 0] = (grad_q + turn(mirror, turned)).astype(bf16)
    for block in range(blocks):
        grad_k, grad_v, turned, rel_part = 0.0, 0.0, 0.0, 0.0
        for head in range(2):
            grad = grad_ref[head, :, rows(block)]
            by_offset = unskew(dot_nt(mirror, grad)).astype(bf16)
            grad_k = grad_k + dot_tn(grad, queries[head])
            turned = turned + dot_nn(by_offset, rel_queries_of[head][window(block)])
            grad_v = grad_v + dot_tn(probs_ref[head, :, rows(block)], ctxs[head])
            mirrored = dot_nn(mirror, keys[head][rows(block)]).astype(bf16)
            rel_part = rel_part + dot_tn(by_offset, mirrored)
        grad_rel[window(block), 128:] += rel_part
        grads[block, 1] = (grad_k + turn(mirror, turned)).astype(bf16)
        grads[block, 2] = grad_v.astype(bf16)


def attend(lengths, heads_in, rel):
    return pl.pallas_call(
        attend_kernel,
        grid=(2,),
        in_specs=[
            pl.BlockSpec(memory_space=pltpu.SMEM),
            pl.BlockSpec((4, 3, 128, 128), lambda row: (row, 0, 0, 0)),
            pl.BlockSpec((2 * SEQ, 256), lambda row: (0, 0)),
        ],
        out_specs=pl.BlockSpec((4, 128, 128), lambda row: (row, 0, 0)),
        out_shape=jax.ShapeDtypeStruct((8, 128, 128), bf16),
        scratch_shapes=[pltpu.VMEM((SEQ, SEQ), f32)],
        compiler_params=pltpu.CompilerParams(vmem_limit_bytes=48 * 2**20),
        name="attend",
    )(lengths, heads_in, rel)


def attend_back(lengths, heads_in, rel, grad_context):
    return pl.pallas_call(
        attend_back_kernel,
        grid=(2,),
        in_specs=[
            pl.BlockSpec(memory_space=pltpu.SMEM),
            pl.BlockSpec((4, 3, 128, 128), lambda row: (row, 0, 0, 0)),
            pl.BlockSpec((2 * SEQ, 256), lambda row: (0, 0)),
            pl.BlockSpec((4, 128, 128), lambda row: (row, 0, 0)),
        ],
        out_specs=[
            pl.BlockSpec((4, 3, 128, 128), lambda row: (row, 0, 0, 0)),
            pl.BlockSpec((2 * SEQ, 256), lambda row: (0, 0)),
        ],
        out_shape=[
            jax.ShapeDtypeStruct((8, 3, 128, 128), bf16),
            jax.ShapeDtypeStruct((2 * SEQ, 256), f32),
        ],
        scratch_shapes=[
            pltpu.VMEM((2, SEQ, SEQ), f32),
            pltpu.VMEM((2, SEQ, SEQ), bf16),
            pltpu.VMEM((2, SEQ, SEQ), bf16),
        ],
        compiler_params=pltpu.CompilerParams(vmem_limit_bytes=48 * 2**20),
        name="attend_back",
    )(lengths, heads_in, rel, grad_context)


def owner_rows(block):
    wide = block.astype(f32).reshape(8, STEP, 2, 8, block.shape[-1])
    return wide.transpose(1, 2, 0, 3, 4).reshape(STEP * 128, block.shape[-1]).astype(bf16)


def project_back_kernel(context, tokens, weights, resid):
    rows_in = jnp.concatenate([context[group] for group in range(8)], axis=1)
    resid[...] = tokens[...].astype(f32) + dot_nt(rows_in, owner_rows(weights[...]))


def project_back(context, tokens, gathered):
    return pl.pallas_call(
        project_back_kernel,
        grid=(8 // STEP,),
        in_specs=[
            pl.BlockSpec((8, 128, 128), lambda k: (0, 0, 0)),
            pl.BlockSpec((128, STEP * 128), lambda k: (0, k)),
            pl.BlockSpec((8, STEP, 16, D), lambda k: (0, k, 4, 0)),
        ],
        out_specs=pl.BlockSpec((128, STEP * 128), lambda k: (0, k)),
        out_shape=jax.ShapeDtypeStruct((128, D), f32),
        compiler_params=pltpu.CompilerParams(vmem_limit_bytes=48 * 2**20),
        name="project_back",
    )(context, tokens, gathered)


def ffn_kernel(mine, theirs, vec, expand, reduce, act, slope, partial, low):
    phase, k = pl.program_id(0), pl.program_id(1)

    @pl.when((phase == 0) & (k == 0))
    def _():
        for half, resid in enumerate((mine, theirs)):
            first_norm, scaled, inverse = normalize(resid[...], vec[0:1], vec[1:2])
            low[128 * half : 128 * (half + 1)] = first_norm.astype(bf16)

    @pl.when(phase == 0)
    def _():
        for column in range(STEP):
            inner = dot_nt(low[...], expand[:, column].reshape(256, D))
            spread_in = 0.5 + 0.5 * lax.erf(inner * math.sqrt(0.5))
            act[STEP * k + column] = (inner * spread_in).astype(bf16)
            density = jnp.exp(-0.5 * inner * inner) * (1.0 / math.sqrt(2.0 * math.pi))
            slope[column] = spread_in + inner * density

    @pl.when(phase == 1)
    def _():
        total = jnp.zeros((256, STEP * 128), f32)
        for half in range(2):
            rows_in = jnp.concatenate([act[4 * half + part] for part in range(4)], axis=1)
            weights = owner_rows(reduce[:, :, 16 * half : 16 * (half + 1)])
            total = total + dot_nt(rows_in, weights)
        partial[...] = total


def ffn_forward(mine, theirs, vec, gathered):
    whole = lambda phase, k: (0, 0)
    return pl.pallas_call(
        ffn_kernel,
        grid=(2, 8 // STEP),
        in_specs=[
            pl.BlockSpec((128, D), whole),
            pl.BlockSpec((128, D), whole),
            pl.BlockSpec((4, D), whole),
            pl.BlockSpec((8, STEP, 32, D), lambda phase, k: (0, jnp.where(phase == 0, k, 8 // STEP - 1), 0, 0)),
            pl.BlockSpec((8, STEP, 32, D), lambda phase, k: (0, jnp.where(phase == 0, 0, k), 1, 0)),
        ],
        out_specs=[
            pl.BlockSpec((8, 256, 256), lambda phase, k: (0, 0, 0)),
            pl.BlockSpec((STEP, 256, 256), lambda phase, k: (jnp.where(phase == 0, k, 8 // STEP - 1), 0, 0)),
            pl.BlockSpec((256, STEP * 128), lambda phase, k: (0, jnp.where(phase == 0, 0, k))),
        ],
        out_shape=[
            jax.ShapeDtypeStruct((8, 256, 256), bf16),
            jax.ShapeDtypeStruct((8, 256, 256), f32),
            jax.ShapeDtypeStruct((256, D), f32),
        ],
        scratch_shapes=[pltpu.VMEM((256, D), bf16)],
        compiler_params=pltpu.CompilerParams(vmem_limit_bytes=48 * 2**20),
        name="ffn_forward",
    )(mine, theirs, vec, gathered, gathered)


def own_half(core, wide):
    return jnp.where(core[0] == 0, wide[:, :64], wide[:, 64:])


def ffn_back_kernel(
    core,
    mine,
    theirs,
    vec,
    ffn_own,
    ffn_got,
    cot_own,
    cot_got,
    act_own,
    act_got,
    slope,
    expand,
    reduce,
    output,
    blocks,
    partial,
    sums,
    low,
    grad_ffn,
    grad_act,
    act,
):
    phase, k = pl.program_id(0), pl.program_id(1)

    @pl.when((phase == 0) & (k == 0))
    def _():
        sums[...] = jnp.zeros_like(sums)
        for half, (resid, cot) in enumerate(((mine, cot_own), (theirs, cot_got))):
            span = slice(128 * half, 128 * (half + 1))
            cross = slice(128 * (1 - half), 128 * (2 - half))
            first_norm, scaled, inverse = normalize(resid[...], vec[0:1], vec[1:2])
            low[span] = first_norm.astype(bf16)
            resid2 = first_norm + (ffn_own[span] + ffn_got[cross])
            normed, scaled, inverse = normalize(resid2, vec[2:3], vec[3:4])
            grad = cot[...].astype(f32)
            if half == 0:
                output[...] = normed.astype(bf16)
            sums[2:3] += jnp.sum(grad * scaled, axis=0, keepdims=True)
            sums[3:4] += jnp.sum(grad, axis=0, keepdims=True)
            grad = normalize_back(grad, scaled, inverse, vec[2:3])
            partial[span] = 0.5 * grad
            grad = grad.astype(bf16)
            for chunk in range(8 // STEP):
                grad_ffn[chunk, span] = grad[:, STEP * 128 * chunk : STEP * 128 * (chunk + 1)]
        grad_act[...] = jnp.zeros_like(grad_act)
        for chunk in range(8):
            own, got = act_own[chunk], act_got[chunk]
            got = jnp.concatenate([got[128:], got[:128]], axis=0)
            start = 512 * (chunk % 2)
            act[chunk // 2, :, start : start + 256] = jnp.where(core[0] == 0, own, got)
            act[chunk // 2, :, start + 256 : start + 512] = jnp.where(core[0] == 0, got, own)

    @pl.when(phase == 0)
    def _():
        grad = grad_ffn[k]
        own = [own_half(core, grad[:, 128 * column : 128 * (column + 1)]) for column in range(STEP)]
        own = jnp.concatenate(own, axis=1)
        for half in range(2):
            weights = owner_rows(reduce[:, :, 16 * half : 16 * (half + 1)])
            for part in range(4):
                grad_act[4 * half + part] += dot_nn(grad, weights[:, 256 * part : 256 * (part + 1)])
            made = [dot_tn(own, act[2 * half + part]).reshape(STEP, 8, 8, D) for part in range(2)]
            made = jnp.concatenate(made, axis=2).astype(bf16).reshape(STEP, 4, 2, 16, D)
            blocks[:, :, 0, :, 16 * half : 16 * (half + 1)] = made

    @pl.when(phase == 1)
    def _():
        for column in range(STEP):
            weights = expand[:, column].reshape(256, D)
            grad = (slope[column] * grad_act[STEP * k + column]).astype(bf16)
            made = dot_tn(grad, low[...]).astype(bf16)
            blocks[column, :, 0] = made.reshape(4, 2, 32, D)
            partial[...] += dot_nn(grad, weights)


def ffn_backward(
    core, mine, theirs, vec, ffn_own, ffn_got, cot_own, cot_got, act_own, act_got, slope, gathered
):
    whole = lambda phase, k: (0, 0)
    return pl.pallas_call(
        ffn_back_kernel,
        grid=(2, 8 // STEP),
        in_specs=[
            pl.BlockSpec(memory_space=pltpu.SMEM),
            pl.BlockSpec((128, D), whole),
            pl.BlockSpec((128, D), whole),
            pl.BlockSpec((4, D), whole),
            pl.BlockSpec((256, D), whole),
            pl.BlockSpec((256, D), whole),
            pl.BlockSpec((128, D), whole),
            pl.BlockSpec((128, D), whole),
            pl.BlockSpec((8, 256, 256), lambda phase, k: (0, 0, 0)),
            pl.BlockSpec((8, 256, 256), lambda phase, k: (0, 0, 0)),
            pl.BlockSpec((STEP, 256, 256), lambda phase, k: (jnp.where(phase == 0, 0, k), 0, 0)),
            pl.BlockSpec((8, STEP, 32, D), lambda phase, k: (0, jnp.where(phase == 0, 0, k), 0, 0)),
            pl.BlockSpec((8, STEP, 32, D), lambda phase, k: (0, jnp.where(phase == 0, k, 8 // STEP - 1), 1, 0)),
        ],
        out_specs=[
            pl.BlockSpec((128, D), whole),
            pl.BlockSpec(
                (STEP, 4, 1, 2, 32, D),
                lambda phase, k: (k % (4 // STEP), 0, k // (4 // STEP), 0, 1 - phase, 0),
            ),
            pl.BlockSpec((256, D), whole),
            pl.BlockSpec((8, D), whole),
        ],
        out_shape=[
            jax.ShapeDtypeStruct((128, D), bf16),
            jax.ShapeDtypeStruct((4, 4, 2, 2, 64, D), bf16),
            jax.ShapeDtypeStruct((256, D), f32),
            jax.ShapeDtypeStruct((8, D), f32),
        ],
        scratch_shapes=[
            pltpu.VMEM((256, D), bf16),
            pltpu.VMEM((8 // STEP, 256, STEP * 128), bf16),
            pltpu.VMEM((8, 256, 256), f32),
            pltpu.VMEM((4, 256, D), bf16),
        ],
        compiler_params=pltpu.CompilerParams(vmem_limit_bytes=56 * 2**20),
        name="ffn_backward",
    )(
        core,
        mine,
        theirs,
        vec,
        ffn_own,
        ffn_got,
        cot_own,
        cot_got,
        act_own,
        act_got,
        slope,
        gathered,
        gathered,
    )


def first_back_kernel(
    core,
    mine,
    theirs,
    vec,
    grad_own,
    grad_got,
    ctx_own,
    ctx_got,
    sums,
    weights,
    grad_resid,
    grad_context,
    blocks,
    grad_low,
    total,
    vec_sums,
):
    k = pl.program_id(0)

    @pl.when(k == 0)
    def _():
        found = sums[...]
        place = lax.broadcasted_iota(jnp.int32, (8, D), 0)
        for half, resid in enumerate((mine, theirs)):
            span = slice(128 * half, 128 * (half + 1))
            cross = slice(128 * (1 - half), 128 * (2 - half))
            normed, scaled, inverse = normalize(resid[...], vec[0:1], vec[1:2])
            grad = grad_own[span] + grad_got[cross]
            found += jnp.where(place == 0, jnp.sum(grad * scaled, axis=0, keepdims=True), 0.0)
            found += jnp.where(place == 1, jnp.sum(grad, axis=0, keepdims=True), 0.0)
            grad = normalize_back(grad, scaled, inverse, vec[0:1])
            if half == 0:
                grad_resid[...] = grad
            grad = grad.astype(bf16)
            for chunk in range(8 // STEP):
                grad_low[chunk, span] = grad[:, STEP * 128 * chunk : STEP * 128 * (chunk + 1)]
        for chunk in range(8):
            vec_sums[chunk] = found[:, 128 * chunk : 128 * (chunk + 1)]
        total[...] = jnp.zeros_like(total)

    grad = grad_low[k]
    total[...] += dot_nn(grad[:128], owner_rows(weights[...]))
    ctx = [jnp.concatenate([part[group] for group in range(8)], axis=1) for part in (ctx_own, ctx_got)]
    own = [own_half(core, grad[:, 128 * column : 128 * (column + 1)]) for column in range(STEP)]
    made = dot_tn(jnp.concatenate(own, axis=1), jnp.concatenate(ctx, axis=0)).reshape(STEP, 8, 8, D)
    for column in range(STEP):
        row = jnp.broadcast_to(vec_sums[STEP * k + column][None], (8, 8, 128))
        blocks[column] = jnp.concatenate([made[column], row], axis=-1).astype(bf16)

    @pl.when(k == 8 // STEP - 1)
    def _():
        for group in range(8):
            grad_context[group] = total[:, 128 * group : 128 * (group + 1)].astype(bf16)


def first_backward(
    core, mine, theirs, vec, grad_own, grad_got, ctx_own, ctx_got, sums, gathered
):
    whole = lambda k: (0, 0)
    return pl.pallas_call(
        first_back_kernel,
        grid=(8 // STEP,),
        in_specs=[
            pl.BlockSpec(memory_space=pltpu.SMEM),
            pl.BlockSpec((128, D), whole),
            pl.BlockSpec((128, D), whole),
            pl.BlockSpec((4, D), whole),
            pl.BlockSpec((256, D), whole),
            pl.BlockSpec((256, D), whole),
            pl.BlockSpec((8, 128, 128), lambda k: (0, 0, 0)),
            pl.BlockSpec((8, 128, 128), lambda k: (0, 0, 0)),
            pl.BlockSpec((8, D), whole),
            pl.BlockSpec((8, STEP, 16, D), lambda k: (0, k, 4, 0)),
        ],
        out_specs=[
            pl.BlockSpec((128, D), whole),
            pl.BlockSpec((8, 128, 128), lambda k: (0, 0, 0)),
            pl.BlockSpec((STEP, 8, 8, D + 128), lambda k: (k, 0, 0, 0)),
        ],
        out_shape=[
            jax.ShapeDtypeStruct((128, D), f32),
            jax.ShapeDtypeStruct((8, 128, 128), bf16),
            jax.ShapeDtypeStruct((8, 8, 8, D + 128), bf16),
        ],
        scratch_shapes=[
            pltpu.VMEM((8 // STEP, 256, STEP * 128), bf16),
            pltpu.VMEM((128, D), f32),
            pltpu.VMEM((8, 8, 128), f32),
        ],
        compiler_params=pltpu.CompilerParams(vmem_limit_bytes=56 * 2**20),
        name="first_backward",
    )(core, mine, theirs, vec, grad_own, grad_got, ctx_own, ctx_got, sums, gathered)


def swap(value):
    return lax.ppermute(value, "core", [(0, 1), (1, 0)])


def exchange(value, axes):
    return lax.all_to_all(value, axes, 0, 0, tiled=True)


def shifted(value, axis, size, step):
    return lax.ppermute(value, axis, [(i, (i + step) % size) for i in range(size)])


def stacked(value, axis):
    size = lax.axis_size(axis)
    return jnp.stack([value] + [shifted(value, axis, size, step) for step in range(1, size)])


def places_back(axis):
    size = lax.axis_size(axis)
    return (lax.axis_index(axis) - jnp.arange(size)) % size


def pick(blocks, index):
    return blocks.at[index.reshape(-1)].get(mode="promise_in_bounds")


def spread(value, axes):
    return exchange(jnp.broadcast_to(value[None], (8,) + value.shape), axes)


def gather_projection(rows_t, table_rows, position_rows):
    first = jnp.concatenate([rows_t[:, :512], table_rows], axis=0)
    second = rows_t[:, 512:]
    first = spread(first, GROUP).reshape(256, 512)
    second = stacked(stacked(second, "x"), "yl").reshape(8 * 24, 512)
    second = spread(second, GROUP)
    first = jnp.concatenate([first, position_rows], axis=0)
    first = stacked(stacked(first, "yl"), "x").reshape(8, 288, 512)
    x, yl = places_back("x")[None], places_back("yl")[:, None]
    first = pick(first, yl + 2 * x)
    position_rows = first[:, 256:]
    first = first[:, :256].reshape(64, 32, 512)
    second = second.reshape(8, 8, 24, 512)
    second = jnp.take(second, (x + 4 * yl).reshape(-1), axis=1, mode="clip")
    second = jnp.swapaxes(second, 0, 1).reshape(64, 24, 512)
    project_t = jnp.concatenate([first[:, :24], second], axis=2).reshape(1536, D)
    return project_t, first[:, 24:].reshape(512, 512), position_rows


def arrange_kernel(core, mine, theirs, heads):
    for column in range(8):
        span = slice(192 * column, 192 * (column + 1))
        own, other = mine[:, span].astype(f32), theirs[:, span].astype(f32)
        first = core[0] == 0
        joined = jnp.concatenate(
            [jnp.where(first, own, other), jnp.where(first, other, own)], axis=1
        )
        for place in range(3):
            chunk = 3 * column + place
            heads[chunk % 8, chunk // 8] = joined[:, 128 * place : 128 * (place + 1)].astype(bf16)


def arrange(core, mine, theirs):
    return pl.pallas_call(
        arrange_kernel,
        in_specs=[
            pl.BlockSpec(memory_space=pltpu.SMEM),
            pl.BlockSpec(memory_space=pltpu.VMEM),
            pl.BlockSpec(memory_space=pltpu.VMEM),
        ],
        out_specs=pl.BlockSpec(memory_space=pltpu.VMEM),
        out_shape=jax.ShapeDtypeStruct((8, 3, 128, 128), bf16),
        compiler_params=pltpu.CompilerParams(vmem_limit_bytes=32 * 2**20),
        name="arrange",
    )(core, mine, theirs)


def ring_scatter(blocks, axis, size, dtype=f32):
    place = lax.axis_index(axis)
    total = lax.dynamic_index_in_dim(blocks, place, 0, keepdims=False).astype(f32)
    for step in range(1, size):
        sent = lax.dynamic_index_in_dim(blocks, (place + step) % size, 0, keepdims=False)
        total = total + shifted(sent, axis, size, step).astype(f32)
    return total.astype(dtype)


def y_scatter(blocks):
    yl, yh = lax.axis_index("yl"), lax.axis_index("yh")
    blocks = jnp.swapaxes(blocks, 0, 1).reshape((4,) + blocks.shape[2:])
    place = 2 * yh + yl
    total = lax.dynamic_index_in_dim(blocks, place, 0, keepdims=False).astype(f32)

    def on_mesh(y):
        return 2 * (y % 2) + y // 2

    for step in range(1, 4):
        sent = lax.dynamic_index_in_dim(blocks, (place + step) % 4, 0, keepdims=False)
        ring = [(on_mesh(y), on_mesh((y + step) % 4)) for y in range(4)]
        total = total + lax.ppermute(sent, ("yl", "yh"), ring).astype(f32)
    return total


def ring_sum(value, axis, size):
    total = value
    for step in range(1, size):
        total = total + shifted(value, axis, size, step)
    return total


def split_kernel(core, heads, keep, give):
    for column in range(8):
        chunks = [3 * column + place for place in range(3)]
        joined = jnp.concatenate(
            [heads[chunk % 8, chunk // 8].astype(f32) for chunk in chunks], axis=1
        )
        first = core[0] == 0
        zero, one = joined[:, :192], joined[:, 192:]
        span = slice(192 * column, 192 * (column + 1))
        keep[:, span] = jnp.where(first, zero, one).astype(bf16)
        give[:, span] = jnp.where(first, one, zero).astype(bf16)


def split(core, heads):
    return pl.pallas_call(
        split_kernel,
        in_specs=[
            pl.BlockSpec(memory_space=pltpu.SMEM),
            pl.BlockSpec(memory_space=pltpu.VMEM),
        ],
        out_specs=[pl.BlockSpec(memory_space=pltpu.VMEM)] * 2,
        out_shape=[jax.ShapeDtypeStruct((128, 1536), bf16)] * 2,
        compiler_params=pltpu.CompilerParams(vmem_limit_bytes=32 * 2**20),
        name="split",
    )(core, heads)


def per_device(
    tokens,
    w_project,
    w_attend,
    first_gain,
    first_shift,
    w_expand,
    w_reduce,
    second_gain,
    second_shift,
    position_table,
    w_query,
    w_key,
    lengths,
    cotangent,
):
    core = lax.axis_index("core")
    group = lax.axis_index(GROUP)
    local = tokens.shape[0]
    core_id = core.reshape(1)
    pair = 2 * local
    column_bucket = bucket_values(SEQ - 1 - np.arange(2 * SEQ - 1), SPAN)
    fold = np.append(column_bucket, -1)[None, :] == np.arange(2 * SPAN)[:, None]
    fold = jnp.asarray(fold.astype(np.float32)).astype(bf16)

    def by_core(zero, one):
        return jnp.where(core == 0, zero, one)

    def in_order(mine, theirs):
        return by_core(mine, theirs), by_core(theirs, mine)

    def both(value):
        return jnp.concatenate([value, swap(value)], axis=0)

    cotangent_got = swap(cotangent)
    tokens_two = both(tokens)
    weights_own = jnp.concatenate([w_key, w_query], axis=1)
    project_t, table_t, position_rows = gather_projection(
        w_project.T,
        position_table.T,
        jnp.concatenate([weights_own[:32], weights_own[32:]], axis=1),
    )
    position_weights = jnp.stack([position_rows[..., :256], position_rows[..., 256:]], axis=1)
    position_weights = position_weights.reshape(512, 256)

    vectors = jnp.stack([first_gain, first_shift, second_gain, second_shift])
    vectors = jnp.pad(vectors, ((0, 0), (0, D - 8)))
    vectors = jnp.concatenate(in_order(vectors, swap(vectors)), axis=0)
    reduce_rows = jnp.moveaxis(w_reduce.T.reshape(8, 8, 2, 256), 2, 0).reshape(2, 8, 2048)
    mine, theirs = in_order(reduce_rows[0], reduce_rows[1])
    reduce_rows = jnp.concatenate(in_order(mine, swap(theirs)), axis=0)
    attend_rows = w_attend.T
    attend_rows = jnp.concatenate(in_order(attend_rows, swap(attend_rows)), axis=0)
    packet = jnp.concatenate(
        [w_expand.T, reduce_rows[:, :D], reduce_rows[:, D:], attend_rows, vectors], axis=0
    )
    gathered = lax.all_gather(packet, CHIPS, axis=0, tiled=False).reshape(8, 8, 88, D)
    vec = gathered[..., 80:, :8].reshape(8, 8, 2, 4, 8).transpose(3, 1, 2, 0, 4)
    vec = vec.reshape(4, D).astype(f32)
    gain_one, shift_one, gain_two, shift_two = vec[0], vec[1], vec[2], vec[3]

    packed = dot_nt(tokens_two, project_t).astype(bf16)
    heads_in = exchange(arrange(core_id, packed[:local], swap(packed[local:])), GROUP)
    rel = dot_tn(table_t, position_weights)
    rel = dot_tn(fold, (rel + swap(rel)).astype(bf16)).astype(bf16)
    context = exchange(attend(lengths, heads_in, rel), GROUP)
    context_got = swap(context)

    resid_own = project_back(context, tokens, gathered)
    resid_got = swap(resid_own)
    activ, slope, ffn_own = ffn_forward(resid_own, resid_got, vec, gathered)
    output, blocks, grad_own, sums = ffn_backward(
        core_id,
        resid_own,
        resid_got,
        vec,
        ffn_own,
        swap(ffn_own),
        cotangent,
        cotangent_got,
        activ,
        swap(activ),
        slope,
        gathered,
    )
    grad_resid1, grad_context, attend_blocks = first_backward(
        core_id,
        resid_own,
        resid_got,
        vec,
        grad_own,
        swap(grad_own),
        context,
        context_got,
        sums,
        gathered,
    )

    summed = lax.psum_scatter(
        blocks.reshape(16, 4 * 64, D), ("x", "z"), scatter_dimension=0, tiled=True
    )
    summed = y_scatter(summed.reshape(2, 2, 64, D))
    grad_expand = summed[:32].T
    grad_reduce = summed[32:].reshape(4, 8, D).transpose(1, 0, 2).reshape(8, FF).T
    attend_blocks, grad_ctx = lax.optimization_barrier(
        (attend_blocks, exchange(grad_context, GROUP))
    )
    attend_sum = exchange(attend_blocks.reshape(64, 8, D + 128), COLUMN + GROUP)

    grads, rel_grad = attend_back(lengths, heads_in, rel, grad_ctx)
    grads, attend_sum = lax.optimization_barrier((grads, attend_sum))
    upper = rel_grad.astype(bf16)
    lower = (rel_grad - upper.astype(f32)).astype(bf16)
    rel_grad = dot_nn(fold, upper) + dot_nn(fold, lower)
    rel_got = swap(rel_grad)
    grads, rel_got = lax.optimization_barrier((exchange(grads, GROUP), rel_got))
    rel_grad = rel_grad + rel_got
    upper = rel_grad.astype(bf16)
    lower = (rel_grad - upper.astype(f32)).astype(bf16)
    position_grads = dot_nn(table_t, upper) + dot_nn(table_t, lower)
    position_grads = position_grads.reshape(2, 4, 64, 256).transpose(1, 0, 2, 3)
    position_grads = ring_scatter(position_grads, "x", 4)
    table_blocks = dot_nt(position_weights, upper) + dot_nt(position_weights, lower)
    table_blocks = table_blocks.astype(bf16).reshape(64, 8, 512)

    keep, give = split(core_id, grads)
    grad_packed = jnp.concatenate([keep, swap(give)], axis=0)
    tokens_part = dot_nn(grad_packed, project_t)
    tokens_got = swap(tokens_part[local:])
    project_blocks = [
        dot_tn(grad_packed, half).astype(bf16).reshape(64, 24, 512)
        for half in (tokens_two[:, :512], tokens_two[:, 512:])
    ]
    blocks = jnp.concatenate(project_blocks + [table_blocks], axis=1)
    blocks, tokens_got, position_grads = lax.optimization_barrier(
        (blocks, tokens_got, position_grads)
    )
    received = jnp.sum(exchange(blocks, COLUMN + GROUP).astype(f32), axis=0)
    grad_project = jnp.concatenate([received[:24], received[24:48]], axis=1).T
    grad_table = received[48:].T
    tokens_grad = grad_resid1 + (tokens_part[:local] + tokens_got)
    position_grads = ring_scatter(position_grads, "yl", 2)
    grad_key, grad_query = position_grads[:, :128], position_grads[:, 128:]
    attend_sum = jnp.sum(attend_sum.astype(f32), axis=0)
    grad_attend = attend_sum[:, :D].T
    vectors = attend_sum[:4, D:].reshape(4, 16, 8)
    vectors = lax.dynamic_index_in_dim(vectors, 8 * core + group, axis=1, keepdims=False)

    return (
        output,
        tokens_grad.astype(bf16),
        grad_project,
        grad_attend,
        vectors[0],
        vectors[1],
        grad_expand,
        grad_reduce,
        vectors[2],
        vectors[3],
        grad_table,
        grad_query,
        grad_key,
    )


def solution(mesh):
    parts = Mesh(mesh.devices.reshape(2, 4, 2, 4, 2), EVERY)
    in_specs = (
        P(EVERY, None),
        P(None, EVERY),
        P(None, EVERY),
        P(EVERY),
        P(EVERY),
        P(None, EVERY),
        P(None, EVERY),
        P(EVERY),
        P(EVERY),
        P(None, EVERY),
        P(DP, GROUP),
        P(DP, GROUP),
        P(DP),
        P(EVERY, None),
    )
    out_specs = (
        P(EVERY, None),
        P(EVERY, None),
        P(None, EVERY),
        P(None, EVERY),
        P(EVERY),
        P(EVERY),
        P(None, EVERY),
        P(None, EVERY),
        P(EVERY),
        P(EVERY),
        P(None, EVERY),
        P(DP, GROUP),
        P(DP, GROUP),
    )
    return jax.shard_map(
        per_device, mesh=parts, in_specs=in_specs, out_specs=out_specs, check_vma=False
    )
```

```python
import math

import jax
import jax.numpy as jnp
import numpy as np
from jax import lax
from jax.experimental import pallas as pl
from jax.experimental.pallas import tpu as pltpu
from jax.sharding import Mesh
from jax.sharding import PartitionSpec as P

D = 1024
HEADS = 16
HEAD_DIM = 64
FF = 4096
SPAN = 256
SEQ = 512
BLOCK = 128
WINDOW = SEQ + BLOCK
STEP = 4

EPS = 1e-07
MASKED = -1e30

DP = ("yl", "x", "core")
GROUP = ("z", "yh")
COLUMN = ("yl", "x")
EVERY = DP + GROUP
CHIPS = ("z", "yh", "yl", "x")
DEVICES = ("core",) + CHIPS
bf16 = jnp.bfloat16
f32 = jnp.float32


def bucket_values(offset, span):
    middle = span // 2
    absolute = np.where((offset < middle) & (offset > -middle), middle - 1, np.abs(offset))
    log_place = (
        np.ceil(np.log(absolute / middle) / np.log((2 * span - 1) / middle) * (middle - 1)) + middle
    )
    buckets = np.where(absolute <= middle, offset, log_place * np.sign(offset)).astype(np.int64)
    return np.clip(buckets + span, 0, 2 * span - 1).astype(np.int32)


def normalize(value, gain, shift):
    center = value - jnp.mean(value, axis=-1, keepdims=True)
    inverse = lax.rsqrt(jnp.mean(center * center, axis=-1, keepdims=True) + EPS)
    scaled = center * inverse
    return (scaled * gain + shift, scaled, inverse)


def normalize_back(incoming, scaled, inverse, gain):
    grad_scaled = incoming * gain
    middle = (
        grad_scaled
        - jnp.mean(grad_scaled, axis=-1, keepdims=True)
        - scaled * jnp.mean(grad_scaled * scaled, axis=-1, keepdims=True)
    )
    return inverse * middle


def dot_nn(left, right):
    return lax.dot_general(left, right, (((1,), (0,)), ((), ())), preferred_element_type=f32)


def dot_nt(left, right):
    return lax.dot_general(left, right, (((1,), (1,)), ((), ())), preferred_element_type=f32)


def dot_tn(left, right):
    return lax.dot_general(left, right, (((0,), (0,)), ((), ())), preferred_element_type=f32)


def window(block):
    start = SEQ - BLOCK - BLOCK * block
    return slice(start, start + WINDOW)


def rows(block):
    return slice(BLOCK * block, BLOCK * (block + 1))


def skew(values):
    return pltpu.roll(values, SEQ + 1, 1, stride=1, stride_axis=0)[:, :SEQ]


def unskew(values):
    wide = jnp.concatenate([values, jnp.zeros((BLOCK, BLOCK), f32)], axis=1)
    return pltpu.roll(wide, 0, 1, stride=1, stride_axis=0)


def turn(mirror, values):
    upper = values.astype(bf16)
    return dot_nn(mirror, upper) + dot_nn(mirror, (values - upper.astype(f32)).astype(bf16))


def one_head(value, head):
    lane = lax.broadcasted_iota(jnp.int32, value.shape, 1)
    return jnp.where(lane // HEAD_DIM == head, value, jnp.zeros_like(value))


def query_bias(key, rel_queries, bias):
    for block in range(SEQ // BLOCK):
        by_offset = dot_nt(key[rows(block)], rel_queries[window(block)])
        bias[:, rows(block)] = skew(by_offset).T


def probabilities(query, key, rel_keys, bias, block, length):
    part = query[rows(block)]
    logits = dot_nt(part, key) + skew(dot_nt(part, rel_keys[window(block)])) + bias[rows(block)]
    logits = logits * (1.0 / math.sqrt(3 * HEAD_DIM))
    column = lax.broadcasted_iota(jnp.int32, logits.shape, 1)
    logits = jnp.where(column < length, logits, MASKED)
    exponent = jnp.exp(logits - jnp.max(logits, axis=1, keepdims=True))
    return exponent * (1.0 / jnp.sum(exponent, axis=1, keepdims=True))


def attend_kernel(lengths, heads_in, rel, context, bias):
    length = lengths[pl.program_id(0)]
    query, key, values = (heads_in[:, part].reshape(SEQ, 128) for part in range(3))
    rel_keys, rel_queries = rel[:, :128], rel[:, 128:]
    total = [jnp.zeros((BLOCK, 128), f32) for _ in range(SEQ // BLOCK)]
    for head in range(2):
        query_h, key_h, values_h = (one_head(part, head) for part in (query, key, values))
        query_bias(key_h, rel_queries, bias)
        for block in range(SEQ // BLOCK):
            probs = probabilities(query_h, key, rel_keys, bias, block, length)
            total[block] = total[block] + dot_nn(probs.astype(bf16), values_h)
    for block in range(SEQ // BLOCK):
        context[block] = total[block].astype(bf16)


def attend_back_kernel(
    lengths, heads_in, rel, grad_context, grads, grad_rel, bias, probs_ref, grad_ref
):
    length = lengths[pl.program_id(0)]
    query, key, values = (heads_in[:, part].reshape(SEQ, 128) for part in range(3))
    grad_ctx = grad_context[...].reshape(SEQ, 128)
    rel_keys, rel_queries = rel[:, :128], rel[:, 128:]
    blocks = SEQ // BLOCK
    first = lax.broadcasted_iota(jnp.int32, (BLOCK, BLOCK), 0)
    second = lax.broadcasted_iota(jnp.int32, (BLOCK, BLOCK), 1)
    mirror = jnp.where(first + second == BLOCK - 1, 1.0, 0.0).astype(bf16)

    @pl.when(pl.program_id(0) == 0)
    def _():
        grad_rel[...] = jnp.zeros_like(grad_rel)

    queries, keys, ctxs = (
        [one_head(part, head) for head in range(2)] for part in (query, key, grad_ctx)
    )
    rel_keys_of = [one_head(rel_keys, head) for head in range(2)]
    rel_queries_of = [one_head(rel_queries, head) for head in range(2)]
    for head in range(2):
        query_bias(keys[head], rel_queries, bias.at[head])
    for block in range(blocks):
        grad_q, turned, rel_part = 0.0, 0.0, 0.0
        for head in range(2):
            probs = probabilities(queries[head], key, rel_keys, bias.at[head], block, length)
            probs_ref[head, rows(block)] = probs.astype(bf16)
            grad_probs = dot_nt(ctxs[head][rows(block)], values)
            inner = jnp.sum(probs * grad_probs, axis=1, keepdims=True)
            grad = (probs * (grad_probs - inner) * (1.0 / math.sqrt(3 * HEAD_DIM))).astype(bf16)
            grad_ref[head, rows(block)] = grad
            by_offset = unskew(dot_nn(mirror, grad)).astype(bf16)
            grad_q = grad_q + dot_nn(grad, keys[head])
            turned = turned + dot_nn(by_offset, rel_keys_of[head][window(block)])
            mirrored = dot_nn(mirror, queries[head][rows(block)]).astype(bf16)
            rel_part = rel_part + dot_tn(by_offset, mirrored)
        grad_rel[window(block), :128] += rel_part
        grads[block, 0] = (grad_q + turn(mirror, turned)).astype(bf16)
    for block in range(blocks):
        grad_k, grad_v, turned, rel_part = 0.0, 0.0, 0.0, 0.0
        for head in range(2):
            grad = grad_ref[head, :, rows(block)]
            by_offset = unskew(dot_nt(mirror, grad)).astype(bf16)
            grad_k = grad_k + dot_tn(grad, queries[head])
            turned = turned + dot_nn(by_offset, rel_queries_of[head][window(block)])
            grad_v = grad_v + dot_tn(probs_ref[head, :, rows(block)], ctxs[head])
            mirrored = dot_nn(mirror, keys[head][rows(block)]).astype(bf16)
            rel_part = rel_part + dot_tn(by_offset, mirrored)
        grad_rel[window(block), 128:] += rel_part
        grads[block, 1] = (grad_k + turn(mirror, turned)).astype(bf16)
        grads[block, 2] = grad_v.astype(bf16)


def attend(lengths, heads_in, rel):
    return pl.pallas_call(
        attend_kernel,
        grid=(2,),
        in_specs=[
            pl.BlockSpec(memory_space=pltpu.SMEM),
            pl.BlockSpec((4, 3, 128, 128), lambda row: (row, 0, 0, 0)),
            pl.BlockSpec((2 * SEQ, 256), lambda row: (0, 0)),
        ],
        out_specs=pl.BlockSpec((4, 128, 128), lambda row: (row, 0, 0)),
        out_shape=jax.ShapeDtypeStruct((8, 128, 128), bf16),
        scratch_shapes=[pltpu.VMEM((SEQ, SEQ), f32)],
        compiler_params=pltpu.CompilerParams(vmem_limit_bytes=48 * 2**20),
        name="attend",
    )(lengths, heads_in, rel)


def attend_back(lengths, heads_in, rel, grad_context):
    return pl.pallas_call(
        attend_back_kernel,
        grid=(2,),
        in_specs=[
            pl.BlockSpec(memory_space=pltpu.SMEM),
            pl.BlockSpec((4, 3, 128, 128), lambda row: (row, 0, 0, 0)),
            pl.BlockSpec((2 * SEQ, 256), lambda row: (0, 0)),
            pl.BlockSpec((4, 128, 128), lambda row: (row, 0, 0)),
        ],
        out_specs=[
            pl.BlockSpec((4, 3, 128, 128), lambda row: (row, 0, 0, 0)),
            pl.BlockSpec((2 * SEQ, 256), lambda row: (0, 0)),
        ],
        out_shape=[
            jax.ShapeDtypeStruct((8, 3, 128, 128), bf16),
            jax.ShapeDtypeStruct((2 * SEQ, 256), f32),
        ],
        scratch_shapes=[
            pltpu.VMEM((2, SEQ, SEQ), f32),
            pltpu.VMEM((2, SEQ, SEQ), bf16),
            pltpu.VMEM((2, SEQ, SEQ), bf16),
        ],
        compiler_params=pltpu.CompilerParams(vmem_limit_bytes=48 * 2**20),
        name="attend_back",
    )(lengths, heads_in, rel, grad_context)


def owner_rows(block):
    wide = block.astype(f32).reshape(8, STEP, 2, 8, block.shape[-1])
    return wide.transpose(1, 2, 0, 3, 4).reshape(STEP * 128, block.shape[-1]).astype(bf16)


def project_back_kernel(context, tokens, weights, resid):
    rows_in = jnp.concatenate([context[group] for group in range(8)], axis=1)
    resid[...] = tokens[...].astype(f32) + dot_nt(rows_in, owner_rows(weights[...]))


def project_back(context, tokens, gathered):
    return pl.pallas_call(
        project_back_kernel,
        grid=(8 // STEP,),
        in_specs=[
            pl.BlockSpec((8, 128, 128), lambda k: (0, 0, 0)),
            pl.BlockSpec((128, STEP * 128), lambda k: (0, k)),
            pl.BlockSpec((8, STEP, 16, D), lambda k: (0, k, 4, 0)),
        ],
        out_specs=pl.BlockSpec((128, STEP * 128), lambda k: (0, k)),
        out_shape=jax.ShapeDtypeStruct((128, D), f32),
        compiler_params=pltpu.CompilerParams(vmem_limit_bytes=48 * 2**20),
        name="project_back",
    )(context, tokens, gathered)


def ffn_kernel(mine, theirs, vec, expand, reduce, act, slope, partial, sent, low):
    phase, k = pl.program_id(0), pl.program_id(1)

    @pl.when((phase == 0) & (k == 0))
    def _():
        for half, resid in enumerate((mine, theirs)):
            first_norm, scaled, inverse = normalize(resid[...], vec[0:1], vec[1:2])
            low[128 * half : 128 * (half + 1)] = first_norm.astype(bf16)

    @pl.when(phase == 0)
    def _():
        for column in range(STEP):
            inner = dot_nt(low[...], expand[:, column].reshape(256, D))
            spread_in = 0.5 + 0.5 * lax.erf(inner * math.sqrt(0.5))
            act[STEP * k + column] = (inner * spread_in).astype(bf16)
            density = jnp.exp(-0.5 * inner * inner) * (1.0 / math.sqrt(2.0 * math.pi))
            slope[column] = spread_in + inner * density

    @pl.when(phase == 1)
    def _():
        total = jnp.zeros((256, STEP * 128), f32)
        for half in range(2):
            rows_in = jnp.concatenate([act[4 * half + part] for part in range(4)], axis=1)
            weights = owner_rows(reduce[:, :, 16 * half : 16 * (half + 1)])
            total = total + dot_nt(rows_in, weights)
        partial[...] = total
        sent[...] = total.astype(bf16)


def ffn_forward(mine, theirs, vec, gathered):
    whole = lambda phase, k: (0, 0)
    return pl.pallas_call(
        ffn_kernel,
        grid=(2, 8 // STEP),
        in_specs=[
            pl.BlockSpec((128, D), whole),
            pl.BlockSpec((128, D), whole),
            pl.BlockSpec((4, D), whole),
            pl.BlockSpec((8, STEP, 32, D), lambda phase, k: (0, jnp.where(phase == 0, k, 8 // STEP - 1), 0, 0)),
            pl.BlockSpec((8, STEP, 32, D), lambda phase, k: (0, jnp.where(phase == 0, 0, k), 1, 0)),
        ],
        out_specs=[
            pl.BlockSpec((8, 256, 256), lambda phase, k: (0, 0, 0)),
            pl.BlockSpec((STEP, 256, 256), lambda phase, k: (jnp.where(phase == 0, k, 8 // STEP - 1), 0, 0)),
            pl.BlockSpec((256, STEP * 128), lambda phase, k: (0, jnp.where(phase == 0, 0, k))),
            pl.BlockSpec((256, STEP * 128), lambda phase, k: (0, jnp.where(phase == 0, 0, k))),
        ],
        out_shape=[
            jax.ShapeDtypeStruct((8, 256, 256), bf16),
            jax.ShapeDtypeStruct((8, 256, 256), f32),
            jax.ShapeDtypeStruct((256, D), f32),
            jax.ShapeDtypeStruct((256, D), bf16),
        ],
        scratch_shapes=[pltpu.VMEM((256, D), bf16)],
        compiler_params=pltpu.CompilerParams(vmem_limit_bytes=48 * 2**20),
        name="ffn_forward",
    )(mine, theirs, vec, gathered, gathered)


def own_half(core, wide):
    return jnp.where(core[0] == 0, wide[:, :64], wide[:, 64:])


def ffn_back_kernel(
    core,
    mine,
    theirs,
    vec,
    ffn_own,
    ffn_got,
    cot_own,
    cot_got,
    act_own,
    act_got,
    slope,
    expand,
    reduce,
    output,
    blocks,
    partial,
    sent,
    sums,
    low,
    grad_ffn,
    grad_act,
    act,
):
    phase, k = pl.program_id(0), pl.program_id(1)

    @pl.when((phase == 0) & (k == 0))
    def _():
        sums[...] = jnp.zeros_like(sums)
        for half, (resid, cot) in enumerate(((mine, cot_own), (theirs, cot_got))):
            span = slice(128 * half, 128 * (half + 1))
            cross = slice(128 * (1 - half), 128 * (2 - half))
            first_norm, scaled, inverse = normalize(resid[...], vec[0:1], vec[1:2])
            low[span] = first_norm.astype(bf16)
            resid2 = first_norm + (ffn_own[span] + ffn_got[cross])
            normed, scaled, inverse = normalize(resid2, vec[2:3], vec[3:4])
            grad = cot[...].astype(f32)
            if half == 0:
                output[...] = normed.astype(bf16)
            sums[2:3] += jnp.sum(grad * scaled, axis=0, keepdims=True)
            sums[3:4] += jnp.sum(grad, axis=0, keepdims=True)
            grad = normalize_back(grad, scaled, inverse, vec[2:3])
            partial[span] = 0.5 * grad
            grad = grad.astype(bf16)
            for chunk in range(8 // STEP):
                grad_ffn[chunk, span] = grad[:, STEP * 128 * chunk : STEP * 128 * (chunk + 1)]
        grad_act[...] = jnp.zeros_like(grad_act)
        for chunk in range(8):
            own, got = act_own[chunk], act_got[chunk]
            got = jnp.concatenate([got[128:], got[:128]], axis=0)
            start = 512 * (chunk % 2)
            act[chunk // 2, :, start : start + 256] = jnp.where(core[0] == 0, own, got)
            act[chunk // 2, :, start + 256 : start + 512] = jnp.where(core[0] == 0, got, own)

    @pl.when(phase == 0)
    def _():
        grad = grad_ffn[k]
        own = [own_half(core, grad[:, 128 * column : 128 * (column + 1)]) for column in range(STEP)]
        own = jnp.concatenate(own, axis=1)
        for half in range(2):
            weights = owner_rows(reduce[:, :, 16 * half : 16 * (half + 1)])
            for part in range(4):
                grad_act[4 * half + part] += dot_nn(grad, weights[:, 256 * part : 256 * (part + 1)])
            made = [dot_tn(own, act[2 * half + part]).reshape(STEP, 8, 8, D) for part in range(2)]
            made = jnp.concatenate(made, axis=2).astype(bf16).reshape(STEP, 4, 2, 16, D)
            blocks[:, :, :, 0, 16 * half : 16 * (half + 1)] = made

    @pl.when(phase == 1)
    def _():
        for column in range(STEP):
            weights = expand[:, column].reshape(256, D)
            grad = (slope[column] * grad_act[STEP * k + column]).astype(bf16)
            made = dot_tn(grad, low[...]).astype(bf16)
            blocks[column, :, :, 0] = made.reshape(4, 2, 32, D)
            partial[...] += dot_nn(grad, weights)

    @pl.when((phase == 1) & (k == 8 // STEP - 1))
    def _():
        sent[...] = partial[...].astype(bf16)


def ffn_backward(
    core, mine, theirs, vec, ffn_own, ffn_got, cot_own, cot_got, act_own, act_got, slope, gathered
):
    whole = lambda phase, k: (0, 0)
    return pl.pallas_call(
        ffn_back_kernel,
        grid=(2, 8 // STEP),
        in_specs=[
            pl.BlockSpec(memory_space=pltpu.SMEM),
            pl.BlockSpec((128, D), whole),
            pl.BlockSpec((128, D), whole),
            pl.BlockSpec((4, D), whole),
            pl.BlockSpec((256, D), whole),
            pl.BlockSpec((256, D), whole),
            pl.BlockSpec((128, D), whole),
            pl.BlockSpec((128, D), whole),
            pl.BlockSpec((8, 256, 256), lambda phase, k: (0, 0, 0)),
            pl.BlockSpec((8, 256, 256), lambda phase, k: (0, 0, 0)),
            pl.BlockSpec((STEP, 256, 256), lambda phase, k: (jnp.where(phase == 0, 0, k), 0, 0)),
            pl.BlockSpec((8, STEP, 32, D), lambda phase, k: (0, jnp.where(phase == 0, 0, k), 0, 0)),
            pl.BlockSpec((8, STEP, 32, D), lambda phase, k: (0, jnp.where(phase == 0, k, 8 // STEP - 1), 1, 0)),
        ],
        out_specs=[
            pl.BlockSpec((128, D), whole),
            pl.BlockSpec(
                (STEP, 4, 2, 1, 32, D),
                lambda phase, k: (k % (4 // STEP), 0, 0, k // (4 // STEP), 1 - phase, 0),
            ),
            pl.BlockSpec((256, D), whole),
            pl.BlockSpec((256, D), whole),
            pl.BlockSpec((8, D), whole),
        ],
        out_shape=[
            jax.ShapeDtypeStruct((128, D), bf16),
            jax.ShapeDtypeStruct((4, 4, 2, 2, 64, D), bf16),
            jax.ShapeDtypeStruct((256, D), f32),
            jax.ShapeDtypeStruct((256, D), bf16),
            jax.ShapeDtypeStruct((8, D), f32),
        ],
        scratch_shapes=[
            pltpu.VMEM((256, D), bf16),
            pltpu.VMEM((8 // STEP, 256, STEP * 128), bf16),
            pltpu.VMEM((8, 256, 256), f32),
            pltpu.VMEM((4, 256, D), bf16),
        ],
        compiler_params=pltpu.CompilerParams(vmem_limit_bytes=56 * 2**20),
        name="ffn_backward",
    )(
        core,
        mine,
        theirs,
        vec,
        ffn_own,
        ffn_got,
        cot_own,
        cot_got,
        act_own,
        act_got,
        slope,
        gathered,
        gathered,
    )


def first_back_kernel(
    core,
    mine,
    theirs,
    vec,
    grad_own,
    grad_got,
    ctx_own,
    ctx_got,
    sums,
    weights,
    grad_resid,
    grad_context,
    blocks,
    grad_low,
    total,
    vec_sums,
):
    k = pl.program_id(0)

    @pl.when(k == 0)
    def _():
        found = sums[...]
        place = lax.broadcasted_iota(jnp.int32, (8, D), 0)
        for half, resid in enumerate((mine, theirs)):
            span = slice(128 * half, 128 * (half + 1))
            cross = slice(128 * (1 - half), 128 * (2 - half))
            normed, scaled, inverse = normalize(resid[...], vec[0:1], vec[1:2])
            grad = grad_own[span] + grad_got[cross]
            found += jnp.where(place == 0, jnp.sum(grad * scaled, axis=0, keepdims=True), 0.0)
            found += jnp.where(place == 1, jnp.sum(grad, axis=0, keepdims=True), 0.0)
            grad = normalize_back(grad, scaled, inverse, vec[0:1])
            if half == 0:
                grad_resid[...] = grad
            grad = grad.astype(bf16)
            for chunk in range(8 // STEP):
                grad_low[chunk, span] = grad[:, STEP * 128 * chunk : STEP * 128 * (chunk + 1)]
        for chunk in range(8):
            vec_sums[chunk] = found[:, 128 * chunk : 128 * (chunk + 1)]
        total[...] = jnp.zeros_like(total)

    grad = grad_low[k]
    total[...] += dot_nn(grad[:128], owner_rows(weights[...]))
    ctx = [jnp.concatenate([part[group] for group in range(8)], axis=1) for part in (ctx_own, ctx_got)]
    own = [own_half(core, grad[:, 128 * column : 128 * (column + 1)]) for column in range(STEP)]
    made = dot_tn(jnp.concatenate(own, axis=1), jnp.concatenate(ctx, axis=0)).reshape(STEP, 8, 8, D)
    for column in range(STEP):
        row = jnp.broadcast_to(vec_sums[STEP * k + column][None], (8, 8, 128))
        blocks[column] = jnp.concatenate([made[column], row], axis=-1).astype(bf16)

    @pl.when(k == 8 // STEP - 1)
    def _():
        for group in range(8):
            grad_context[group] = total[:, 128 * group : 128 * (group + 1)].astype(bf16)


def first_backward(
    core, mine, theirs, vec, grad_own, grad_got, ctx_own, ctx_got, sums, gathered
):
    whole = lambda k: (0, 0)
    return pl.pallas_call(
        first_back_kernel,
        grid=(8 // STEP,),
        in_specs=[
            pl.BlockSpec(memory_space=pltpu.SMEM),
            pl.BlockSpec((128, D), whole),
            pl.BlockSpec((128, D), whole),
            pl.BlockSpec((4, D), whole),
            pl.BlockSpec((256, D), whole),
            pl.BlockSpec((256, D), whole),
            pl.BlockSpec((8, 128, 128), lambda k: (0, 0, 0)),
            pl.BlockSpec((8, 128, 128), lambda k: (0, 0, 0)),
            pl.BlockSpec((8, D), whole),
            pl.BlockSpec((8, STEP, 16, D), lambda k: (0, k, 4, 0)),
        ],
        out_specs=[
            pl.BlockSpec((128, D), whole),
            pl.BlockSpec((8, 128, 128), lambda k: (0, 0, 0)),
            pl.BlockSpec((STEP, 8, 8, D + 128), lambda k: (k, 0, 0, 0)),
        ],
        out_shape=[
            jax.ShapeDtypeStruct((128, D), f32),
            jax.ShapeDtypeStruct((8, 128, 128), bf16),
            jax.ShapeDtypeStruct((8, 8, 8, D + 128), bf16),
        ],
        scratch_shapes=[
            pltpu.VMEM((8 // STEP, 256, STEP * 128), bf16),
            pltpu.VMEM((128, D), f32),
            pltpu.VMEM((8, 8, 128), f32),
        ],
        compiler_params=pltpu.CompilerParams(vmem_limit_bytes=56 * 2**20),
        name="first_backward",
    )(core, mine, theirs, vec, grad_own, grad_got, ctx_own, ctx_got, sums, gathered)


def two_parts(value):
    upper = value.astype(bf16)
    return upper, (value - upper.astype(f32)).astype(bf16)


def swap(value):
    return lax.ppermute(value, "core", [(0, 1), (1, 0)])


def exchange(value, axes):
    return lax.all_to_all(value, axes, 0, 0, tiled=True)


def shifted(value, axis, size, step):
    return lax.ppermute(value, axis, [(i, (i + step) % size) for i in range(size)])


def stacked(value, axis):
    size = lax.axis_size(axis)
    return jnp.stack([value] + [shifted(value, axis, size, step) for step in range(1, size)])


def places_back(axis):
    size = lax.axis_size(axis)
    return (lax.axis_index(axis) - jnp.arange(size)) % size


def pick(blocks, index):
    return blocks.at[index.reshape(-1)].get(mode="promise_in_bounds")


def spread(value, axes):
    return exchange(jnp.broadcast_to(value[None], (8,) + value.shape), axes)


def gather_projection(rows_t, table_rows, position_rows):
    first = spread(jnp.concatenate([rows_t[:, :512], table_rows], axis=0), GROUP)
    second = stacked(stacked(rows_t[:, 512:], "x"), "yl").reshape(8 * 24, 512)
    first = jnp.concatenate([first.reshape(256, 512), position_rows], axis=0)
    first, second = lax.optimization_barrier((stacked(first, "yl"), second))
    first = first.reshape(2, 9, 32, 512)
    table = jnp.concatenate([first[:, :8, 24:].reshape(2, 64, 512), first[:, 8]], axis=1)
    first = stacked(first[:, :8, :24], "x").reshape(8, 8, 24, 512)
    second = spread(second, GROUP).reshape(8, 8, 24, 512)
    table = stacked(table, "x").reshape(8, 96, 512)
    x, yl = places_back("x")[None], places_back("yl")[:, None]
    order = jnp.stack([(yl + 2 * x).reshape(-1), (x + 4 * yl).reshape(-1)])
    table = table.at[order[0]].get(mode="promise_in_bounds")
    return first, second, order, table[:, :64].reshape(512, 512), table[:, 64:]


def pack_kernel(core, expand, reduce, attend, vectors, got, packet):
    first = core[0] == 0
    packet[:32] = expand[...]
    inner = []
    for source in (reduce, got):
        spans = [source[:, 512 * k : 512 * (k + 1)].astype(f32) for k in range(8)]
        inner.append([jnp.where(first, span[:, :256], span[:, 256:]) for span in spans])
    for half in range(2):
        parts = [jnp.concatenate(rows_in[4 * half : 4 * half + 4], axis=1) for rows_in in inner]
        low, high = jnp.where(first, *parts), jnp.where(first, *reversed(parts))
        joined = jnp.concatenate([low, high], axis=0).astype(bf16)
        packet[32 + 16 * half : 48 + 16 * half] = joined
    own, other = attend[...].astype(f32), got[:, FF : FF + D].astype(f32)
    joined = jnp.concatenate([jnp.where(first, own, other), jnp.where(first, other, own)], axis=0)
    packet[64:80] = joined.astype(bf16)
    own, other = vectors[:4].astype(f32), got[:4, FF + D :].astype(f32)
    joined = jnp.concatenate([jnp.where(first, own, other), jnp.where(first, other, own)], axis=0)
    packet[80:] = jnp.concatenate([joined, jnp.zeros((8, D - 128), f32)], axis=1).astype(bf16)


def pack(core, expand, reduce, attend, vectors, got):
    return pl.pallas_call(
        pack_kernel,
        in_specs=[pl.BlockSpec(memory_space=pltpu.SMEM)]
        + [pl.BlockSpec(memory_space=pltpu.VMEM)] * 5,
        out_specs=pl.BlockSpec(memory_space=pltpu.VMEM),
        out_shape=jax.ShapeDtypeStruct((88, D), bf16),
        compiler_params=pltpu.CompilerParams(vmem_limit_bytes=32 * 2**20),
        name="pack",
    )(core, expand, reduce, attend, vectors, got)


def project_kernel(order, mine, theirs, first, second, packed, rows_out):
    tokens = jnp.concatenate([mine[...], theirs[...]], axis=0)
    low = first[0].astype(f32).reshape(192, 512).astype(bf16)
    high = second[:, 0].astype(f32).reshape(192, 512).astype(bf16)
    made = dot_nt(tokens[:, :512], low) + dot_nt(tokens[:, 512:], high)
    packed[0] = made.astype(bf16)
    rows_out[:, :512] = low
    rows_out[:, 512:] = high


def project(order, mine, theirs, first, second):
    return pl.pallas_call(
        project_kernel,
        grid_spec=pltpu.PrefetchScalarGridSpec(
            num_scalar_prefetch=1,
            grid=(8,),
            in_specs=[
                pl.BlockSpec((128, D), lambda k, order: (0, 0)),
                pl.BlockSpec((128, D), lambda k, order: (0, 0)),
                pl.BlockSpec((1, 8, 24, 512), lambda k, order: (order[0, k], 0, 0, 0)),
                pl.BlockSpec((8, 1, 24, 512), lambda k, order: (0, order[1, k], 0, 0)),
            ],
            out_specs=[
                pl.BlockSpec((1, 256, 192), lambda k, order: (k, 0, 0)),
                pl.BlockSpec((192, D), lambda k, order: (k, 0)),
            ],
        ),
        out_shape=[
            jax.ShapeDtypeStruct((8, 256, 192), bf16),
            jax.ShapeDtypeStruct((1536, D), bf16),
        ],
        compiler_params=pltpu.CompilerParams(vmem_limit_bytes=32 * 2**20),
        name="project",
    )(order, mine, theirs, first, second)


def arrange_kernel(core, mine, theirs, heads):
    for column in range(8):
        own, other = mine[column].astype(f32), theirs[column].astype(f32)
        first = core[0] == 0
        joined = jnp.concatenate(
            [jnp.where(first, own, other), jnp.where(first, other, own)], axis=1
        )
        for place in range(3):
            chunk = 3 * column + place
            heads[chunk % 8, chunk // 8] = joined[:, 128 * place : 128 * (place + 1)].astype(bf16)


def arrange(core, mine, theirs):
    return pl.pallas_call(
        arrange_kernel,
        in_specs=[
            pl.BlockSpec(memory_space=pltpu.SMEM),
            pl.BlockSpec(memory_space=pltpu.VMEM),
            pl.BlockSpec(memory_space=pltpu.VMEM),
        ],
        out_specs=pl.BlockSpec(memory_space=pltpu.VMEM),
        out_shape=jax.ShapeDtypeStruct((8, 3, 128, 128), bf16),
        compiler_params=pltpu.CompilerParams(vmem_limit_bytes=32 * 2**20),
        name="arrange",
    )(core, mine, theirs)


def project_grad_kernel(
    keep, got, tokens_own, tokens_got, weights, table, blocks, part_own, part_theirs
):
    tokens = jnp.concatenate([tokens_own[...], tokens_got[...]], axis=0)
    part_own[...] = dot_nn(keep[...], weights[...])
    part_theirs[...] = dot_nn(got[...], weights[...]).astype(bf16)
    for step in range(4):
        span = slice(384 * step, 384 * (step + 1))
        grads = jnp.concatenate([keep[:, span], got[:, span]], axis=0)
        made = dot_tn(grads, tokens).reshape(16, 24, D)
        rest = table[128 * step : 128 * (step + 1)].reshape(16, 8, 512)
        made = jnp.concatenate([made[..., :512], made[..., 512:], rest], axis=1)
        blocks[16 * step : 16 * (step + 1)] = made.astype(bf16)


def project_grad(keep, got, tokens_own, tokens_got, weights, table):
    return pl.pallas_call(
        project_grad_kernel,
        in_specs=[pl.BlockSpec(memory_space=pltpu.VMEM)] * 6,
        out_specs=[pl.BlockSpec(memory_space=pltpu.VMEM)] * 3,
        out_shape=[
            jax.ShapeDtypeStruct((64, 56, 512), bf16),
            jax.ShapeDtypeStruct((128, D), f32),
            jax.ShapeDtypeStruct((128, D), bf16),
        ],
        compiler_params=pltpu.CompilerParams(vmem_limit_bytes=48 * 2**20),
        name="project_grad",
    )(keep, got, tokens_own, tokens_got, weights, table)


def ring_scatter(blocks, axis, size, dtype=f32):
    place = lax.axis_index(axis)
    total = lax.dynamic_index_in_dim(blocks, place, 0, keepdims=False).astype(f32)
    for step in range(1, size):
        sent = lax.dynamic_index_in_dim(blocks, (place + step) % size, 0, keepdims=False)
        total = total + shifted(sent, axis, size, step).astype(f32)
    return total.astype(dtype)


def y_scatter(blocks):
    place = 2 * lax.axis_index("yh") + lax.axis_index("yl")
    total = lax.dynamic_index_in_dim(blocks, place, 0, keepdims=False).astype(f32)

    def on_mesh(y):
        return 2 * (y % 2) + y // 2

    for step in range(1, 4):
        sent = lax.dynamic_index_in_dim(blocks, (place + step) % 4, 0, keepdims=False)
        ring = [(on_mesh(y), on_mesh((y + step) % 4)) for y in range(4)]
        total = total + lax.ppermute(sent, ("yl", "yh"), ring).astype(f32)
    return total


def split_kernel(core, heads, keep, give):
    for column in range(8):
        chunks = [3 * column + place for place in range(3)]
        joined = jnp.concatenate(
            [heads[chunk % 8, chunk // 8].astype(f32) for chunk in chunks], axis=1
        )
        first = core[0] == 0
        zero, one = joined[:, :192], joined[:, 192:]
        span = slice(192 * column, 192 * (column + 1))
        keep[:, span] = jnp.where(first, zero, one).astype(bf16)
        give[:, span] = jnp.where(first, one, zero).astype(bf16)


def split(core, heads):
    return pl.pallas_call(
        split_kernel,
        in_specs=[
            pl.BlockSpec(memory_space=pltpu.SMEM),
            pl.BlockSpec(memory_space=pltpu.VMEM),
        ],
        out_specs=[pl.BlockSpec(memory_space=pltpu.VMEM)] * 2,
        out_shape=[jax.ShapeDtypeStruct((128, 1536), bf16)] * 2,
        compiler_params=pltpu.CompilerParams(vmem_limit_bytes=32 * 2**20),
        name="split",
    )(core, heads)


def per_device(
    tokens,
    w_project,
    w_attend,
    first_gain,
    first_shift,
    w_expand,
    w_reduce,
    second_gain,
    second_shift,
    position_table,
    w_query,
    w_key,
    lengths,
    cotangent,
):
    core = lax.axis_index("core")
    group = lax.axis_index(GROUP)
    local = tokens.shape[0]
    core_id = core.reshape(1)
    pair = 2 * local
    column_bucket = bucket_values(SEQ - 1 - np.arange(2 * SEQ - 1), SPAN)
    fold = np.append(column_bucket, -1)[None, :] == np.arange(2 * SPAN)[:, None]
    fold = jnp.asarray(fold.astype(np.float32)).astype(bf16)

    def by_core(zero, one):
        return jnp.where(core == 0, zero, one)

    def in_order(mine, theirs):
        return by_core(mine, theirs), by_core(theirs, mine)

    cotangent_got = swap(cotangent)
    tokens_got = swap(tokens)
    weights_own = jnp.concatenate([w_key, w_query], axis=1)
    first, second, order, table_t, position_rows = gather_projection(
        w_project.T,
        position_table.T,
        jnp.concatenate([weights_own[:32], weights_own[32:]], axis=1),
    )
    position_weights = jnp.stack([position_rows[..., :256], position_rows[..., 256:]], axis=1)
    position_weights = position_weights.reshape(512, 256)

    vectors = jnp.stack([first_gain, first_shift, second_gain, second_shift])
    vectors = jnp.pad(vectors, ((0, 4), (0, 128 - 8)))
    reduce_rows = w_reduce.T
    got = swap(jnp.concatenate([reduce_rows, w_attend.T, vectors], axis=1))
    packet = pack(core_id, w_expand.T, reduce_rows, w_attend.T, vectors, got)
    gathered = lax.all_gather(packet, CHIPS, axis=0, tiled=False).reshape(8, 8, 88, D)
    vec = gathered[..., 80:, :8].reshape(8, 8, 2, 4, 8).transpose(3, 1, 2, 0, 4)
    vec = vec.reshape(4, D).astype(f32)
    gain_one, shift_one, gain_two, shift_two = vec[0], vec[1], vec[2], vec[3]

    packed, project_t = project(order, tokens, tokens_got, first, second)
    heads_in = exchange(arrange(core_id, packed[:, :local], swap(packed[:, local:])), GROUP)
    rel = dot_tn(table_t, position_weights)
    rel = dot_tn(fold, (rel + swap(rel)).astype(bf16)).astype(bf16)
    context = exchange(attend(lengths, heads_in, rel), GROUP)
    context_got = swap(context)

    resid_own = project_back(context, tokens, gathered)
    resid_got = swap(resid_own)
    activ, slope, ffn_own, ffn_sent = ffn_forward(resid_own, resid_got, vec, gathered)
    output, blocks, grad_own, grad_sent, sums = ffn_backward(
        core_id,
        resid_own,
        resid_got,
        vec,
        ffn_own,
        swap(ffn_sent),
        cotangent,
        cotangent_got,
        activ,
        swap(activ),
        slope,
        gathered,
    )
    grad_resid1, grad_context, attend_blocks = first_backward(
        core_id,
        resid_own,
        resid_got,
        vec,
        grad_own,
        swap(grad_sent),
        context,
        context_got,
        sums,
        gathered,
    )

    summed = lax.psum_scatter(
        blocks.reshape(16, 4 * 64, D), ("x", "z"), scatter_dimension=0, tiled=True
    )
    attend_blocks, grad_ctx = lax.optimization_barrier(
        (attend_blocks, exchange(grad_context, GROUP))
    )
    attend_sum = exchange(attend_blocks.reshape(64, 8, D + 128), COLUMN + GROUP)

    grads, rel_grad = attend_back(lengths, heads_in, rel, grad_ctx)
    grads, attend_sum = lax.optimization_barrier((grads, attend_sum))
    attend_sum = jnp.sum(attend_sum.astype(f32), axis=0)
    grad_attend = attend_sum[:, :D].T
    vectors = attend_sum[:4, D:].reshape(4, 16, 8)
    vectors = lax.dynamic_index_in_dim(vectors, 8 * core + group, axis=1, keepdims=False)
    keep, give = split(core_id, exchange(grads, GROUP))
    rel_grad = sum(dot_nn(fold, part) for part in two_parts(rel_grad))
    rel_grad = two_parts(rel_grad + swap(rel_grad))
    position_grads = sum(dot_nn(table_t, part) for part in rel_grad)
    position_grads = position_grads.reshape(2, 4, 64, 256).transpose(1, 0, 2, 3)
    position_grads = ring_scatter(position_grads, "x", 4)
    table_blocks = sum(dot_nt(position_weights, part) for part in rel_grad)

    blocks, tokens_part, tokens_sent = project_grad(
        keep, swap(give), tokens, tokens_got, project_t, table_blocks
    )
    blocks, tokens_back, position_grads = lax.optimization_barrier(
        (blocks, swap(tokens_sent), position_grads)
    )
    position_grads, summed = lax.optimization_barrier((position_grads, summed))
    received, summed, position_grads = lax.optimization_barrier(
        (
            exchange(blocks, COLUMN + GROUP),
            y_scatter(summed.reshape(4, 64, D)),
            ring_scatter(position_grads, "yl", 2),
        )
    )
    grad_expand = summed[:32].T
    grad_reduce = summed[32:64].reshape(4, 8, D).transpose(1, 0, 2).reshape(8, FF).T
    received = jnp.sum(received.astype(f32), axis=0)
    grad_project = jnp.concatenate([received[:24], received[24:48]], axis=1).T
    grad_table = received[48:].T
    tokens_grad = grad_resid1 + (tokens_part + tokens_back)
    grad_key, grad_query = position_grads[:, :128], position_grads[:, 128:]

    return (
        output,
        tokens_grad.astype(bf16),
        grad_project,
        grad_attend,
        vectors[0],
        vectors[1],
        grad_expand,
        grad_reduce,
        vectors[2],
        vectors[3],
        grad_table,
        grad_query,
        grad_key,
    )


def solution(mesh):
    parts = Mesh(mesh.devices.reshape(2, 4, 2, 4, 2), EVERY)
    in_specs = (
        P(EVERY, None),
        P(None, EVERY),
        P(None, EVERY),
        P(EVERY),
        P(EVERY),
        P(None, EVERY),
        P(None, EVERY),
        P(EVERY),
        P(EVERY),
        P(None, EVERY),
        P(DP, GROUP),
        P(DP, GROUP),
        P(DP),
        P(EVERY, None),
    )
    out_specs = (
        P(EVERY, None),
        P(EVERY, None),
        P(None, EVERY),
        P(None, EVERY),
        P(EVERY),
        P(EVERY),
        P(None, EVERY),
        P(None, EVERY),
        P(EVERY),
        P(EVERY),
        P(None, EVERY),
        P(DP, GROUP),
        P(DP, GROUP),
    )
    return jax.shard_map(
        per_device, mesh=parts, in_specs=in_specs, out_specs=out_specs, check_vma=False
    )
```

```python
import math

import jax
import jax.numpy as jnp
import numpy as np
from jax import lax
from jax.experimental import pallas as pl
from jax.experimental.pallas import tpu as pltpu
from jax.sharding import Mesh
from jax.sharding import PartitionSpec as P

D = 1024
HEADS = 16
HEAD_DIM = 64
FF = 4096
SPAN = 256
SEQ = 512
BLOCK = 128
WINDOW = SEQ + BLOCK
STEP = 4

EPS = 1e-07
MASKED = -1e30

DP = ("yl", "x", "core")
GROUP = ("z", "yh")
COLUMN = ("yl", "x")
EVERY = DP + GROUP
CHIPS = ("z", "yh", "yl", "x")
DEVICES = ("core",) + CHIPS
bf16 = jnp.bfloat16
f32 = jnp.float32


def bucket_values(offset, span):
    middle = span // 2
    absolute = np.where((offset < middle) & (offset > -middle), middle - 1, np.abs(offset))
    log_place = (
        np.ceil(np.log(absolute / middle) / np.log((2 * span - 1) / middle) * (middle - 1)) + middle
    )
    buckets = np.where(absolute <= middle, offset, log_place * np.sign(offset)).astype(np.int64)
    return np.clip(buckets + span, 0, 2 * span - 1).astype(np.int32)


def normalize(value, gain, shift):
    center = value - jnp.mean(value, axis=-1, keepdims=True)
    inverse = lax.rsqrt(jnp.mean(center * center, axis=-1, keepdims=True) + EPS)
    scaled = center * inverse
    return (scaled * gain + shift, scaled, inverse)


def normalize_back(incoming, scaled, inverse, gain):
    grad_scaled = incoming * gain
    middle = (
        grad_scaled
        - jnp.mean(grad_scaled, axis=-1, keepdims=True)
        - scaled * jnp.mean(grad_scaled * scaled, axis=-1, keepdims=True)
    )
    return inverse * middle


def dot_nn(left, right):
    return lax.dot_general(left, right, (((1,), (0,)), ((), ())), preferred_element_type=f32)


def dot_nt(left, right):
    return lax.dot_general(left, right, (((1,), (1,)), ((), ())), preferred_element_type=f32)


def dot_tn(left, right):
    return lax.dot_general(left, right, (((0,), (0,)), ((), ())), preferred_element_type=f32)


def window(block):
    start = SEQ - BLOCK - BLOCK * block
    return slice(start, start + WINDOW)


def rows(block):
    return slice(BLOCK * block, BLOCK * (block + 1))


def skew(values):
    return pltpu.roll(values, SEQ + 1, 1, stride=1, stride_axis=0)[:, :SEQ]


def unskew(values):
    wide = jnp.concatenate([values, jnp.zeros((BLOCK, BLOCK), f32)], axis=1)
    return pltpu.roll(wide, 0, 1, stride=1, stride_axis=0)


def turn(mirror, values):
    upper = values.astype(bf16)
    return dot_nn(mirror, upper) + dot_nn(mirror, (values - upper.astype(f32)).astype(bf16))


def one_head(value, head):
    lane = lax.broadcasted_iota(jnp.int32, value.shape, 1)
    return jnp.where(lane // HEAD_DIM == head, value, jnp.zeros_like(value))


def query_bias(key, rel_queries, bias):
    for block in range(SEQ // BLOCK):
        by_offset = dot_nt(key[rows(block)], rel_queries[window(block)])
        bias[:, rows(block)] = skew(by_offset).T


def probabilities(query, key, rel_keys, bias, block, length):
    part = query[rows(block)]
    logits = dot_nt(part, key) + skew(dot_nt(part, rel_keys[window(block)])) + bias[rows(block)]
    logits = logits * (1.0 / math.sqrt(3 * HEAD_DIM))
    column = lax.broadcasted_iota(jnp.int32, logits.shape, 1)
    logits = jnp.where(column < length, logits, MASKED)
    exponent = jnp.exp(logits - jnp.max(logits, axis=1, keepdims=True))
    return exponent * (1.0 / jnp.sum(exponent, axis=1, keepdims=True))


def attend_kernel(lengths, heads_in, rel, context, bias):
    length = lengths[pl.program_id(0)]
    query, key, values = (heads_in[:, part].reshape(SEQ, 128) for part in range(3))
    rel_keys, rel_queries = rel[:, :128], rel[:, 128:]
    total = [jnp.zeros((BLOCK, 128), f32) for _ in range(SEQ // BLOCK)]
    for head in range(2):
        query_h, key_h, values_h = (one_head(part, head) for part in (query, key, values))
        query_bias(key_h, rel_queries, bias)
        for block in range(SEQ // BLOCK):
            probs = probabilities(query_h, key, rel_keys, bias, block, length)
            total[block] = total[block] + dot_nn(probs.astype(bf16), values_h)
    for block in range(SEQ // BLOCK):
        context[block] = total[block].astype(bf16)


def attend_back_kernel(
    lengths, heads_in, rel, grad_context, grads, grad_rel, bias, probs_ref, grad_ref
):
    length = lengths[pl.program_id(0)]
    query, key, values = (heads_in[:, part].reshape(SEQ, 128) for part in range(3))
    grad_ctx = grad_context[...].reshape(SEQ, 128)
    rel_keys, rel_queries = rel[:, :128], rel[:, 128:]
    blocks = SEQ // BLOCK
    first = lax.broadcasted_iota(jnp.int32, (BLOCK, BLOCK), 0)
    second = lax.broadcasted_iota(jnp.int32, (BLOCK, BLOCK), 1)
    mirror = jnp.where(first + second == BLOCK - 1, 1.0, 0.0).astype(bf16)

    @pl.when(pl.program_id(0) == 0)
    def _():
        grad_rel[...] = jnp.zeros_like(grad_rel)

    queries, keys, ctxs = (
        [one_head(part, head) for head in range(2)] for part in (query, key, grad_ctx)
    )
    rel_keys_of = [one_head(rel_keys, head) for head in range(2)]
    rel_queries_of = [one_head(rel_queries, head) for head in range(2)]
    for head in range(2):
        query_bias(keys[head], rel_queries, bias.at[head])
    for block in range(blocks):
        grad_q, turned, rel_part = 0.0, 0.0, 0.0
        for head in range(2):
            probs = probabilities(queries[head], key, rel_keys, bias.at[head], block, length)
            probs_ref[head, rows(block)] = probs.astype(bf16)
            grad_probs = dot_nt(ctxs[head][rows(block)], values)
            inner = jnp.sum(probs * grad_probs, axis=1, keepdims=True)
            grad = (probs * (grad_probs - inner) * (1.0 / math.sqrt(3 * HEAD_DIM))).astype(bf16)
            grad_ref[head, rows(block)] = grad
            by_offset = unskew(dot_nn(mirror, grad)).astype(bf16)
            grad_q = grad_q + dot_nn(grad, keys[head])
            turned = turned + dot_nn(by_offset, rel_keys_of[head][window(block)])
            mirrored = dot_nn(mirror, queries[head][rows(block)]).astype(bf16)
            rel_part = rel_part + dot_tn(by_offset, mirrored)
        grad_rel[window(block), :128] += rel_part
        grads[block, 0] = (grad_q + turn(mirror, turned)).astype(bf16)
    for block in range(blocks):
        grad_k, grad_v, turned, rel_part = 0.0, 0.0, 0.0, 0.0
        for head in range(2):
            grad = grad_ref[head, :, rows(block)]
            by_offset = unskew(dot_nt(mirror, grad)).astype(bf16)
            grad_k = grad_k + dot_tn(grad, queries[head])
            turned = turned + dot_nn(by_offset, rel_queries_of[head][window(block)])
            grad_v = grad_v + dot_tn(probs_ref[head, :, rows(block)], ctxs[head])
            mirrored = dot_nn(mirror, keys[head][rows(block)]).astype(bf16)
            rel_part = rel_part + dot_tn(by_offset, mirrored)
        grad_rel[window(block), 128:] += rel_part
        grads[block, 1] = (grad_k + turn(mirror, turned)).astype(bf16)
        grads[block, 2] = grad_v.astype(bf16)


def attend(lengths, heads_in, rel):
    return pl.pallas_call(
        attend_kernel,
        grid=(2,),
        in_specs=[
            pl.BlockSpec(memory_space=pltpu.SMEM),
            pl.BlockSpec((4, 3, 128, 128), lambda row: (row, 0, 0, 0)),
            pl.BlockSpec((2 * SEQ, 256), lambda row: (0, 0)),
        ],
        out_specs=pl.BlockSpec((4, 128, 128), lambda row: (row, 0, 0)),
        out_shape=jax.ShapeDtypeStruct((8, 128, 128), bf16),
        scratch_shapes=[pltpu.VMEM((SEQ, SEQ), f32)],
        compiler_params=pltpu.CompilerParams(vmem_limit_bytes=48 * 2**20),
        name="attend",
    )(lengths, heads_in, rel)


def attend_back(lengths, heads_in, rel, grad_context):
    return pl.pallas_call(
        attend_back_kernel,
        grid=(2,),
        in_specs=[
            pl.BlockSpec(memory_space=pltpu.SMEM),
            pl.BlockSpec((4, 3, 128, 128), lambda row: (row, 0, 0, 0)),
            pl.BlockSpec((2 * SEQ, 256), lambda row: (0, 0)),
            pl.BlockSpec((4, 128, 128), lambda row: (row, 0, 0)),
        ],
        out_specs=[
            pl.BlockSpec((4, 3, 128, 128), lambda row: (row, 0, 0, 0)),
            pl.BlockSpec((2 * SEQ, 256), lambda row: (0, 0)),
        ],
        out_shape=[
            jax.ShapeDtypeStruct((8, 3, 128, 128), bf16),
            jax.ShapeDtypeStruct((2 * SEQ, 256), f32),
        ],
        scratch_shapes=[
            pltpu.VMEM((2, SEQ, SEQ), f32),
            pltpu.VMEM((2, SEQ, SEQ), bf16),
            pltpu.VMEM((2, SEQ, SEQ), bf16),
        ],
        compiler_params=pltpu.CompilerParams(vmem_limit_bytes=48 * 2**20),
        name="attend_back",
    )(lengths, heads_in, rel, grad_context)


def owner_rows(block):
    wide = block.astype(f32).reshape(8, STEP, 2, 8, block.shape[-1])
    return wide.transpose(1, 2, 0, 3, 4).reshape(STEP * 128, block.shape[-1]).astype(bf16)


def project_back_kernel(context, tokens, weights, resid):
    rows_in = jnp.concatenate([context[group] for group in range(8)], axis=1)
    resid[...] = tokens[...].astype(f32) + dot_nt(rows_in, owner_rows(weights[...]))


def project_back(context, tokens, gathered):
    return pl.pallas_call(
        project_back_kernel,
        grid=(8 // STEP,),
        in_specs=[
            pl.BlockSpec((8, 128, 128), lambda k: (0, 0, 0)),
            pl.BlockSpec((128, STEP * 128), lambda k: (0, k)),
            pl.BlockSpec((8, STEP, 16, D), lambda k: (0, k, 4, 0)),
        ],
        out_specs=pl.BlockSpec((128, STEP * 128), lambda k: (0, k)),
        out_shape=jax.ShapeDtypeStruct((128, D), f32),
        compiler_params=pltpu.CompilerParams(vmem_limit_bytes=48 * 2**20),
        name="project_back",
    )(context, tokens, gathered)


def ffn_kernel(mine, theirs, vec, expand, reduce, act, slope, partial, sent, low):
    phase, k = pl.program_id(0), pl.program_id(1)

    @pl.when((phase == 0) & (k == 0))
    def _():
        for half, resid in enumerate((mine, theirs)):
            first_norm, scaled, inverse = normalize(resid[...], vec[0:1], vec[1:2])
            low[128 * half : 128 * (half + 1)] = first_norm.astype(bf16)

    @pl.when(phase == 0)
    def _():
        for column in range(STEP):
            inner = dot_nt(low[...], expand[:, column].reshape(256, D))
            spread_in = 0.5 + 0.5 * lax.erf(inner * math.sqrt(0.5))
            act[STEP * k + column] = (inner * spread_in).astype(bf16)
            density = jnp.exp(-0.5 * inner * inner) * (1.0 / math.sqrt(2.0 * math.pi))
            slope[column] = spread_in + inner * density

    @pl.when(phase == 1)
    def _():
        total = jnp.zeros((256, STEP * 128), f32)
        for half in range(2):
            rows_in = jnp.concatenate([act[4 * half + part] for part in range(4)], axis=1)
            weights = owner_rows(reduce[:, :, 16 * half : 16 * (half + 1)])
            total = total + dot_nt(rows_in, weights)
        partial[...] = total
        sent[...] = total.astype(bf16)


def ffn_forward(mine, theirs, vec, gathered):
    whole = lambda phase, k: (0, 0)
    return pl.pallas_call(
        ffn_kernel,
        grid=(2, 8 // STEP),
        in_specs=[
            pl.BlockSpec((128, D), whole),
            pl.BlockSpec((128, D), whole),
            pl.BlockSpec((4, D), whole),
            pl.BlockSpec((8, STEP, 32, D), lambda phase, k: (0, jnp.where(phase == 0, k, 8 // STEP - 1), 0, 0)),
            pl.BlockSpec((8, STEP, 32, D), lambda phase, k: (0, jnp.where(phase == 0, 0, k), 1, 0)),
        ],
        out_specs=[
            pl.BlockSpec((8, 256, 256), lambda phase, k: (0, 0, 0)),
            pl.BlockSpec((STEP, 256, 256), lambda phase, k: (jnp.where(phase == 0, k, 8 // STEP - 1), 0, 0)),
            pl.BlockSpec((256, STEP * 128), lambda phase, k: (0, jnp.where(phase == 0, 0, k))),
            pl.BlockSpec((256, STEP * 128), lambda phase, k: (0, jnp.where(phase == 0, 0, k))),
        ],
        out_shape=[
            jax.ShapeDtypeStruct((8, 256, 256), bf16),
            jax.ShapeDtypeStruct((8, 256, 256), f32),
            jax.ShapeDtypeStruct((256, D), f32),
            jax.ShapeDtypeStruct((256, D), bf16),
        ],
        scratch_shapes=[pltpu.VMEM((256, D), bf16)],
        compiler_params=pltpu.CompilerParams(vmem_limit_bytes=48 * 2**20),
        name="ffn_forward",
    )(mine, theirs, vec, gathered, gathered)


def own_half(core, wide):
    return jnp.where(core[0] == 0, wide[:, :64], wide[:, 64:])


def ffn_back_kernel(
    core,
    mine,
    theirs,
    vec,
    ffn_own,
    ffn_got,
    cot_own,
    cot_got,
    act_own,
    act_got,
    slope,
    expand,
    reduce,
    output,
    blocks,
    partial,
    sent,
    sums,
    low,
    grad_ffn,
    grad_act,
    act,
):
    phase, k = pl.program_id(0), pl.program_id(1)

    @pl.when((phase == 0) & (k == 0))
    def _():
        sums[...] = jnp.zeros_like(sums)
        for half, (resid, cot) in enumerate(((mine, cot_own), (theirs, cot_got))):
            span = slice(128 * half, 128 * (half + 1))
            cross = slice(128 * (1 - half), 128 * (2 - half))
            first_norm, scaled, inverse = normalize(resid[...], vec[0:1], vec[1:2])
            low[span] = first_norm.astype(bf16)
            resid2 = first_norm + (ffn_own[span] + ffn_got[cross])
            normed, scaled, inverse = normalize(resid2, vec[2:3], vec[3:4])
            grad = cot[...].astype(f32)
            if half == 0:
                output[...] = normed.astype(bf16)
            sums[2:3] += jnp.sum(grad * scaled, axis=0, keepdims=True)
            sums[3:4] += jnp.sum(grad, axis=0, keepdims=True)
            grad = normalize_back(grad, scaled, inverse, vec[2:3])
            partial[span] = 0.5 * grad
            grad = grad.astype(bf16)
            for chunk in range(8 // STEP):
                grad_ffn[chunk, span] = grad[:, STEP * 128 * chunk : STEP * 128 * (chunk + 1)]
        grad_act[...] = jnp.zeros_like(grad_act)
        for chunk in range(8):
            own, got = act_own[chunk], act_got[chunk]
            got = jnp.concatenate([got[128:], got[:128]], axis=0)
            start = 512 * (chunk % 2)
            act[chunk // 2, :, start : start + 256] = jnp.where(core[0] == 0, own, got)
            act[chunk // 2, :, start + 256 : start + 512] = jnp.where(core[0] == 0, got, own)

    @pl.when(phase == 0)
    def _():
        grad = grad_ffn[k]
        own = [own_half(core, grad[:, 128 * column : 128 * (column + 1)]) for column in range(STEP)]
        own = jnp.concatenate(own, axis=1)
        for half in range(2):
            weights = owner_rows(reduce[:, :, 16 * half : 16 * (half + 1)])
            for part in range(4):
                grad_act[4 * half + part] += dot_nn(grad, weights[:, 256 * part : 256 * (part + 1)])
            made = [dot_tn(own, act[2 * half + part]).reshape(STEP, 8, 8, D) for part in range(2)]
            made = jnp.concatenate(made, axis=2).astype(bf16).reshape(STEP, 4, 2, 16, D)
            blocks[:, :, :, 0, 16 * half : 16 * (half + 1)] = made

    @pl.when(phase == 1)
    def _():
        for column in range(STEP):
            weights = expand[:, column].reshape(256, D)
            grad = (slope[column] * grad_act[STEP * k + column]).astype(bf16)
            made = dot_tn(grad, low[...]).astype(bf16)
            blocks[column, :, :, 0] = made.reshape(4, 2, 32, D)
            partial[...] += dot_nn(grad, weights)

    @pl.when((phase == 1) & (k == 8 // STEP - 1))
    def _():
        sent[...] = partial[...].astype(bf16)


def ffn_backward(
    core, mine, theirs, vec, ffn_own, ffn_got, cot_own, cot_got, act_own, act_got, slope, gathered
):
    whole = lambda phase, k: (0, 0)
    return pl.pallas_call(
        ffn_back_kernel,
        grid=(2, 8 // STEP),
        in_specs=[
            pl.BlockSpec(memory_space=pltpu.SMEM),
            pl.BlockSpec((128, D), whole),
            pl.BlockSpec((128, D), whole),
            pl.BlockSpec((4, D), whole),
            pl.BlockSpec((256, D), whole),
            pl.BlockSpec((256, D), whole),
            pl.BlockSpec((128, D), whole),
            pl.BlockSpec((128, D), whole),
            pl.BlockSpec((8, 256, 256), lambda phase, k: (0, 0, 0)),
            pl.BlockSpec((8, 256, 256), lambda phase, k: (0, 0, 0)),
            pl.BlockSpec((STEP, 256, 256), lambda phase, k: (jnp.where(phase == 0, 0, k), 0, 0)),
            pl.BlockSpec((8, STEP, 32, D), lambda phase, k: (0, jnp.where(phase == 0, 0, k), 0, 0)),
            pl.BlockSpec((8, STEP, 32, D), lambda phase, k: (0, jnp.where(phase == 0, k, 8 // STEP - 1), 1, 0)),
        ],
        out_specs=[
            pl.BlockSpec((128, D), whole),
            pl.BlockSpec(
                (STEP, 4, 2, 1, 32, D),
                lambda phase, k: (k % (4 // STEP), 0, 0, k // (4 // STEP), 1 - phase, 0),
            ),
            pl.BlockSpec((256, D), whole),
            pl.BlockSpec((256, D), whole),
            pl.BlockSpec((8, D), whole),
        ],
        out_shape=[
            jax.ShapeDtypeStruct((128, D), bf16),
            jax.ShapeDtypeStruct((4, 4, 2, 2, 64, D), bf16),
            jax.ShapeDtypeStruct((256, D), f32),
            jax.ShapeDtypeStruct((256, D), bf16),
            jax.ShapeDtypeStruct((8, D), f32),
        ],
        scratch_shapes=[
            pltpu.VMEM((256, D), bf16),
            pltpu.VMEM((8 // STEP, 256, STEP * 128), bf16),
            pltpu.VMEM((8, 256, 256), f32),
            pltpu.VMEM((4, 256, D), bf16),
        ],
        compiler_params=pltpu.CompilerParams(vmem_limit_bytes=56 * 2**20),
        name="ffn_backward",
    )(
        core,
        mine,
        theirs,
        vec,
        ffn_own,
        ffn_got,
        cot_own,
        cot_got,
        act_own,
        act_got,
        slope,
        gathered,
        gathered,
    )


def first_back_kernel(
    core,
    mine,
    theirs,
    vec,
    grad_own,
    grad_got,
    ctx_own,
    ctx_got,
    sums,
    weights,
    grad_resid,
    grad_context,
    blocks,
    grad_low,
    total,
    vec_sums,
):
    k = pl.program_id(0)

    @pl.when(k == 0)
    def _():
        found = sums[...]
        place = lax.broadcasted_iota(jnp.int32, (8, D), 0)
        for half, resid in enumerate((mine, theirs)):
            span = slice(128 * half, 128 * (half + 1))
            cross = slice(128 * (1 - half), 128 * (2 - half))
            normed, scaled, inverse = normalize(resid[...], vec[0:1], vec[1:2])
            grad = grad_own[span] + grad_got[cross]
            found += jnp.where(place == 0, jnp.sum(grad * scaled, axis=0, keepdims=True), 0.0)
            found += jnp.where(place == 1, jnp.sum(grad, axis=0, keepdims=True), 0.0)
            grad = normalize_back(grad, scaled, inverse, vec[0:1])
            if half == 0:
                grad_resid[...] = grad
            grad = grad.astype(bf16)
            for chunk in range(8 // STEP):
                grad_low[chunk, span] = grad[:, STEP * 128 * chunk : STEP * 128 * (chunk + 1)]
        for chunk in range(8):
            vec_sums[chunk] = found[:, 128 * chunk : 128 * (chunk + 1)]
        total[...] = jnp.zeros_like(total)

    grad = grad_low[k]
    total[...] += dot_nn(grad[:128], owner_rows(weights[...]))
    ctx = [jnp.concatenate([part[group] for group in range(8)], axis=1) for part in (ctx_own, ctx_got)]
    own = [own_half(core, grad[:, 128 * column : 128 * (column + 1)]) for column in range(STEP)]
    made = dot_tn(jnp.concatenate(own, axis=1), jnp.concatenate(ctx, axis=0)).reshape(STEP, 8, 8, D)
    for column in range(STEP):
        row = jnp.broadcast_to(vec_sums[STEP * k + column][None], (8, 8, 128))
        blocks[column] = jnp.concatenate([made[column], row], axis=-1).astype(bf16)

    @pl.when(k == 8 // STEP - 1)
    def _():
        for group in range(8):
            grad_context[group] = total[:, 128 * group : 128 * (group + 1)].astype(bf16)


def first_backward(
    core, mine, theirs, vec, grad_own, grad_got, ctx_own, ctx_got, sums, gathered
):
    whole = lambda k: (0, 0)
    return pl.pallas_call(
        first_back_kernel,
        grid=(8 // STEP,),
        in_specs=[
            pl.BlockSpec(memory_space=pltpu.SMEM),
            pl.BlockSpec((128, D), whole),
            pl.BlockSpec((128, D), whole),
            pl.BlockSpec((4, D), whole),
            pl.BlockSpec((256, D), whole),
            pl.BlockSpec((256, D), whole),
            pl.BlockSpec((8, 128, 128), lambda k: (0, 0, 0)),
            pl.BlockSpec((8, 128, 128), lambda k: (0, 0, 0)),
            pl.BlockSpec((8, D), whole),
            pl.BlockSpec((8, STEP, 16, D), lambda k: (0, k, 4, 0)),
        ],
        out_specs=[
            pl.BlockSpec((128, D), whole),
            pl.BlockSpec((8, 128, 128), lambda k: (0, 0, 0)),
            pl.BlockSpec((STEP, 8, 8, D + 128), lambda k: (k, 0, 0, 0)),
        ],
        out_shape=[
            jax.ShapeDtypeStruct((128, D), f32),
            jax.ShapeDtypeStruct((8, 128, 128), bf16),
            jax.ShapeDtypeStruct((8, 8, 8, D + 128), bf16),
        ],
        scratch_shapes=[
            pltpu.VMEM((8 // STEP, 256, STEP * 128), bf16),
            pltpu.VMEM((128, D), f32),
            pltpu.VMEM((8, 8, 128), f32),
        ],
        compiler_params=pltpu.CompilerParams(vmem_limit_bytes=56 * 2**20),
        name="first_backward",
    )(core, mine, theirs, vec, grad_own, grad_got, ctx_own, ctx_got, sums, gathered)


def two_parts(value):
    upper = value.astype(bf16)
    return upper, (value - upper.astype(f32)).astype(bf16)


def swap(value):
    return lax.ppermute(value, "core", [(0, 1), (1, 0)])


def exchange(value, axes):
    return lax.all_to_all(value, axes, 0, 0, tiled=True)


def shifted(value, axis, size, step):
    return lax.ppermute(value, axis, [(i, (i + step) % size) for i in range(size)])


def stacked(value, axis):
    size = lax.axis_size(axis)
    return jnp.stack([value] + [shifted(value, axis, size, step) for step in range(1, size)])


def places_back(axis):
    size = lax.axis_size(axis)
    return (lax.axis_index(axis) - jnp.arange(size)) % size


def pick(blocks, index):
    return blocks.at[index.reshape(-1)].get(mode="promise_in_bounds")


def spread(value, axes):
    return exchange(jnp.broadcast_to(value[None], (8,) + value.shape), axes)


def gather_projection(rows_t, table_rows, position_rows):
    first = spread(jnp.concatenate([rows_t[:, :512], table_rows], axis=0), GROUP)
    first, second = lax.optimization_barrier((first, rows_t[:, 512:]))
    second = stacked(stacked(second, "x"), "yl").reshape(8 * 24, 512)
    first = jnp.concatenate([first.reshape(256, 512), position_rows], axis=0)
    first, second = lax.optimization_barrier((stacked(first, "yl"), second))
    first = first.reshape(2, 9, 32, 512)
    table = jnp.concatenate([first[:, :8, 24:].reshape(2, 64, 512), first[:, 8]], axis=1)
    first = stacked(first[:, :8, :24], "x").reshape(8, 8, 24, 512)
    second = spread(second, GROUP).reshape(8, 8, 24, 512)
    table = stacked(table, "x").reshape(8, 96, 512)
    x, yl = places_back("x")[None], places_back("yl")[:, None]
    order = jnp.stack([(yl + 2 * x).reshape(-1), (x + 4 * yl).reshape(-1)])
    table = table.at[order[0]].get(mode="promise_in_bounds")
    return first, second, order, table[:, :64].reshape(512, 512), table[:, 64:]


def pack_kernel(core, expand, reduce, attend, vectors, got, packet):
    first = core[0] == 0
    packet[:32] = expand[...]
    inner = []
    for source in (reduce, got):
        spans = [source[:, 512 * k : 512 * (k + 1)].astype(f32) for k in range(8)]
        inner.append([jnp.where(first, span[:, :256], span[:, 256:]) for span in spans])
    for half in range(2):
        parts = [jnp.concatenate(rows_in[4 * half : 4 * half + 4], axis=1) for rows_in in inner]
        low, high = jnp.where(first, *parts), jnp.where(first, *reversed(parts))
        joined = jnp.concatenate([low, high], axis=0).astype(bf16)
        packet[32 + 16 * half : 48 + 16 * half] = joined
    own, other = attend[...].astype(f32), got[:, FF : FF + D].astype(f32)
    joined = jnp.concatenate([jnp.where(first, own, other), jnp.where(first, other, own)], axis=0)
    packet[64:80] = joined.astype(bf16)
    own, other = vectors[:4].astype(f32), got[:4, FF + D :].astype(f32)
    joined = jnp.concatenate([jnp.where(first, own, other), jnp.where(first, other, own)], axis=0)
    packet[80:] = jnp.concatenate([joined, jnp.zeros((8, D - 128), f32)], axis=1).astype(bf16)


def pack(core, expand, reduce, attend, vectors, got):
    return pl.pallas_call(
        pack_kernel,
        in_specs=[pl.BlockSpec(memory_space=pltpu.SMEM)]
        + [pl.BlockSpec(memory_space=pltpu.VMEM)] * 5,
        out_specs=pl.BlockSpec(memory_space=pltpu.VMEM),
        out_shape=jax.ShapeDtypeStruct((88, D), bf16),
        compiler_params=pltpu.CompilerParams(vmem_limit_bytes=32 * 2**20),
        name="pack",
    )(core, expand, reduce, attend, vectors, got)


def project_kernel(order, mine, theirs, first, second, packed, rows_out):
    tokens = jnp.concatenate([mine[...], theirs[...]], axis=0)
    low = first[0].astype(f32).reshape(192, 512).astype(bf16)
    high = second[:, 0].astype(f32).reshape(192, 512).astype(bf16)
    made = dot_nt(tokens[:, :512], low) + dot_nt(tokens[:, 512:], high)
    packed[0] = made.astype(bf16)
    rows_out[:, :512] = low
    rows_out[:, 512:] = high


def project(order, mine, theirs, first, second):
    return pl.pallas_call(
        project_kernel,
        grid_spec=pltpu.PrefetchScalarGridSpec(
            num_scalar_prefetch=1,
            grid=(8,),
            in_specs=[
                pl.BlockSpec((128, D), lambda k, order: (0, 0)),
                pl.BlockSpec((128, D), lambda k, order: (0, 0)),
                pl.BlockSpec((1, 8, 24, 512), lambda k, order: (order[0, k], 0, 0, 0)),
                pl.BlockSpec((8, 1, 24, 512), lambda k, order: (0, order[1, k], 0, 0)),
            ],
            out_specs=[
                pl.BlockSpec((1, 256, 192), lambda k, order: (k, 0, 0)),
                pl.BlockSpec((192, D), lambda k, order: (k, 0)),
            ],
        ),
        out_shape=[
            jax.ShapeDtypeStruct((8, 256, 192), bf16),
            jax.ShapeDtypeStruct((1536, D), bf16),
        ],
        compiler_params=pltpu.CompilerParams(vmem_limit_bytes=32 * 2**20),
        name="project",
    )(order, mine, theirs, first, second)


def arrange_kernel(core, mine, theirs, heads):
    for column in range(8):
        own, other = mine[column].astype(f32), theirs[column].astype(f32)
        first = core[0] == 0
        joined = jnp.concatenate(
            [jnp.where(first, own, other), jnp.where(first, other, own)], axis=1
        )
        for place in range(3):
            chunk = 3 * column + place
            heads[chunk % 8, chunk // 8] = joined[:, 128 * place : 128 * (place + 1)].astype(bf16)


def arrange(core, mine, theirs):
    return pl.pallas_call(
        arrange_kernel,
        in_specs=[
            pl.BlockSpec(memory_space=pltpu.SMEM),
            pl.BlockSpec(memory_space=pltpu.VMEM),
            pl.BlockSpec(memory_space=pltpu.VMEM),
        ],
        out_specs=pl.BlockSpec(memory_space=pltpu.VMEM),
        out_shape=jax.ShapeDtypeStruct((8, 3, 128, 128), bf16),
        compiler_params=pltpu.CompilerParams(vmem_limit_bytes=32 * 2**20),
        name="arrange",
    )(core, mine, theirs)


def project_grad_kernel(
    keep, got, tokens_own, tokens_got, weights, table, blocks, part_own, part_theirs
):
    tokens = jnp.concatenate([tokens_own[...], tokens_got[...]], axis=0)
    part_own[...] = dot_nn(keep[...], weights[...])
    part_theirs[...] = dot_nn(got[...], weights[...]).astype(bf16)
    for step in range(4):
        span = slice(384 * step, 384 * (step + 1))
        grads = jnp.concatenate([keep[:, span], got[:, span]], axis=0)
        made = dot_tn(grads, tokens).reshape(16, 24, D)
        rest = table[128 * step : 128 * (step + 1)].reshape(16, 8, 512)
        made = jnp.concatenate([made[..., :512], made[..., 512:], rest], axis=1)
        blocks[16 * step : 16 * (step + 1)] = made.astype(bf16)


def project_grad(keep, got, tokens_own, tokens_got, weights, table):
    return pl.pallas_call(
        project_grad_kernel,
        in_specs=[pl.BlockSpec(memory_space=pltpu.VMEM)] * 6,
        out_specs=[pl.BlockSpec(memory_space=pltpu.VMEM)] * 3,
        out_shape=[
            jax.ShapeDtypeStruct((64, 56, 512), bf16),
            jax.ShapeDtypeStruct((128, D), f32),
            jax.ShapeDtypeStruct((128, D), bf16),
        ],
        compiler_params=pltpu.CompilerParams(vmem_limit_bytes=48 * 2**20),
        name="project_grad",
    )(keep, got, tokens_own, tokens_got, weights, table)


def ring_scatter(blocks, axis, size, dtype=f32):
    place = lax.axis_index(axis)
    total = lax.dynamic_index_in_dim(blocks, place, 0, keepdims=False).astype(f32)
    for step in range(1, size):
        sent = lax.dynamic_index_in_dim(blocks, (place + step) % size, 0, keepdims=False)
        total = total + shifted(sent, axis, size, step).astype(f32)
    return total.astype(dtype)


def y_scatter(blocks):
    place = 2 * lax.axis_index("yh") + lax.axis_index("yl")
    total = lax.dynamic_index_in_dim(blocks, place, 0, keepdims=False).astype(f32)

    def on_mesh(y):
        return 2 * (y % 2) + y // 2

    for step in range(1, 4):
        sent = lax.dynamic_index_in_dim(blocks, (place + step) % 4, 0, keepdims=False)
        ring = [(on_mesh(y), on_mesh((y + step) % 4)) for y in range(4)]
        total = total + lax.ppermute(sent, ("yl", "yh"), ring).astype(f32)
    return total


def split_kernel(core, heads, keep, give):
    for column in range(8):
        chunks = [3 * column + place for place in range(3)]
        joined = jnp.concatenate(
            [heads[chunk % 8, chunk // 8].astype(f32) for chunk in chunks], axis=1
        )
        first = core[0] == 0
        zero, one = joined[:, :192], joined[:, 192:]
        span = slice(192 * column, 192 * (column + 1))
        keep[:, span] = jnp.where(first, zero, one).astype(bf16)
        give[:, span] = jnp.where(first, one, zero).astype(bf16)


def split(core, heads):
    return pl.pallas_call(
        split_kernel,
        in_specs=[
            pl.BlockSpec(memory_space=pltpu.SMEM),
            pl.BlockSpec(memory_space=pltpu.VMEM),
        ],
        out_specs=[pl.BlockSpec(memory_space=pltpu.VMEM)] * 2,
        out_shape=[jax.ShapeDtypeStruct((128, 1536), bf16)] * 2,
        compiler_params=pltpu.CompilerParams(vmem_limit_bytes=32 * 2**20),
        name="split",
    )(core, heads)


def per_device(
    tokens,
    w_project,
    w_attend,
    first_gain,
    first_shift,
    w_expand,
    w_reduce,
    second_gain,
    second_shift,
    position_table,
    w_query,
    w_key,
    lengths,
    cotangent,
):
    core = lax.axis_index("core")
    group = lax.axis_index(GROUP)
    local = tokens.shape[0]
    core_id = core.reshape(1)
    pair = 2 * local
    column_bucket = bucket_values(SEQ - 1 - np.arange(2 * SEQ - 1), SPAN)
    fold = np.append(column_bucket, -1)[None, :] == np.arange(2 * SPAN)[:, None]
    fold = jnp.asarray(fold.astype(np.float32)).astype(bf16)

    def by_core(zero, one):
        return jnp.where(core == 0, zero, one)

    def in_order(mine, theirs):
        return by_core(mine, theirs), by_core(theirs, mine)

    cotangent_got = swap(cotangent)
    tokens_got = swap(tokens)
    weights_own = jnp.concatenate([w_key, w_query], axis=1)
    first, second, order, table_t, position_rows = gather_projection(
        w_project.T,
        position_table.T,
        jnp.concatenate([weights_own[:32], weights_own[32:]], axis=1),
    )
    position_weights = jnp.stack([position_rows[..., :256], position_rows[..., 256:]], axis=1)
    position_weights = position_weights.reshape(512, 256)

    vectors = jnp.stack([first_gain, first_shift, second_gain, second_shift])
    vectors = jnp.pad(vectors, ((0, 4), (0, 128 - 8)))
    reduce_rows = w_reduce.T
    got = swap(jnp.concatenate([reduce_rows, w_attend.T, vectors], axis=1))
    packet = pack(core_id, w_expand.T, reduce_rows, w_attend.T, vectors, got)
    gathered = lax.all_gather(packet, CHIPS, axis=0, tiled=False).reshape(8, 8, 88, D)
    vec = gathered[..., 80:, :8].reshape(8, 8, 2, 4, 8).transpose(3, 1, 2, 0, 4)
    vec = vec.reshape(4, D).astype(f32)
    gain_one, shift_one, gain_two, shift_two = vec[0], vec[1], vec[2], vec[3]

    packed, project_t = project(order, tokens, tokens_got, first, second)
    heads_in = exchange(arrange(core_id, packed[:, :local], swap(packed[:, local:])), GROUP)
    rel = dot_tn(table_t, position_weights)
    rel = dot_tn(fold, (rel + swap(rel)).astype(bf16)).astype(bf16)
    context = exchange(attend(lengths, heads_in, rel), GROUP)
    context_got = swap(context)

    resid_own = project_back(context, tokens, gathered)
    resid_got = swap(resid_own)
    activ, slope, ffn_own, ffn_sent = ffn_forward(resid_own, resid_got, vec, gathered)
    output, blocks, grad_own, grad_sent, sums = ffn_backward(
        core_id,
        resid_own,
        resid_got,
        vec,
        ffn_own,
        swap(ffn_sent),
        cotangent,
        cotangent_got,
        activ,
        swap(activ),
        slope,
        gathered,
    )
    grad_resid1, grad_context, attend_blocks = first_backward(
        core_id,
        resid_own,
        resid_got,
        vec,
        grad_own,
        swap(grad_sent),
        context,
        context_got,
        sums,
        gathered,
    )

    summed = lax.psum_scatter(
        blocks.reshape(16, 4 * 64, D), ("x", "z"), scatter_dimension=0, tiled=True
    )
    attend_blocks, grad_ctx = lax.optimization_barrier(
        (attend_blocks, exchange(grad_context, GROUP))
    )
    attend_sum = exchange(attend_blocks.reshape(64, 8, D + 128), COLUMN + GROUP)

    grads, rel_grad = attend_back(lengths, heads_in, rel, grad_ctx)
    grads, attend_sum = lax.optimization_barrier((grads, attend_sum))
    attend_sum = jnp.sum(attend_sum.astype(f32), axis=0)
    grad_attend = attend_sum[:, :D].T
    vectors = attend_sum[:4, D:].reshape(4, 16, 8)
    vectors = lax.dynamic_index_in_dim(vectors, 8 * core + group, axis=1, keepdims=False)
    grads = exchange(grads, GROUP)
    rel_grad = sum(dot_nn(fold, part) for part in two_parts(rel_grad))
    rel_grad = two_parts(rel_grad + swap(rel_grad))
    position_grads = sum(dot_nn(table_t, part) for part in rel_grad)
    position_grads = position_grads.reshape(2, 4, 64, 256).transpose(1, 0, 2, 3)
    position_grads = ring_scatter(position_grads, "x", 4)
    table_blocks = sum(dot_nt(position_weights, part) for part in rel_grad)

    grads, position_grads = lax.optimization_barrier((grads, position_grads))
    keep, give = split(core_id, grads)
    blocks, tokens_part, tokens_sent = project_grad(
        keep, swap(give), tokens, tokens_got, project_t, table_blocks
    )
    position_grads, tokens_sent, summed = lax.optimization_barrier(
        (position_grads, tokens_sent, summed)
    )
    received, summed, position_grads, tokens_back = lax.optimization_barrier(
        (
            exchange(blocks, COLUMN + GROUP),
            y_scatter(summed.reshape(4, 64, D)),
            ring_scatter(position_grads, "yl", 2),
            swap(tokens_sent),
        )
    )
    grad_expand = summed[:32].T
    grad_reduce = summed[32:64].reshape(4, 8, D).transpose(1, 0, 2).reshape(8, FF).T
    received = jnp.sum(received.astype(f32), axis=0)
    grad_project = jnp.concatenate([received[:24], received[24:48]], axis=1).T
    grad_table = received[48:].T
    tokens_grad = grad_resid1 + (tokens_part + tokens_back)
    grad_key, grad_query = position_grads[:, :128], position_grads[:, 128:]

    return (
        output,
        tokens_grad.astype(bf16),
        grad_project,
        grad_attend,
        vectors[0],
        vectors[1],
        grad_expand,
        grad_reduce,
        vectors[2],
        vectors[3],
        grad_table,
        grad_query,
        grad_key,
    )


def solution(mesh):
    parts = Mesh(mesh.devices.reshape(2, 4, 2, 4, 2), EVERY)
    in_specs = (
        P(EVERY, None),
        P(None, EVERY),
        P(None, EVERY),
        P(EVERY),
        P(EVERY),
        P(None, EVERY),
        P(None, EVERY),
        P(EVERY),
        P(EVERY),
        P(None, EVERY),
        P(DP, GROUP),
        P(DP, GROUP),
        P(DP),
        P(EVERY, None),
    )
    out_specs = (
        P(EVERY, None),
        P(EVERY, None),
        P(None, EVERY),
        P(None, EVERY),
        P(EVERY),
        P(EVERY),
        P(None, EVERY),
        P(None, EVERY),
        P(EVERY),
        P(EVERY),
        P(None, EVERY),
        P(DP, GROUP),
        P(DP, GROUP),
    )
    return jax.shard_map(
        per_device, mesh=parts, in_specs=in_specs, out_specs=out_specs, check_vma=False
    )
```

```python
import math

import jax
import jax.numpy as jnp
import numpy as np
from jax import lax
from jax.experimental import pallas as pl
from jax.experimental.pallas import tpu as pltpu
from jax.sharding import Mesh
from jax.sharding import PartitionSpec as P

D = 1024
HEADS = 16
HEAD_DIM = 64
FF = 4096
SPAN = 256
SEQ = 512
BLOCK = 128
WINDOW = SEQ + BLOCK
STEP = 4

EPS = 1e-07
MASKED = -1e30

DP = ("yl", "x", "core")
GROUP = ("z", "yh")
COLUMN = ("yl", "x")
EVERY = DP + GROUP
CHIPS = ("z", "yh", "yl", "x")
DEVICES = ("core",) + CHIPS
bf16 = jnp.bfloat16
f32 = jnp.float32


def bucket_values(offset, span):
    middle = span // 2
    absolute = np.where((offset < middle) & (offset > -middle), middle - 1, np.abs(offset))
    log_place = (
        np.ceil(np.log(absolute / middle) / np.log((2 * span - 1) / middle) * (middle - 1)) + middle
    )
    buckets = np.where(absolute <= middle, offset, log_place * np.sign(offset)).astype(np.int64)
    return np.clip(buckets + span, 0, 2 * span - 1).astype(np.int32)


def normalize(value, gain, shift):
    center = value - jnp.mean(value, axis=-1, keepdims=True)
    inverse = lax.rsqrt(jnp.mean(center * center, axis=-1, keepdims=True) + EPS)
    scaled = center * inverse
    return (scaled * gain + shift, scaled, inverse)


def normalize_back(incoming, scaled, inverse, gain):
    grad_scaled = incoming * gain
    middle = (
        grad_scaled
        - jnp.mean(grad_scaled, axis=-1, keepdims=True)
        - scaled * jnp.mean(grad_scaled * scaled, axis=-1, keepdims=True)
    )
    return inverse * middle


def dot_nn(left, right):
    return lax.dot_general(left, right, (((1,), (0,)), ((), ())), preferred_element_type=f32)


def dot_nt(left, right):
    return lax.dot_general(left, right, (((1,), (1,)), ((), ())), preferred_element_type=f32)


def dot_tn(left, right):
    return lax.dot_general(left, right, (((0,), (0,)), ((), ())), preferred_element_type=f32)


def window(block):
    start = SEQ - BLOCK - BLOCK * block
    return slice(start, start + WINDOW)


def rows(block):
    return slice(BLOCK * block, BLOCK * (block + 1))


def skew(values):
    return pltpu.roll(values, SEQ + 1, 1, stride=1, stride_axis=0)[:, :SEQ]


def unskew(values):
    wide = jnp.concatenate([values, jnp.zeros((BLOCK, BLOCK), f32)], axis=1)
    return pltpu.roll(wide, 0, 1, stride=1, stride_axis=0)


def turn(mirror, values):
    upper = values.astype(bf16)
    return dot_nn(mirror, upper) + dot_nn(mirror, (values - upper.astype(f32)).astype(bf16))


def one_head(value, head):
    lane = lax.broadcasted_iota(jnp.int32, value.shape, 1)
    return jnp.where(lane // HEAD_DIM == head, value, jnp.zeros_like(value))


def query_bias(key, rel_queries, bias):
    for block in range(SEQ // BLOCK):
        by_offset = dot_nt(key[rows(block)], rel_queries[window(block)])
        bias[:, rows(block)] = skew(by_offset).T


def probabilities(query, key, rel_keys, bias, block, length):
    part = query[rows(block)]
    logits = dot_nt(part, key) + skew(dot_nt(part, rel_keys[window(block)])) + bias[rows(block)]
    logits = logits * (1.0 / math.sqrt(3 * HEAD_DIM))
    column = lax.broadcasted_iota(jnp.int32, logits.shape, 1)
    logits = jnp.where(column < length, logits, MASKED)
    exponent = jnp.exp(logits - jnp.max(logits, axis=1, keepdims=True))
    return exponent * (1.0 / jnp.sum(exponent, axis=1, keepdims=True))


def attend_kernel(lengths, heads_in, rel, context, bias):
    length = lengths[pl.program_id(0)]
    query, key, values = (heads_in[:, part].reshape(SEQ, 128) for part in range(3))
    rel_keys, rel_queries = rel[:, :128], rel[:, 128:]
    total = [jnp.zeros((BLOCK, 128), f32) for _ in range(SEQ // BLOCK)]
    for head in range(2):
        query_h, key_h, values_h = (one_head(part, head) for part in (query, key, values))
        query_bias(key_h, rel_queries, bias)
        for block in range(SEQ // BLOCK):
            probs = probabilities(query_h, key, rel_keys, bias, block, length)
            total[block] = total[block] + dot_nn(probs.astype(bf16), values_h)
    for block in range(SEQ // BLOCK):
        context[block] = total[block].astype(bf16)


def attend_back_kernel(
    lengths, heads_in, rel, grad_context, grads, grad_rel, bias, probs_ref, grad_ref
):
    length = lengths[pl.program_id(0)]
    query, key, values = (heads_in[:, part].reshape(SEQ, 128) for part in range(3))
    grad_ctx = grad_context[...].reshape(SEQ, 128)
    rel_keys, rel_queries = rel[:, :128], rel[:, 128:]
    blocks = SEQ // BLOCK
    first = lax.broadcasted_iota(jnp.int32, (BLOCK, BLOCK), 0)
    second = lax.broadcasted_iota(jnp.int32, (BLOCK, BLOCK), 1)
    mirror = jnp.where(first + second == BLOCK - 1, 1.0, 0.0).astype(bf16)

    @pl.when(pl.program_id(0) == 0)
    def _():
        grad_rel[...] = jnp.zeros_like(grad_rel)

    queries, keys, ctxs = (
        [one_head(part, head) for head in range(2)] for part in (query, key, grad_ctx)
    )
    rel_keys_of = [one_head(rel_keys, head) for head in range(2)]
    rel_queries_of = [one_head(rel_queries, head) for head in range(2)]
    for head in range(2):
        query_bias(keys[head], rel_queries, bias.at[head])
    for block in range(blocks):
        grad_q, turned, rel_part = 0.0, 0.0, 0.0
        for head in range(2):
            probs = probabilities(queries[head], key, rel_keys, bias.at[head], block, length)
            probs_ref[head, rows(block)] = probs.astype(bf16)
            grad_probs = dot_nt(ctxs[head][rows(block)], values)
            inner = jnp.sum(probs * grad_probs, axis=1, keepdims=True)
            grad = (probs * (grad_probs - inner) * (1.0 / math.sqrt(3 * HEAD_DIM))).astype(bf16)
            grad_ref[head, rows(block)] = grad
            by_offset = unskew(dot_nn(mirror, grad)).astype(bf16)
            grad_q = grad_q + dot_nn(grad, keys[head])
            turned = turned + dot_nn(by_offset, rel_keys_of[head][window(block)])
            mirrored = dot_nn(mirror, queries[head][rows(block)]).astype(bf16)
            rel_part = rel_part + dot_tn(by_offset, mirrored)
        grad_rel[window(block), :128] += rel_part
        grads[block, 0] = (grad_q + turn(mirror, turned)).astype(bf16)
    for block in range(blocks):
        grad_k, grad_v, turned, rel_part = 0.0, 0.0, 0.0, 0.0
        for head in range(2):
            grad = grad_ref[head, :, rows(block)]
            by_offset = unskew(dot_nt(mirror, grad)).astype(bf16)
            grad_k = grad_k + dot_tn(grad, queries[head])
            turned = turned + dot_nn(by_offset, rel_queries_of[head][window(block)])
            grad_v = grad_v + dot_tn(probs_ref[head, :, rows(block)], ctxs[head])
            mirrored = dot_nn(mirror, keys[head][rows(block)]).astype(bf16)
            rel_part = rel_part + dot_tn(by_offset, mirrored)
        grad_rel[window(block), 128:] += rel_part
        grads[block, 1] = (grad_k + turn(mirror, turned)).astype(bf16)
        grads[block, 2] = grad_v.astype(bf16)


def attend(lengths, heads_in, rel):
    return pl.pallas_call(
        attend_kernel,
        grid=(2,),
        in_specs=[
            pl.BlockSpec(memory_space=pltpu.SMEM),
            pl.BlockSpec((4, 3, 128, 128), lambda row: (row, 0, 0, 0)),
            pl.BlockSpec((2 * SEQ, 256), lambda row: (0, 0)),
        ],
        out_specs=pl.BlockSpec((4, 128, 128), lambda row: (row, 0, 0)),
        out_shape=jax.ShapeDtypeStruct((8, 128, 128), bf16),
        scratch_shapes=[pltpu.VMEM((SEQ, SEQ), f32)],
        compiler_params=pltpu.CompilerParams(vmem_limit_bytes=48 * 2**20),
        name="attend",
    )(lengths, heads_in, rel)


def attend_back(lengths, heads_in, rel, grad_context):
    return pl.pallas_call(
        attend_back_kernel,
        grid=(2,),
        in_specs=[
            pl.BlockSpec(memory_space=pltpu.SMEM),
            pl.BlockSpec((4, 3, 128, 128), lambda row: (row, 0, 0, 0)),
            pl.BlockSpec((2 * SEQ, 256), lambda row: (0, 0)),
            pl.BlockSpec((4, 128, 128), lambda row: (row, 0, 0)),
        ],
        out_specs=[
            pl.BlockSpec((4, 3, 128, 128), lambda row: (row, 0, 0, 0)),
            pl.BlockSpec((2 * SEQ, 256), lambda row: (0, 0)),
        ],
        out_shape=[
            jax.ShapeDtypeStruct((8, 3, 128, 128), bf16),
            jax.ShapeDtypeStruct((2 * SEQ, 256), f32),
        ],
        scratch_shapes=[
            pltpu.VMEM((2, SEQ, SEQ), f32),
            pltpu.VMEM((2, SEQ, SEQ), bf16),
            pltpu.VMEM((2, SEQ, SEQ), bf16),
        ],
        compiler_params=pltpu.CompilerParams(vmem_limit_bytes=48 * 2**20),
        cost_estimate=pl.CostEstimate(
            flops=25 * 10**9, bytes_accessed=8 * 2**20, transcendentals=2**20
        ),
        name="attend_back",
    )(lengths, heads_in, rel, grad_context)


def owner_rows(block):
    wide = block.astype(f32).reshape(8, STEP, 2, 8, block.shape[-1])
    return wide.transpose(1, 2, 0, 3, 4).reshape(STEP * 128, block.shape[-1]).astype(bf16)


def project_back_kernel(context, tokens, weights, resid):
    rows_in = jnp.concatenate([context[group] for group in range(8)], axis=1)
    resid[...] = tokens[...].astype(f32) + dot_nt(rows_in, owner_rows(weights[...]))


def project_back(context, tokens, gathered):
    return pl.pallas_call(
        project_back_kernel,
        grid=(8 // STEP,),
        in_specs=[
            pl.BlockSpec((8, 128, 128), lambda k: (0, 0, 0)),
            pl.BlockSpec((128, STEP * 128), lambda k: (0, k)),
            pl.BlockSpec((8, STEP, 16, D), lambda k: (0, k, 4, 0)),
        ],
        out_specs=pl.BlockSpec((128, STEP * 128), lambda k: (0, k)),
        out_shape=jax.ShapeDtypeStruct((128, D), f32),
        compiler_params=pltpu.CompilerParams(vmem_limit_bytes=48 * 2**20),
        name="project_back",
    )(context, tokens, gathered)


def ffn_kernel(mine, theirs, vec, expand, reduce, act, slope, partial, sent, low):
    phase, k = pl.program_id(0), pl.program_id(1)

    @pl.when((phase == 0) & (k == 0))
    def _():
        for half, resid in enumerate((mine, theirs)):
            first_norm, scaled, inverse = normalize(resid[...], vec[0:1], vec[1:2])
            low[128 * half : 128 * (half + 1)] = first_norm.astype(bf16)

    @pl.when(phase == 0)
    def _():
        for column in range(STEP):
            inner = dot_nt(low[...], expand[:, column].reshape(256, D))
            spread_in = 0.5 + 0.5 * lax.erf(inner * math.sqrt(0.5))
            act[STEP * k + column] = (inner * spread_in).astype(bf16)
            density = jnp.exp(-0.5 * inner * inner) * (1.0 / math.sqrt(2.0 * math.pi))
            slope[column] = spread_in + inner * density

    @pl.when(phase == 1)
    def _():
        total = jnp.zeros((256, STEP * 128), f32)
        for half in range(2):
            rows_in = jnp.concatenate([act[4 * half + part] for part in range(4)], axis=1)
            weights = owner_rows(reduce[:, :, 16 * half : 16 * (half + 1)])
            total = total + dot_nt(rows_in, weights)
        partial[...] = total
        sent[...] = total.astype(bf16)


def ffn_forward(mine, theirs, vec, gathered):
    whole = lambda phase, k: (0, 0)
    return pl.pallas_call(
        ffn_kernel,
        grid=(2, 8 // STEP),
        in_specs=[
            pl.BlockSpec((128, D), whole),
            pl.BlockSpec((128, D), whole),
            pl.BlockSpec((4, D), whole),
            pl.BlockSpec((8, STEP, 32, D), lambda phase, k: (0, jnp.where(phase == 0, k, 8 // STEP - 1), 0, 0)),
            pl.BlockSpec((8, STEP, 32, D), lambda phase, k: (0, jnp.where(phase == 0, 0, k), 1, 0)),
        ],
        out_specs=[
            pl.BlockSpec((8, 256, 256), lambda phase, k: (0, 0, 0)),
            pl.BlockSpec((STEP, 256, 256), lambda phase, k: (jnp.where(phase == 0, k, 8 // STEP - 1), 0, 0)),
            pl.BlockSpec((256, STEP * 128), lambda phase, k: (0, jnp.where(phase == 0, 0, k))),
            pl.BlockSpec((256, STEP * 128), lambda phase, k: (0, jnp.where(phase == 0, 0, k))),
        ],
        out_shape=[
            jax.ShapeDtypeStruct((8, 256, 256), bf16),
            jax.ShapeDtypeStruct((8, 256, 256), f32),
            jax.ShapeDtypeStruct((256, D), f32),
            jax.ShapeDtypeStruct((256, D), bf16),
        ],
        scratch_shapes=[pltpu.VMEM((256, D), bf16)],
        compiler_params=pltpu.CompilerParams(vmem_limit_bytes=48 * 2**20),
        name="ffn_forward",
    )(mine, theirs, vec, gathered, gathered)


def own_half(core, wide):
    return jnp.where(core[0] == 0, wide[:, :64], wide[:, 64:])


def ffn_back_kernel(
    core,
    mine,
    theirs,
    vec,
    ffn_own,
    ffn_got,
    cot_own,
    cot_got,
    act_own,
    act_got,
    slope,
    expand,
    reduce,
    output,
    blocks,
    partial,
    sent,
    sums,
    low,
    grad_ffn,
    grad_act,
    act,
):
    phase, k = pl.program_id(0), pl.program_id(1)

    @pl.when((phase == 0) & (k == 0))
    def _():
        sums[...] = jnp.zeros_like(sums)
        for half, (resid, cot) in enumerate(((mine, cot_own), (theirs, cot_got))):
            span = slice(128 * half, 128 * (half + 1))
            cross = slice(128 * (1 - half), 128 * (2 - half))
            first_norm, scaled, inverse = normalize(resid[...], vec[0:1], vec[1:2])
            low[span] = first_norm.astype(bf16)
            resid2 = first_norm + (ffn_own[span] + ffn_got[cross])
            normed, scaled, inverse = normalize(resid2, vec[2:3], vec[3:4])
            grad = cot[...].astype(f32)
            if half == 0:
                output[...] = normed.astype(bf16)
            sums[2:3] += jnp.sum(grad * scaled, axis=0, keepdims=True)
            sums[3:4] += jnp.sum(grad, axis=0, keepdims=True)
            grad = normalize_back(grad, scaled, inverse, vec[2:3])
            partial[span] = 0.5 * grad
            grad = grad.astype(bf16)
            for chunk in range(8 // STEP):
                grad_ffn[chunk, span] = grad[:, STEP * 128 * chunk : STEP * 128 * (chunk + 1)]
        grad_act[...] = jnp.zeros_like(grad_act)
        for chunk in range(8):
            own, got = act_own[chunk], act_got[chunk]
            got = jnp.concatenate([got[128:], got[:128]], axis=0)
            start = 512 * (chunk % 2)
            act[chunk // 2, :, start : start + 256] = jnp.where(core[0] == 0, own, got)
            act[chunk // 2, :, start + 256 : start + 512] = jnp.where(core[0] == 0, got, own)

    @pl.when(phase == 0)
    def _():
        grad = grad_ffn[k]
        own = [own_half(core, grad[:, 128 * column : 128 * (column + 1)]) for column in range(STEP)]
        own = jnp.concatenate(own, axis=1)
        for half in range(2):
            weights = owner_rows(reduce[:, :, 16 * half : 16 * (half + 1)])
            for part in range(4):
                grad_act[4 * half + part] += dot_nn(grad, weights[:, 256 * part : 256 * (part + 1)])
            made = [dot_tn(own, act[2 * half + part]).reshape(STEP, 8, 8, D) for part in range(2)]
            made = jnp.concatenate(made, axis=2).astype(bf16).reshape(STEP, 4, 2, 16, D)
            blocks[:, :, :, 0, 16 * half : 16 * (half + 1)] = made

    @pl.when(phase == 1)
    def _():
        for column in range(STEP):
            weights = expand[:, column].reshape(256, D)
            grad = (slope[column] * grad_act[STEP * k + column]).astype(bf16)
            made = dot_tn(grad, low[...]).astype(bf16)
            blocks[column, :, :, 0] = made.reshape(4, 2, 32, D)
            partial[...] += dot_nn(grad, weights)

    @pl.when((phase == 1) & (k == 8 // STEP - 1))
    def _():
        sent[...] = partial[...].astype(bf16)


def ffn_backward(
    core, mine, theirs, vec, ffn_own, ffn_got, cot_own, cot_got, act_own, act_got, slope, gathered
):
    whole = lambda phase, k: (0, 0)
    return pl.pallas_call(
        ffn_back_kernel,
        grid=(2, 8 // STEP),
        in_specs=[
            pl.BlockSpec(memory_space=pltpu.SMEM),
            pl.BlockSpec((128, D), whole),
            pl.BlockSpec((128, D), whole),
            pl.BlockSpec((4, D), whole),
            pl.BlockSpec((256, D), whole),
            pl.BlockSpec((256, D), whole),
            pl.BlockSpec((128, D), whole),
            pl.BlockSpec((128, D), whole),
            pl.BlockSpec((8, 256, 256), lambda phase, k: (0, 0, 0)),
            pl.BlockSpec((8, 256, 256), lambda phase, k: (0, 0, 0)),
            pl.BlockSpec((STEP, 256, 256), lambda phase, k: (jnp.where(phase == 0, 0, k), 0, 0)),
            pl.BlockSpec((8, STEP, 32, D), lambda phase, k: (0, jnp.where(phase == 0, 0, k), 0, 0)),
            pl.BlockSpec((8, STEP, 32, D), lambda phase, k: (0, jnp.where(phase == 0, k, 8 // STEP - 1), 1, 0)),
        ],
        out_specs=[
            pl.BlockSpec((128, D), whole),
            pl.BlockSpec(
                (STEP, 4, 2, 1, 32, D),
                lambda phase, k: (k % (4 // STEP), 0, 0, k // (4 // STEP), 1 - phase, 0),
            ),
            pl.BlockSpec((256, D), whole),
            pl.BlockSpec((256, D), whole),
            pl.BlockSpec((8, D), whole),
        ],
        out_shape=[
            jax.ShapeDtypeStruct((128, D), bf16),
            jax.ShapeDtypeStruct((4, 4, 2, 2, 64, D), bf16),
            jax.ShapeDtypeStruct((256, D), f32),
            jax.ShapeDtypeStruct((256, D), bf16),
            jax.ShapeDtypeStruct((8, D), f32),
        ],
        scratch_shapes=[
            pltpu.VMEM((256, D), bf16),
            pltpu.VMEM((8 // STEP, 256, STEP * 128), bf16),
            pltpu.VMEM((8, 256, 256), f32),
            pltpu.VMEM((4, 256, D), bf16),
        ],
        compiler_params=pltpu.CompilerParams(vmem_limit_bytes=56 * 2**20),
        name="ffn_backward",
    )(
        core,
        mine,
        theirs,
        vec,
        ffn_own,
        ffn_got,
        cot_own,
        cot_got,
        act_own,
        act_got,
        slope,
        gathered,
        gathered,
    )


def first_back_kernel(
    core,
    mine,
    theirs,
    vec,
    grad_own,
    grad_got,
    ctx_own,
    ctx_got,
    sums,
    weights,
    grad_resid,
    grad_context,
    blocks,
    grad_low,
    total,
    vec_sums,
):
    k = pl.program_id(0)

    @pl.when(k == 0)
    def _():
        found = sums[...]
        place = lax.broadcasted_iota(jnp.int32, (8, D), 0)
        for half, resid in enumerate((mine, theirs)):
            span = slice(128 * half, 128 * (half + 1))
            cross = slice(128 * (1 - half), 128 * (2 - half))
            normed, scaled, inverse = normalize(resid[...], vec[0:1], vec[1:2])
            grad = grad_own[span] + grad_got[cross]
            found += jnp.where(place == 0, jnp.sum(grad * scaled, axis=0, keepdims=True), 0.0)
            found += jnp.where(place == 1, jnp.sum(grad, axis=0, keepdims=True), 0.0)
            grad = normalize_back(grad, scaled, inverse, vec[0:1])
            if half == 0:
                grad_resid[...] = grad
            grad = grad.astype(bf16)
            for chunk in range(8 // STEP):
                grad_low[chunk, span] = grad[:, STEP * 128 * chunk : STEP * 128 * (chunk + 1)]
        for chunk in range(8):
            vec_sums[chunk] = found[:, 128 * chunk : 128 * (chunk + 1)]
        total[...] = jnp.zeros_like(total)

    grad = grad_low[k]
    total[...] += dot_nn(grad[:128], owner_rows(weights[...]))
    ctx = [jnp.concatenate([part[group] for group in range(8)], axis=1) for part in (ctx_own, ctx_got)]
    own = [own_half(core, grad[:, 128 * column : 128 * (column + 1)]) for column in range(STEP)]
    made = dot_tn(jnp.concatenate(own, axis=1), jnp.concatenate(ctx, axis=0)).reshape(STEP, 8, 8, D)
    for column in range(STEP):
        row = jnp.broadcast_to(vec_sums[STEP * k + column][None], (8, 8, 128))
        blocks[column] = jnp.concatenate([made[column], row], axis=-1).astype(bf16)

    @pl.when(k == 8 // STEP - 1)
    def _():
        for group in range(8):
            grad_context[group] = total[:, 128 * group : 128 * (group + 1)].astype(bf16)


def first_backward(
    core, mine, theirs, vec, grad_own, grad_got, ctx_own, ctx_got, sums, gathered
):
    whole = lambda k: (0, 0)
    return pl.pallas_call(
        first_back_kernel,
        grid=(8 // STEP,),
        in_specs=[
            pl.BlockSpec(memory_space=pltpu.SMEM),
            pl.BlockSpec((128, D), whole),
            pl.BlockSpec((128, D), whole),
            pl.BlockSpec((4, D), whole),
            pl.BlockSpec((256, D), whole),
            pl.BlockSpec((256, D), whole),
            pl.BlockSpec((8, 128, 128), lambda k: (0, 0, 0)),
            pl.BlockSpec((8, 128, 128), lambda k: (0, 0, 0)),
            pl.BlockSpec((8, D), whole),
            pl.BlockSpec((8, STEP, 16, D), lambda k: (0, k, 4, 0)),
        ],
        out_specs=[
            pl.BlockSpec((128, D), whole),
            pl.BlockSpec((8, 128, 128), lambda k: (0, 0, 0)),
            pl.BlockSpec((STEP, 8, 8, D + 128), lambda k: (k, 0, 0, 0)),
        ],
        out_shape=[
            jax.ShapeDtypeStruct((128, D), f32),
            jax.ShapeDtypeStruct((8, 128, 128), bf16),
            jax.ShapeDtypeStruct((8, 8, 8, D + 128), bf16),
        ],
        scratch_shapes=[
            pltpu.VMEM((8 // STEP, 256, STEP * 128), bf16),
            pltpu.VMEM((128, D), f32),
            pltpu.VMEM((8, 8, 128), f32),
        ],
        compiler_params=pltpu.CompilerParams(vmem_limit_bytes=56 * 2**20),
        name="first_backward",
    )(core, mine, theirs, vec, grad_own, grad_got, ctx_own, ctx_got, sums, gathered)


def two_parts(value):
    upper = value.astype(bf16)
    return upper, (value - upper.astype(f32)).astype(bf16)


def swap(value):
    return lax.ppermute(value, "core", [(0, 1), (1, 0)])


def swap_chips(value):
    return lax.ppermute(value, "yl", [(0, 1), (1, 0)])


def exchange(value, axes):
    return lax.all_to_all(value, axes, 0, 0, tiled=True)


def shifted(value, axis, size, step):
    return lax.ppermute(value, axis, [(i, (i + step) % size) for i in range(size)])


def stacked(value, axis):
    size = lax.axis_size(axis)
    return jnp.stack([value] + [shifted(value, axis, size, step) for step in range(1, size)])


def places_back(axis):
    size = lax.axis_size(axis)
    return (lax.axis_index(axis) - jnp.arange(size)) % size


def pick(blocks, index):
    return blocks.at[index.reshape(-1)].get(mode="promise_in_bounds")


def spread(value, axes):
    return exchange(jnp.broadcast_to(value[None], (8,) + value.shape), axes)


def gather_projection(rows_t, table_rows, position_rows):
    first = spread(jnp.concatenate([rows_t[:, :512], table_rows], axis=0), GROUP)
    first, second = lax.optimization_barrier((first, rows_t[:, 512:]))
    second = stacked(stacked(second, "x"), "yl").reshape(8 * 24, 512)
    first = jnp.concatenate([first.reshape(256, 512), position_rows], axis=0)
    first, second = lax.optimization_barrier((stacked(first, "yl"), second))
    first = first.reshape(2, 9, 32, 512)
    table = jnp.concatenate([first[:, :8, 24:].reshape(2, 64, 512), first[:, 8]], axis=1)
    first = stacked(first[:, :8, :24], "x").reshape(8, 8, 24, 512)
    second = spread(second, GROUP).reshape(8, 8, 24, 512)
    table = stacked(table, "x").reshape(8, 96, 512)
    x, yl = places_back("x")[None], places_back("yl")[:, None]
    order = jnp.stack([(yl + 2 * x).reshape(-1), (x + 4 * yl).reshape(-1)])
    table = table.at[order[0]].get(mode="promise_in_bounds")
    return first, second, order, table[:, :64].reshape(512, 512), table[:, 64:]


def pack_kernel(core, expand, reduce, attend, vectors, got, packet):
    first = core[0] == 0
    packet[:32] = expand[...]
    inner = []
    for source in (reduce, got):
        spans = [source[:, 512 * k : 512 * (k + 1)].astype(f32) for k in range(8)]
        inner.append([jnp.where(first, span[:, :256], span[:, 256:]) for span in spans])
    for half in range(2):
        parts = [jnp.concatenate(rows_in[4 * half : 4 * half + 4], axis=1) for rows_in in inner]
        low, high = jnp.where(first, *parts), jnp.where(first, *reversed(parts))
        joined = jnp.concatenate([low, high], axis=0).astype(bf16)
        packet[32 + 16 * half : 48 + 16 * half] = joined
    own, other = attend[...].astype(f32), got[:, FF : FF + D].astype(f32)
    joined = jnp.concatenate([jnp.where(first, own, other), jnp.where(first, other, own)], axis=0)
    packet[64:80] = joined.astype(bf16)
    own, other = vectors[:4].astype(f32), got[:4, FF + D :].astype(f32)
    joined = jnp.concatenate([jnp.where(first, own, other), jnp.where(first, other, own)], axis=0)
    packet[80:] = jnp.concatenate([joined, jnp.zeros((8, D - 128), f32)], axis=1).astype(bf16)


def pack(core, expand, reduce, attend, vectors, got):
    return pl.pallas_call(
        pack_kernel,
        in_specs=[pl.BlockSpec(memory_space=pltpu.SMEM)]
        + [pl.BlockSpec(memory_space=pltpu.VMEM)] * 5,
        out_specs=pl.BlockSpec(memory_space=pltpu.VMEM),
        out_shape=jax.ShapeDtypeStruct((88, D), bf16),
        compiler_params=pltpu.CompilerParams(vmem_limit_bytes=60 * 2**20),
        name="pack",
    )(core, expand, reduce, attend, vectors, got)


def project_kernel(order, mine, theirs, first, second, packed, rows_out):
    tokens = jnp.concatenate([mine[...], theirs[...]], axis=0)
    low = first[0].astype(f32).reshape(192, 512).astype(bf16)
    high = second[:, 0].astype(f32).reshape(192, 512).astype(bf16)
    made = dot_nt(tokens[:, :512], low) + dot_nt(tokens[:, 512:], high)
    packed[0] = made.astype(bf16)
    rows_out[:, :512] = low
    rows_out[:, 512:] = high


def project(order, mine, theirs, first, second):
    return pl.pallas_call(
        project_kernel,
        grid_spec=pltpu.PrefetchScalarGridSpec(
            num_scalar_prefetch=1,
            grid=(8,),
            in_specs=[
                pl.BlockSpec((128, D), lambda k, order: (0, 0)),
                pl.BlockSpec((128, D), lambda k, order: (0, 0)),
                pl.BlockSpec((1, 8, 24, 512), lambda k, order: (order[0, k], 0, 0, 0)),
                pl.BlockSpec((8, 1, 24, 512), lambda k, order: (0, order[1, k], 0, 0)),
            ],
            out_specs=[
                pl.BlockSpec((1, 256, 192), lambda k, order: (k, 0, 0)),
                pl.BlockSpec((192, D), lambda k, order: (k, 0)),
            ],
        ),
        out_shape=[
            jax.ShapeDtypeStruct((8, 256, 192), bf16),
            pltpu.HBM((1536, D), bf16),
        ],
        compiler_params=pltpu.CompilerParams(vmem_limit_bytes=32 * 2**20),
        name="project",
    )(order, mine, theirs, first, second)


def arrange_kernel(core, mine, theirs, heads):
    for column in range(8):
        own, other = mine[column].astype(f32), theirs[column].astype(f32)
        first = core[0] == 0
        joined = jnp.concatenate(
            [jnp.where(first, own, other), jnp.where(first, other, own)], axis=1
        )
        for place in range(3):
            chunk = 3 * column + place
            heads[chunk % 8, chunk // 8] = joined[:, 128 * place : 128 * (place + 1)].astype(bf16)


def arrange(core, mine, theirs):
    return pl.pallas_call(
        arrange_kernel,
        in_specs=[
            pl.BlockSpec(memory_space=pltpu.SMEM),
            pl.BlockSpec(memory_space=pltpu.VMEM),
            pl.BlockSpec(memory_space=pltpu.VMEM),
        ],
        out_specs=pl.BlockSpec(memory_space=pltpu.VMEM),
        out_shape=jax.ShapeDtypeStruct((8, 3, 128, 128), bf16),
        compiler_params=pltpu.CompilerParams(vmem_limit_bytes=32 * 2**20),
        name="arrange",
    )(core, mine, theirs)


def project_grad_kernel(
    keep, got, keep_pair, got_pair, tokens_own, tokens_got, tokens_pair, table, blocks
):
    tokens = jnp.concatenate([tokens_own[...], tokens_got[...], tokens_pair[...]], axis=0)
    for step in range(2):
        span = slice(384 * step, 384 * (step + 1))
        parts = [part[:, span] for part in (keep, got, keep_pair, got_pair)]
        made = dot_tn(jnp.concatenate(parts, axis=0), tokens).reshape(16, 24, D)
        rest = table[128 * step : 128 * (step + 1)].reshape(16, 8, 512)
        made = jnp.concatenate([made[..., :512], made[..., 512:], rest], axis=1)
        blocks[16 * step : 16 * (step + 1)] = made.astype(bf16)


def project_grad(keep, got, keep_pair, got_pair, tokens_own, tokens_got, tokens_pair, table):
    return pl.pallas_call(
        project_grad_kernel,
        in_specs=[pl.BlockSpec(memory_space=pltpu.VMEM)] * 8,
        out_specs=pl.BlockSpec(memory_space=pltpu.VMEM),
        out_shape=jax.ShapeDtypeStruct((32, 56, 512), bf16),
        compiler_params=pltpu.CompilerParams(vmem_limit_bytes=48 * 2**20),
        name="project_grad",
    )(keep, got, keep_pair, got_pair, tokens_own, tokens_got, tokens_pair, table)


def ring_scatter(blocks, axis, size, dtype=f32):
    place = lax.axis_index(axis)
    total = lax.dynamic_index_in_dim(blocks, place, 0, keepdims=False).astype(f32)
    for step in range(1, size):
        sent = lax.dynamic_index_in_dim(blocks, (place + step) % size, 0, keepdims=False)
        total = total + shifted(sent, axis, size, step).astype(f32)
    return total.astype(dtype)


def y_scatter(blocks):
    place = 2 * lax.axis_index("yh") + lax.axis_index("yl")
    total = lax.dynamic_index_in_dim(blocks, place, 0, keepdims=False).astype(f32)

    def on_mesh(y):
        return 2 * (y % 2) + y // 2

    for step in range(1, 4):
        sent = lax.dynamic_index_in_dim(blocks, (place + step) % 4, 0, keepdims=False)
        ring = [(on_mesh(y), on_mesh((y + step) % 4)) for y in range(4)]
        total = total + lax.ppermute(sent, ("yl", "yh"), ring).astype(f32)
    return total


def split_kernel(core, heads, keep, give):
    for column in range(8):
        chunks = [3 * column + place for place in range(3)]
        joined = jnp.concatenate(
            [heads[chunk % 8, chunk // 8].astype(f32) for chunk in chunks], axis=1
        )
        first = core[0] == 0
        zero, one = joined[:, :192], joined[:, 192:]
        span = slice(192 * column, 192 * (column + 1))
        keep[:, span] = jnp.where(first, zero, one).astype(bf16)
        give[:, span] = jnp.where(first, one, zero).astype(bf16)


def split(core, heads):
    return pl.pallas_call(
        split_kernel,
        in_specs=[
            pl.BlockSpec(memory_space=pltpu.SMEM),
            pl.BlockSpec(memory_space=pltpu.VMEM),
        ],
        out_specs=[pl.BlockSpec(memory_space=pltpu.VMEM)] * 2,
        out_shape=[jax.ShapeDtypeStruct((128, 1536), bf16)] * 2,
        compiler_params=pltpu.CompilerParams(vmem_limit_bytes=32 * 2**20),
        name="split",
    )(core, heads)


def per_device(
    tokens,
    w_project,
    w_attend,
    first_gain,
    first_shift,
    w_expand,
    w_reduce,
    second_gain,
    second_shift,
    position_table,
    w_query,
    w_key,
    lengths,
    cotangent,
):
    core = lax.axis_index("core")
    group = lax.axis_index(GROUP)
    local = tokens.shape[0]
    core_id = core.reshape(1)
    pair = 2 * local
    column_bucket = bucket_values(SEQ - 1 - np.arange(2 * SEQ - 1), SPAN)
    fold = np.append(column_bucket, -1)[None, :] == np.arange(2 * SPAN)[:, None]
    fold = jnp.asarray(fold.astype(np.float32)).astype(bf16)

    def by_core(zero, one):
        return jnp.where(core == 0, zero, one)

    def in_order(mine, theirs):
        return by_core(mine, theirs), by_core(theirs, mine)

    cotangent_got = swap(cotangent)
    tokens_got = swap(tokens)
    weights_own = jnp.concatenate([w_key, w_query], axis=1)
    first, second, order, table_t, position_rows = gather_projection(
        w_project.T,
        position_table.T,
        jnp.concatenate([weights_own[:32], weights_own[32:]], axis=1),
    )
    position_weights = jnp.stack([position_rows[..., :256], position_rows[..., 256:]], axis=1)
    position_weights = position_weights.reshape(512, 256)

    vectors = jnp.stack([first_gain, first_shift, second_gain, second_shift])
    vectors = jnp.pad(vectors, ((0, 4), (0, 128 - 8)))
    reduce_rows = w_reduce.T
    got = swap(jnp.concatenate([reduce_rows, w_attend.T, vectors], axis=1))
    packet = pack(core_id, w_expand.T, reduce_rows, w_attend.T, vectors, got)
    gathered = lax.all_gather(packet, CHIPS, axis=0, tiled=False).reshape(8, 8, 88, D)
    vec = gathered[..., 80:, :8].reshape(8, 8, 2, 4, 8).transpose(3, 1, 2, 0, 4)
    vec = vec.reshape(4, D).astype(f32)
    gain_one, shift_one, gain_two, shift_two = vec[0], vec[1], vec[2], vec[3]

    packed, project_t = project(order, tokens, tokens_got, first, second)
    heads_in = exchange(arrange(core_id, packed[:, :local], swap(packed[:, local:])), GROUP)
    rel = dot_tn(table_t, position_weights)
    rel = dot_tn(fold, (rel + swap(rel)).astype(bf16)).astype(bf16)
    heads_in, tokens_both = lax.optimization_barrier(
        (heads_in, jnp.concatenate([tokens, tokens_got], axis=0))
    )
    tokens_pair = swap_chips(tokens_both)
    context, tokens_pair = lax.optimization_barrier(
        (exchange(attend(lengths, heads_in, rel), GROUP), tokens_pair)
    )
    context_got = swap(context)

    resid_own = project_back(context, tokens, gathered)
    resid_got = swap(resid_own)
    activ, slope, ffn_own, ffn_sent = ffn_forward(resid_own, resid_got, vec, gathered)
    output, blocks, grad_own, grad_sent, sums = ffn_backward(
        core_id,
        resid_own,
        resid_got,
        vec,
        ffn_own,
        swap(ffn_sent),
        cotangent,
        cotangent_got,
        activ,
        swap(activ),
        slope,
        gathered,
    )
    grad_resid1, grad_context, attend_blocks = first_backward(
        core_id,
        resid_own,
        resid_got,
        vec,
        grad_own,
        swap(grad_sent),
        context,
        context_got,
        sums,
        gathered,
    )

    summed = lax.psum_scatter(
        blocks.reshape(16, 4 * 64, D), ("x", "z"), scatter_dimension=0, tiled=True
    )
    attend_blocks, grad_ctx = lax.optimization_barrier(
        (attend_blocks, exchange(grad_context, GROUP))
    )
    attend_sum = exchange(attend_blocks.reshape(64, 8, D + 128), COLUMN + GROUP)

    grads, rel_grad = attend_back(lengths, heads_in, rel, grad_ctx)
    grads, attend_sum = lax.optimization_barrier((grads, attend_sum))
    attend_sum = jnp.sum(attend_sum.astype(f32), axis=0)
    grad_attend = attend_sum[:, :D].T
    vectors = attend_sum[:4, D:].reshape(4, 16, 8)
    vectors = lax.dynamic_index_in_dim(vectors, 8 * core + group, axis=1, keepdims=False)
    grads = exchange(grads, GROUP)
    yl = lax.axis_index("yl")
    rel_grad = sum(dot_nn(fold, part) for part in two_parts(rel_grad))
    rel_grad = rel_grad + swap(rel_grad)
    rel_grad = two_parts(rel_grad + swap_chips(rel_grad.astype(bf16)).astype(f32))
    table_half = lax.dynamic_slice_in_dim(table_t, 256 * yl, 256, axis=0)
    weights_half = lax.dynamic_slice_in_dim(position_weights, 256 * yl, 256, axis=0)
    position_grads = sum(dot_nn(table_half, part) for part in rel_grad)
    position_grads = ring_scatter(position_grads.reshape(4, 64, 256), "x", 4)
    table_blocks = sum(dot_nt(weights_half, part) for part in rel_grad)

    def by_chip(value):
        low, high = value[:, :768], value[:, 768:]
        return jnp.where(yl == 0, low, high), jnp.where(yl == 0, high, low)

    grads, position_grads = lax.optimization_barrier((grads, position_grads))
    keep, give = split(core_id, grads)
    keep_half, keep_other = by_chip(keep)
    got = swap(give)
    got_half, got_other = by_chip(got)
    blocks = project_grad(
        keep_half,
        got_half,
        swap_chips(keep_other),
        swap_chips(got_other),
        tokens,
        tokens_got,
        tokens_pair,
        table_blocks,
    )
    blocks, got = lax.optimization_barrier((blocks, got))
    tokens_part = dot_nn(keep, project_t)
    tokens_sent = dot_nn(got, project_t).astype(bf16)
    tokens_sent, summed = lax.optimization_barrier((tokens_sent, summed))
    received, summed, tokens_back = lax.optimization_barrier(
        (
            exchange(blocks, ("x",) + GROUP),
            y_scatter(summed.reshape(4, 64, D)),
            swap(tokens_sent),
        )
    )
    grad_expand = summed[:32].T
    grad_reduce = summed[32:64].reshape(4, 8, D).transpose(1, 0, 2).reshape(8, FF).T
    received = jnp.sum(received.astype(f32), axis=0)
    grad_project = jnp.concatenate([received[:24], received[24:48]], axis=1).T
    grad_table = received[48:].T
    tokens_grad = grad_resid1 + (tokens_part + tokens_back)
    grad_key, grad_query = position_grads[:, :128], position_grads[:, 128:]

    return (
        output,
        tokens_grad.astype(bf16),
        grad_project,
        grad_attend,
        vectors[0],
        vectors[1],
        grad_expand,
        grad_reduce,
        vectors[2],
        vectors[3],
        grad_table,
        grad_query,
        grad_key,
    )


def solution(mesh):
    parts = Mesh(mesh.devices.reshape(2, 4, 2, 4, 2), EVERY)
    in_specs = (
        P(EVERY, None),
        P(None, EVERY),
        P(None, EVERY),
        P(EVERY),
        P(EVERY),
        P(None, EVERY),
        P(None, EVERY),
        P(EVERY),
        P(EVERY),
        P(None, EVERY),
        P(DP, GROUP),
        P(DP, GROUP),
        P(DP),
        P(EVERY, None),
    )
    out_specs = (
        P(EVERY, None),
        P(EVERY, None),
        P(None, EVERY),
        P(None, EVERY),
        P(EVERY),
        P(EVERY),
        P(None, EVERY),
        P(None, EVERY),
        P(EVERY),
        P(EVERY),
        P(None, EVERY),
        P(DP, GROUP),
        P(DP, GROUP),
    )
    return jax.shard_map(
        per_device, mesh=parts, in_specs=in_specs, out_specs=out_specs, check_vma=False
    )
```

```python
import math

import jax
import jax.numpy as jnp
import numpy as np
from jax import lax
from jax.experimental import pallas as pl
from jax.experimental.pallas import tpu as pltpu
from jax.sharding import Mesh
from jax.sharding import PartitionSpec as P

D = 1024
HEADS = 16
HEAD_DIM = 64
FF = 4096
SPAN = 256
SEQ = 512
BLOCK = 128
WINDOW = SEQ + BLOCK
STEP = 4

EPS = 1e-07
MASKED = -1e30

DP = ("yl", "x", "core")
GROUP = ("z", "yh")
COLUMN = ("yl", "x")
EVERY = DP + GROUP
CHIPS = ("z", "yh", "yl", "x")
DEVICES = ("core",) + CHIPS
bf16 = jnp.bfloat16
f32 = jnp.float32


def bucket_values(offset, span):
    middle = span // 2
    absolute = np.where((offset < middle) & (offset > -middle), middle - 1, np.abs(offset))
    log_place = (
        np.ceil(np.log(absolute / middle) / np.log((2 * span - 1) / middle) * (middle - 1)) + middle
    )
    buckets = np.where(absolute <= middle, offset, log_place * np.sign(offset)).astype(np.int64)
    return np.clip(buckets + span, 0, 2 * span - 1).astype(np.int32)


def normalize(value, gain, shift):
    center = value - jnp.mean(value, axis=-1, keepdims=True)
    inverse = lax.rsqrt(jnp.mean(center * center, axis=-1, keepdims=True) + EPS)
    scaled = center * inverse
    return (scaled * gain + shift, scaled, inverse)


def normalize_back(incoming, scaled, inverse, gain):
    grad_scaled = incoming * gain
    middle = (
        grad_scaled
        - jnp.mean(grad_scaled, axis=-1, keepdims=True)
        - scaled * jnp.mean(grad_scaled * scaled, axis=-1, keepdims=True)
    )
    return inverse * middle


def dot_nn(left, right):
    return lax.dot_general(left, right, (((1,), (0,)), ((), ())), preferred_element_type=f32)


def dot_nt(left, right):
    return lax.dot_general(left, right, (((1,), (1,)), ((), ())), preferred_element_type=f32)


def dot_tn(left, right):
    return lax.dot_general(left, right, (((0,), (0,)), ((), ())), preferred_element_type=f32)


def window(block):
    start = SEQ - BLOCK - BLOCK * block
    return slice(start, start + WINDOW)


def rows(block):
    return slice(BLOCK * block, BLOCK * (block + 1))


def skew(values):
    return pltpu.roll(values, SEQ + 1, 1, stride=1, stride_axis=0)[:, :SEQ]


def unskew(values):
    wide = jnp.concatenate([values, jnp.zeros((BLOCK, BLOCK), f32)], axis=1)
    return pltpu.roll(wide, 0, 1, stride=1, stride_axis=0)


def turn(mirror, values):
    upper = values.astype(bf16)
    return dot_nn(mirror, upper) + dot_nn(mirror, (values - upper.astype(f32)).astype(bf16))


def one_head(value, head):
    lane = lax.broadcasted_iota(jnp.int32, value.shape, 1)
    return jnp.where(lane // HEAD_DIM == head, value, jnp.zeros_like(value))


def query_bias(key, rel_queries, bias):
    for block in range(SEQ // BLOCK):
        by_offset = dot_nt(key[rows(block)], rel_queries[window(block)])
        bias[:, rows(block)] = skew(by_offset).T


def probabilities(query, key, rel_keys, bias, block, length):
    part = query[rows(block)]
    logits = dot_nt(part, key) + skew(dot_nt(part, rel_keys[window(block)])) + bias[rows(block)]
    logits = logits * (1.0 / math.sqrt(3 * HEAD_DIM))
    column = lax.broadcasted_iota(jnp.int32, logits.shape, 1)
    logits = jnp.where(column < length, logits, MASKED)
    exponent = jnp.exp(logits - jnp.max(logits, axis=1, keepdims=True))
    return exponent * (1.0 / jnp.sum(exponent, axis=1, keepdims=True))


def attend_kernel(lengths, heads_in, rel, context, kept, bias):
    length = lengths[pl.program_id(0)]
    query, key, values = (heads_in[:, part].reshape(SEQ, 128) for part in range(3))
    rel_keys, rel_queries = rel[:, :128], rel[:, 128:]
    total = [jnp.zeros((BLOCK, 128), f32) for _ in range(SEQ // BLOCK)]
    for head in range(2):
        query_h, key_h, values_h = (one_head(part, head) for part in (query, key, values))
        query_bias(key_h, rel_queries, bias)
        for block in range(SEQ // BLOCK):
            probs = probabilities(query_h, key, rel_keys, bias, block, length)
            kept[0, head, rows(block)] = probs
            total[block] = total[block] + dot_nn(probs.astype(bf16), values_h)
    for block in range(SEQ // BLOCK):
        context[block] = total[block].astype(bf16)


def attend_back_kernel(
    heads_in, rel, grad_context, kept, grads, grad_rel, probs_ref, grad_ref
):
    query, key, values = (heads_in[:, part].reshape(SEQ, 128) for part in range(3))
    grad_ctx = grad_context[...].reshape(SEQ, 128)
    rel_keys, rel_queries = rel[:, :128], rel[:, 128:]
    blocks = SEQ // BLOCK
    first = lax.broadcasted_iota(jnp.int32, (BLOCK, BLOCK), 0)
    second = lax.broadcasted_iota(jnp.int32, (BLOCK, BLOCK), 1)
    mirror = jnp.where(first + second == BLOCK - 1, 1.0, 0.0).astype(bf16)

    @pl.when(pl.program_id(0) == 0)
    def _():
        grad_rel[...] = jnp.zeros_like(grad_rel)

    queries, keys, ctxs = (
        [one_head(part, head) for head in range(2)] for part in (query, key, grad_ctx)
    )
    rel_keys_of = [one_head(rel_keys, head) for head in range(2)]
    rel_queries_of = [one_head(rel_queries, head) for head in range(2)]
    for block in range(blocks):
        grad_q, turned, rel_part = 0.0, 0.0, 0.0
        for head in range(2):
            probs = kept[0, head, rows(block)]
            probs_ref[head, rows(block)] = probs.astype(bf16)
            grad_probs = dot_nt(ctxs[head][rows(block)], values)
            inner = jnp.sum(probs * grad_probs, axis=1, keepdims=True)
            grad = (probs * (grad_probs - inner) * (1.0 / math.sqrt(3 * HEAD_DIM))).astype(bf16)
            grad_ref[head, rows(block)] = grad
            by_offset = unskew(dot_nn(mirror, grad)).astype(bf16)
            grad_q = grad_q + dot_nn(grad, keys[head])
            turned = turned + dot_nn(by_offset, rel_keys_of[head][window(block)])
            mirrored = dot_nn(mirror, queries[head][rows(block)]).astype(bf16)
            rel_part = rel_part + dot_tn(by_offset, mirrored)
        grad_rel[window(block), :128] += rel_part
        grads[block, 0] = (grad_q + turn(mirror, turned)).astype(bf16)
    for block in range(blocks):
        grad_k, grad_v, turned, rel_part = 0.0, 0.0, 0.0, 0.0
        for head in range(2):
            grad = grad_ref[head, :, rows(block)]
            by_offset = unskew(dot_nt(mirror, grad)).astype(bf16)
            grad_k = grad_k + dot_tn(grad, queries[head])
            turned = turned + dot_nn(by_offset, rel_queries_of[head][window(block)])
            grad_v = grad_v + dot_tn(probs_ref[head, :, rows(block)], ctxs[head])
            mirrored = dot_nn(mirror, keys[head][rows(block)]).astype(bf16)
            rel_part = rel_part + dot_tn(by_offset, mirrored)
        grad_rel[window(block), 128:] += rel_part
        grads[block, 1] = (grad_k + turn(mirror, turned)).astype(bf16)
        grads[block, 2] = grad_v.astype(bf16)


def attend(lengths, heads_in, rel):
    return pl.pallas_call(
        attend_kernel,
        grid=(2,),
        in_specs=[
            pl.BlockSpec(memory_space=pltpu.SMEM),
            pl.BlockSpec((4, 3, 128, 128), lambda row: (row, 0, 0, 0)),
            pl.BlockSpec((2 * SEQ, 256), lambda row: (0, 0)),
        ],
        out_specs=[
            pl.BlockSpec((4, 128, 128), lambda row: (row, 0, 0)),
            pl.BlockSpec((1, 2, SEQ, SEQ), lambda row: (row, 0, 0, 0)),
        ],
        out_shape=[
            jax.ShapeDtypeStruct((8, 128, 128), bf16),
            pltpu.HBM((2, 2, SEQ, SEQ), f32),
        ],
        scratch_shapes=[pltpu.VMEM((SEQ, SEQ), f32)],
        compiler_params=pltpu.CompilerParams(vmem_limit_bytes=48 * 2**20),
        name="attend",
    )(lengths, heads_in, rel)


def attend_back(heads_in, rel, grad_context, kept):
    return pl.pallas_call(
        attend_back_kernel,
        grid=(2,),
        in_specs=[
            pl.BlockSpec((4, 3, 128, 128), lambda row: (row, 0, 0, 0)),
            pl.BlockSpec((2 * SEQ, 256), lambda row: (0, 0)),
            pl.BlockSpec((4, 128, 128), lambda row: (row, 0, 0)),
            pl.BlockSpec((1, 2, SEQ, SEQ), lambda row: (row, 0, 0, 0)),
        ],
        out_specs=[
            pl.BlockSpec((4, 3, 128, 128), lambda row: (row, 0, 0, 0)),
            pl.BlockSpec((2 * SEQ, 256), lambda row: (0, 0)),
        ],
        out_shape=[
            jax.ShapeDtypeStruct((8, 3, 128, 128), bf16),
            jax.ShapeDtypeStruct((2 * SEQ, 256), f32),
        ],
        scratch_shapes=[
            pltpu.VMEM((2, SEQ, SEQ), bf16),
            pltpu.VMEM((2, SEQ, SEQ), bf16),
        ],
        compiler_params=pltpu.CompilerParams(vmem_limit_bytes=48 * 2**20),
        cost_estimate=pl.CostEstimate(
            flops=20 * 10**9, bytes_accessed=8 * 2**20, transcendentals=2**20
        ),
        name="attend_back",
    )(heads_in, rel, grad_context, kept)


def owner_rows(block):
    wide = block.astype(f32).reshape(8, STEP, 2, 8, block.shape[-1])
    return wide.transpose(1, 2, 0, 3, 4).reshape(STEP * 128, block.shape[-1]).astype(bf16)


def project_back_kernel(context, tokens, weights, resid):
    rows_in = jnp.concatenate([context[group] for group in range(8)], axis=1)
    resid[...] = tokens[...].astype(f32) + dot_nt(rows_in, owner_rows(weights[...]))


def project_back(context, tokens, gathered):
    return pl.pallas_call(
        project_back_kernel,
        grid=(8 // STEP,),
        in_specs=[
            pl.BlockSpec((8, 128, 128), lambda k: (0, 0, 0)),
            pl.BlockSpec((128, STEP * 128), lambda k: (0, k)),
            pl.BlockSpec((8, STEP, 16, D), lambda k: (0, k, 4, 0)),
        ],
        out_specs=pl.BlockSpec((128, STEP * 128), lambda k: (0, k)),
        out_shape=jax.ShapeDtypeStruct((128, D), f32),
        compiler_params=pltpu.CompilerParams(vmem_limit_bytes=48 * 2**20),
        name="project_back",
    )(context, tokens, gathered)


def ffn_kernel(mine, theirs, vec, expand, reduce, act, slope, partial, sent, low):
    phase, k = pl.program_id(0), pl.program_id(1)

    @pl.when((phase == 0) & (k == 0))
    def _():
        for half, resid in enumerate((mine, theirs)):
            first_norm, scaled, inverse = normalize(resid[...], vec[0:1], vec[1:2])
            low[128 * half : 128 * (half + 1)] = first_norm.astype(bf16)

    @pl.when(phase == 0)
    def _():
        for column in range(STEP):
            inner = dot_nt(low[...], expand[:, column].reshape(256, D))
            spread_in = 0.5 + 0.5 * lax.erf(inner * math.sqrt(0.5))
            act[STEP * k + column] = (inner * spread_in).astype(bf16)
            density = jnp.exp(-0.5 * inner * inner) * (1.0 / math.sqrt(2.0 * math.pi))
            slope[column] = spread_in + inner * density

    @pl.when(phase == 1)
    def _():
        total = jnp.zeros((256, STEP * 128), f32)
        for half in range(2):
            rows_in = jnp.concatenate([act[4 * half + part] for part in range(4)], axis=1)
            weights = owner_rows(reduce[:, :, 16 * half : 16 * (half + 1)])
            total = total + dot_nt(rows_in, weights)
        partial[...] = total
        sent[...] = total.astype(bf16)


def ffn_forward(mine, theirs, vec, gathered):
    whole = lambda phase, k: (0, 0)
    return pl.pallas_call(
        ffn_kernel,
        grid=(2, 8 // STEP),
        in_specs=[
            pl.BlockSpec((128, D), whole),
            pl.BlockSpec((128, D), whole),
            pl.BlockSpec((4, D), whole),
            pl.BlockSpec((8, STEP, 32, D), lambda phase, k: (0, jnp.where(phase == 0, k, 8 // STEP - 1), 0, 0)),
            pl.BlockSpec((8, STEP, 32, D), lambda phase, k: (0, jnp.where(phase == 0, 0, k), 1, 0)),
        ],
        out_specs=[
            pl.BlockSpec((8, 256, 256), lambda phase, k: (0, 0, 0)),
            pl.BlockSpec((STEP, 256, 256), lambda phase, k: (jnp.where(phase == 0, k, 8 // STEP - 1), 0, 0)),
            pl.BlockSpec((256, STEP * 128), lambda phase, k: (0, jnp.where(phase == 0, 0, k))),
            pl.BlockSpec((256, STEP * 128), lambda phase, k: (0, jnp.where(phase == 0, 0, k))),
        ],
        out_shape=[
            jax.ShapeDtypeStruct((8, 256, 256), bf16),
            jax.ShapeDtypeStruct((8, 256, 256), f32),
            jax.ShapeDtypeStruct((256, D), f32),
            jax.ShapeDtypeStruct((256, D), bf16),
        ],
        scratch_shapes=[pltpu.VMEM((256, D), bf16)],
        compiler_params=pltpu.CompilerParams(vmem_limit_bytes=48 * 2**20),
        name="ffn_forward",
    )(mine, theirs, vec, gathered, gathered)


def own_half(core, wide):
    return jnp.where(core[0] == 0, wide[:, :64], wide[:, 64:])


def ffn_back_kernel(
    core,
    mine,
    theirs,
    vec,
    ffn_own,
    ffn_got,
    cot_own,
    cot_got,
    act_own,
    act_got,
    slope,
    expand,
    reduce,
    output,
    blocks,
    partial,
    sent,
    sums,
    low,
    grad_ffn,
    grad_act,
    act,
):
    phase, k = pl.program_id(0), pl.program_id(1)

    @pl.when((phase == 0) & (k == 0))
    def _():
        sums[...] = jnp.zeros_like(sums)
        for half, (resid, cot) in enumerate(((mine, cot_own), (theirs, cot_got))):
            span = slice(128 * half, 128 * (half + 1))
            cross = slice(128 * (1 - half), 128 * (2 - half))
            first_norm, scaled, inverse = normalize(resid[...], vec[0:1], vec[1:2])
            low[span] = first_norm.astype(bf16)
            resid2 = first_norm + (ffn_own[span] + ffn_got[cross])
            normed, scaled, inverse = normalize(resid2, vec[2:3], vec[3:4])
            grad = cot[...].astype(f32)
            if half == 0:
                output[...] = normed.astype(bf16)
            sums[2:3] += jnp.sum(grad * scaled, axis=0, keepdims=True)
            sums[3:4] += jnp.sum(grad, axis=0, keepdims=True)
            grad = normalize_back(grad, scaled, inverse, vec[2:3])
            partial[span] = 0.5 * grad
            grad = grad.astype(bf16)
            for chunk in range(8 // STEP):
                grad_ffn[chunk, span] = grad[:, STEP * 128 * chunk : STEP * 128 * (chunk + 1)]
        grad_act[...] = jnp.zeros_like(grad_act)
        for chunk in range(8):
            own, got = act_own[chunk], act_got[chunk]
            got = jnp.concatenate([got[128:], got[:128]], axis=0)
            start = 512 * (chunk % 2)
            act[chunk // 2, :, start : start + 256] = jnp.where(core[0] == 0, own, got)
            act[chunk // 2, :, start + 256 : start + 512] = jnp.where(core[0] == 0, got, own)

    @pl.when(phase == 0)
    def _():
        grad = grad_ffn[k]
        own = [own_half(core, grad[:, 128 * column : 128 * (column + 1)]) for column in range(STEP)]
        own = jnp.concatenate(own, axis=1)
        for half in range(2):
            weights = owner_rows(reduce[:, :, 16 * half : 16 * (half + 1)])
            for part in range(4):
                grad_act[4 * half + part] += dot_nn(grad, weights[:, 256 * part : 256 * (part + 1)])
            made = [dot_tn(own, act[2 * half + part]).reshape(STEP, 8, 8, D) for part in range(2)]
            made = jnp.concatenate(made, axis=2).astype(bf16).reshape(STEP, 4, 2, 16, D)
            blocks[:, :, :, 0, 16 * half : 16 * (half + 1)] = made

    @pl.when(phase == 1)
    def _():
        for column in range(STEP):
            weights = expand[:, column].reshape(256, D)
            grad = (slope[column] * grad_act[STEP * k + column]).astype(bf16)
            made = dot_tn(grad, low[...]).astype(bf16)
            blocks[column, :, :, 0] = made.reshape(4, 2, 32, D)
            partial[...] += dot_nn(grad, weights)

    @pl.when((phase == 1) & (k == 8 // STEP - 1))
    def _():
        sent[...] = partial[...].astype(bf16)


def ffn_backward(
    core, mine, theirs, vec, ffn_own, ffn_got, cot_own, cot_got, act_own, act_got, slope, gathered
):
    whole = lambda phase, k: (0, 0)
    return pl.pallas_call(
        ffn_back_kernel,
        grid=(2, 8 // STEP),
        in_specs=[
            pl.BlockSpec(memory_space=pltpu.SMEM),
            pl.BlockSpec((128, D), whole),
            pl.BlockSpec((128, D), whole),
            pl.BlockSpec((4, D), whole),
            pl.BlockSpec((256, D), whole),
            pl.BlockSpec((256, D), whole),
            pl.BlockSpec((128, D), whole),
            pl.BlockSpec((128, D), whole),
            pl.BlockSpec((8, 256, 256), lambda phase, k: (0, 0, 0)),
            pl.BlockSpec((8, 256, 256), lambda phase, k: (0, 0, 0)),
            pl.BlockSpec((STEP, 256, 256), lambda phase, k: (jnp.where(phase == 0, 0, k), 0, 0)),
            pl.BlockSpec((8, STEP, 32, D), lambda phase, k: (0, jnp.where(phase == 0, 0, k), 0, 0)),
            pl.BlockSpec((8, STEP, 32, D), lambda phase, k: (0, jnp.where(phase == 0, k, 8 // STEP - 1), 1, 0)),
        ],
        out_specs=[
            pl.BlockSpec((128, D), whole),
            pl.BlockSpec(
                (STEP, 4, 2, 1, 32, D),
                lambda phase, k: (k % (4 // STEP), 0, 0, k // (4 // STEP), 1 - phase, 0),
            ),
            pl.BlockSpec((256, D), whole),
            pl.BlockSpec((256, D), whole),
            pl.BlockSpec((8, D), whole),
        ],
        out_shape=[
            jax.ShapeDtypeStruct((128, D), bf16),
            jax.ShapeDtypeStruct((4, 4, 2, 2, 64, D), bf16),
            jax.ShapeDtypeStruct((256, D), f32),
            jax.ShapeDtypeStruct((256, D), bf16),
            jax.ShapeDtypeStruct((8, D), f32),
        ],
        scratch_shapes=[
            pltpu.VMEM((256, D), bf16),
            pltpu.VMEM((8 // STEP, 256, STEP * 128), bf16),
            pltpu.VMEM((8, 256, 256), f32),
            pltpu.VMEM((4, 256, D), bf16),
        ],
        compiler_params=pltpu.CompilerParams(vmem_limit_bytes=56 * 2**20),
        name="ffn_backward",
    )(
        core,
        mine,
        theirs,
        vec,
        ffn_own,
        ffn_got,
        cot_own,
        cot_got,
        act_own,
        act_got,
        slope,
        gathered,
        gathered,
    )


def first_back_kernel(
    mine, theirs, vec, grad_own, grad_got, sums, weights, grad_resid, grad_context, low, found, total
):
    k = pl.program_id(0)

    @pl.when(k == 0)
    def _():
        partial = sums[...]
        place = lax.broadcasted_iota(jnp.int32, (8, D), 0)
        for half, resid in enumerate((mine, theirs)):
            span = slice(128 * half, 128 * (half + 1))
            cross = slice(128 * (1 - half), 128 * (2 - half))
            normed, scaled, inverse = normalize(resid[...], vec[0:1], vec[1:2])
            grad = grad_own[span] + grad_got[cross]
            partial += jnp.where(place == 0, jnp.sum(grad * scaled, axis=0, keepdims=True), 0.0)
            partial += jnp.where(place == 1, jnp.sum(grad, axis=0, keepdims=True), 0.0)
            grad = normalize_back(grad, scaled, inverse, vec[0:1])
            if half == 0:
                grad_resid[...] = grad
            low[span] = grad.astype(bf16)
        found[...] = partial
        total[...] = jnp.zeros_like(total)

    width = STEP * 128
    for part in range(8 // STEP):

        @pl.when(k == part)
        def _():
            grad = low[:128, width * part : width * (part + 1)]
            total[...] += dot_nn(grad, owner_rows(weights[...]))

    @pl.when(k == 8 // STEP - 1)
    def _():
        for group in range(8):
            grad_context[group] = total[:, 128 * group : 128 * (group + 1)].astype(bf16)


def first_backward(mine, theirs, vec, grad_own, grad_got, sums, gathered):
    whole = lambda k: (0, 0)
    return pl.pallas_call(
        first_back_kernel,
        grid=(8 // STEP,),
        in_specs=[
            pl.BlockSpec((128, D), whole),
            pl.BlockSpec((128, D), whole),
            pl.BlockSpec((4, D), whole),
            pl.BlockSpec((256, D), whole),
            pl.BlockSpec((256, D), whole),
            pl.BlockSpec((8, D), whole),
            pl.BlockSpec((8, STEP, 16, D), lambda k: (0, k, 4, 0)),
        ],
        out_specs=[
            pl.BlockSpec((128, D), whole),
            pl.BlockSpec((8, 128, 128), lambda k: (0, 0, 0)),
            pl.BlockSpec((256, D), whole),
            pl.BlockSpec((8, D), whole),
        ],
        out_shape=[
            jax.ShapeDtypeStruct((128, D), f32),
            jax.ShapeDtypeStruct((8, 128, 128), bf16),
            jax.ShapeDtypeStruct((256, D), bf16),
            jax.ShapeDtypeStruct((8, D), f32),
        ],
        scratch_shapes=[pltpu.VMEM((128, D), f32)],
        compiler_params=pltpu.CompilerParams(vmem_limit_bytes=56 * 2**20),
        name="first_backward",
    )(mine, theirs, vec, grad_own, grad_got, sums, gathered)


def attend_blocks_kernel(core, low, ctx_own, ctx_got, found, blocks):
    ctx = [jnp.concatenate([part[group] for group in range(8)], axis=1) for part in (ctx_own, ctx_got)]
    ctx = jnp.concatenate(ctx, axis=0)
    for half in range(2):
        columns = range(4 * half, 4 * (half + 1))
        own = [own_half(core, low[:, 128 * column : 128 * (column + 1)]) for column in columns]
        made = dot_tn(jnp.concatenate(own, axis=1), ctx).reshape(4, 8, 8, D)
        for place, column in enumerate(columns):
            row = found[:, 128 * column : 128 * (column + 1)]
            row = jnp.broadcast_to(row[None], (8, 8, 128))
            blocks[column] = jnp.concatenate([made[place], row], axis=-1).astype(bf16)


def make_attend_blocks(core, low, ctx_own, ctx_got, found):
    return pl.pallas_call(
        attend_blocks_kernel,
        in_specs=[pl.BlockSpec(memory_space=pltpu.SMEM)]
        + [pl.BlockSpec(memory_space=pltpu.VMEM)] * 4,
        out_specs=pl.BlockSpec(memory_space=pltpu.VMEM),
        out_shape=pltpu.HBM((8, 8, 8, D + 128), bf16),
        compiler_params=pltpu.CompilerParams(vmem_limit_bytes=32 * 2**20),
        name="attend_blocks",
    )(core, low, ctx_own, ctx_got, found)


def two_parts(value):
    upper = value.astype(bf16)
    return upper, (value - upper.astype(f32)).astype(bf16)


def swap(value):
    return lax.ppermute(value, "core", [(0, 1), (1, 0)])


def swap_chips(value):
    return lax.ppermute(value, "yl", [(0, 1), (1, 0)])


def exchange(value, axes):
    return lax.all_to_all(value, axes, 0, 0, tiled=True)


def shifted(value, axis, size, step):
    return lax.ppermute(value, axis, [(i, (i + step) % size) for i in range(size)])


def stacked(value, axis):
    size = lax.axis_size(axis)
    return jnp.stack([value] + [shifted(value, axis, size, step) for step in range(1, size)])


def places_back(axis):
    size = lax.axis_size(axis)
    return (lax.axis_index(axis) - jnp.arange(size)) % size


def pick(blocks, index):
    return blocks.at[index.reshape(-1)].get(mode="promise_in_bounds")


def spread(value, axes):
    return exchange(jnp.broadcast_to(value[None], (8,) + value.shape), axes)


def gather_projection(rows_t, table_rows, position_rows):
    first = spread(jnp.concatenate([rows_t[:, :512], table_rows], axis=0), GROUP)
    first, second = lax.optimization_barrier((first, rows_t[:, 512:]))
    second = stacked(stacked(second, "x"), "yl").reshape(8 * 24, 512)
    first = jnp.concatenate([first.reshape(256, 512), position_rows], axis=0)
    first, second = lax.optimization_barrier((stacked(first, "yl"), second))
    first = first.reshape(2, 9, 32, 512)
    table = jnp.concatenate([first[:, :8, 24:].reshape(2, 64, 512), first[:, 8]], axis=1)
    first = stacked(first[:, :8, :24], "x").reshape(8, 8, 24, 512)
    second = spread(second, GROUP).reshape(8, 8, 24, 512)
    table = stacked(table, "x").reshape(8, 96, 512)
    x, yl = places_back("x")[None], places_back("yl")[:, None]
    order = jnp.stack([(yl + 2 * x).reshape(-1), (x + 4 * yl).reshape(-1)])
    table = table.at[order[0]].get(mode="promise_in_bounds")
    return first, second, order, table[:, :64].reshape(512, 512), table[:, 64:]


def pack_kernel(core, expand, reduce, attend, vectors, got, packet):
    first = core[0] == 0
    packet[:32] = expand[...]
    inner = []
    for source in (reduce, got):
        spans = [source[:, 512 * k : 512 * (k + 1)].astype(f32) for k in range(8)]
        inner.append([jnp.where(first, span[:, :256], span[:, 256:]) for span in spans])
    for half in range(2):
        parts = [jnp.concatenate(rows_in[4 * half : 4 * half + 4], axis=1) for rows_in in inner]
        low, high = jnp.where(first, *parts), jnp.where(first, *reversed(parts))
        joined = jnp.concatenate([low, high], axis=0).astype(bf16)
        packet[32 + 16 * half : 48 + 16 * half] = joined
    own, other = attend[...].astype(f32), got[:, FF : FF + D].astype(f32)
    joined = jnp.concatenate([jnp.where(first, own, other), jnp.where(first, other, own)], axis=0)
    packet[64:80] = joined.astype(bf16)
    own, other = vectors[:4].astype(f32), got[:4, FF + D :].astype(f32)
    joined = jnp.concatenate([jnp.where(first, own, other), jnp.where(first, other, own)], axis=0)
    packet[80:] = jnp.concatenate([joined, jnp.zeros((8, D - 128), f32)], axis=1).astype(bf16)


def pack(core, expand, reduce, attend, vectors, got):
    return pl.pallas_call(
        pack_kernel,
        in_specs=[pl.BlockSpec(memory_space=pltpu.SMEM)]
        + [pl.BlockSpec(memory_space=pltpu.VMEM)] * 5,
        out_specs=pl.BlockSpec(memory_space=pltpu.VMEM),
        out_shape=jax.ShapeDtypeStruct((88, D), bf16),
        compiler_params=pltpu.CompilerParams(vmem_limit_bytes=60 * 2**20),
        name="pack",
    )(core, expand, reduce, attend, vectors, got)


def project_kernel(order, mine, theirs, first, second, packed, rows_out):
    tokens = jnp.concatenate([mine[...], theirs[...]], axis=0)
    low = first[0].astype(f32).reshape(192, 512).astype(bf16)
    high = second[:, 0].astype(f32).reshape(192, 512).astype(bf16)
    made = dot_nt(tokens[:, :512], low) + dot_nt(tokens[:, 512:], high)
    packed[0] = made.astype(bf16)
    rows_out[:, :512] = low
    rows_out[:, 512:] = high


def project(order, mine, theirs, first, second):
    return pl.pallas_call(
        project_kernel,
        grid_spec=pltpu.PrefetchScalarGridSpec(
            num_scalar_prefetch=1,
            grid=(8,),
            in_specs=[
                pl.BlockSpec((128, D), lambda k, order: (0, 0)),
                pl.BlockSpec((128, D), lambda k, order: (0, 0)),
                pl.BlockSpec((1, 8, 24, 512), lambda k, order: (order[0, k], 0, 0, 0)),
                pl.BlockSpec((8, 1, 24, 512), lambda k, order: (0, order[1, k], 0, 0)),
            ],
            out_specs=[
                pl.BlockSpec((1, 256, 192), lambda k, order: (k, 0, 0)),
                pl.BlockSpec((192, D), lambda k, order: (k, 0)),
            ],
        ),
        out_shape=[
            jax.ShapeDtypeStruct((8, 256, 192), bf16),
            pltpu.HBM((1536, D), bf16),
        ],
        compiler_params=pltpu.CompilerParams(vmem_limit_bytes=32 * 2**20),
        name="project",
    )(order, mine, theirs, first, second)


def arrange_kernel(core, mine, theirs, heads):
    for column in range(8):
        own, other = mine[column].astype(f32), theirs[column].astype(f32)
        first = core[0] == 0
        joined = jnp.concatenate(
            [jnp.where(first, own, other), jnp.where(first, other, own)], axis=1
        )
        for place in range(3):
            chunk = 3 * column + place
            heads[chunk % 8, chunk // 8] = joined[:, 128 * place : 128 * (place + 1)].astype(bf16)


def arrange(core, mine, theirs):
    return pl.pallas_call(
        arrange_kernel,
        in_specs=[
            pl.BlockSpec(memory_space=pltpu.SMEM),
            pl.BlockSpec(memory_space=pltpu.VMEM),
            pl.BlockSpec(memory_space=pltpu.VMEM),
        ],
        out_specs=pl.BlockSpec(memory_space=pltpu.VMEM),
        out_shape=jax.ShapeDtypeStruct((8, 3, 128, 128), bf16),
        compiler_params=pltpu.CompilerParams(vmem_limit_bytes=32 * 2**20),
        name="arrange",
    )(core, mine, theirs)


def project_grad_kernel(
    keep, got, keep_pair, got_pair, tokens_own, tokens_got, tokens_pair, table, blocks
):
    tokens = jnp.concatenate([tokens_own[...], tokens_got[...], tokens_pair[...]], axis=0)
    for step in range(2):
        span = slice(384 * step, 384 * (step + 1))
        parts = [part[:, span] for part in (keep, got, keep_pair, got_pair)]
        made = dot_tn(jnp.concatenate(parts, axis=0), tokens).reshape(16, 24, D)
        rest = table[128 * step : 128 * (step + 1)].reshape(16, 8, 512)
        made = jnp.concatenate([made[..., :512], made[..., 512:], rest], axis=1)
        blocks[16 * step : 16 * (step + 1)] = made.astype(bf16)


def project_grad(keep, got, keep_pair, got_pair, tokens_own, tokens_got, tokens_pair, table):
    return pl.pallas_call(
        project_grad_kernel,
        in_specs=[pl.BlockSpec(memory_space=pltpu.VMEM)] * 8,
        out_specs=pl.BlockSpec(memory_space=pltpu.VMEM),
        out_shape=jax.ShapeDtypeStruct((32, 56, 512), bf16),
        compiler_params=pltpu.CompilerParams(vmem_limit_bytes=48 * 2**20),
        name="project_grad",
    )(keep, got, keep_pair, got_pair, tokens_own, tokens_got, tokens_pair, table)


def ring_scatter(blocks, axis, size, dtype=f32):
    place = lax.axis_index(axis)
    total = lax.dynamic_index_in_dim(blocks, place, 0, keepdims=False).astype(f32)
    for step in range(1, size):
        sent = lax.dynamic_index_in_dim(blocks, (place + step) % size, 0, keepdims=False)
        total = total + shifted(sent, axis, size, step).astype(f32)
    return total.astype(dtype)


def y_scatter(blocks):
    place = 2 * lax.axis_index("yh") + lax.axis_index("yl")
    total = lax.dynamic_index_in_dim(blocks, place, 0, keepdims=False).astype(f32)

    def on_mesh(y):
        return 2 * (y % 2) + y // 2

    for step in range(1, 4):
        sent = lax.dynamic_index_in_dim(blocks, (place + step) % 4, 0, keepdims=False)
        ring = [(on_mesh(y), on_mesh((y + step) % 4)) for y in range(4)]
        total = total + lax.ppermute(sent, ("yl", "yh"), ring).astype(f32)
    return total


def split_kernel(core, heads, keep, give):
    for column in range(8):
        chunks = [3 * column + place for place in range(3)]
        joined = jnp.concatenate(
            [heads[chunk % 8, chunk // 8].astype(f32) for chunk in chunks], axis=1
        )
        first = core[0] == 0
        zero, one = joined[:, :192], joined[:, 192:]
        span = slice(192 * column, 192 * (column + 1))
        keep[:, span] = jnp.where(first, zero, one).astype(bf16)
        give[:, span] = jnp.where(first, one, zero).astype(bf16)


def split(core, heads):
    return pl.pallas_call(
        split_kernel,
        in_specs=[
            pl.BlockSpec(memory_space=pltpu.SMEM),
            pl.BlockSpec(memory_space=pltpu.VMEM),
        ],
        out_specs=[pl.BlockSpec(memory_space=pltpu.VMEM)] * 2,
        out_shape=[jax.ShapeDtypeStruct((128, 1536), bf16)] * 2,
        compiler_params=pltpu.CompilerParams(vmem_limit_bytes=32 * 2**20),
        name="split",
    )(core, heads)


def per_device(
    tokens,
    w_project,
    w_attend,
    first_gain,
    first_shift,
    w_expand,
    w_reduce,
    second_gain,
    second_shift,
    position_table,
    w_query,
    w_key,
    lengths,
    cotangent,
):
    core = lax.axis_index("core")
    group = lax.axis_index(GROUP)
    local = tokens.shape[0]
    core_id = core.reshape(1)
    pair = 2 * local
    column_bucket = bucket_values(SEQ - 1 - np.arange(2 * SEQ - 1), SPAN)
    fold = np.append(column_bucket, -1)[None, :] == np.arange(2 * SPAN)[:, None]
    fold = jnp.asarray(fold.astype(np.float32)).astype(bf16)

    def by_core(zero, one):
        return jnp.where(core == 0, zero, one)

    def in_order(mine, theirs):
        return by_core(mine, theirs), by_core(theirs, mine)

    cotangent_got = swap(cotangent)
    tokens_got = swap(tokens)
    weights_own = jnp.concatenate([w_key, w_query], axis=1)
    first, second, order, table_t, position_rows = gather_projection(
        w_project.T,
        position_table.T,
        jnp.concatenate([weights_own[:32], weights_own[32:]], axis=1),
    )
    position_weights = jnp.stack([position_rows[..., :256], position_rows[..., 256:]], axis=1)
    position_weights = position_weights.reshape(512, 256)

    vectors = jnp.stack([first_gain, first_shift, second_gain, second_shift])
    vectors = jnp.pad(vectors, ((0, 4), (0, 128 - 8)))
    reduce_rows = w_reduce.T
    got = swap(jnp.concatenate([reduce_rows, w_attend.T, vectors], axis=1))
    packet = pack(core_id, w_expand.T, reduce_rows, w_attend.T, vectors, got)
    gathered = lax.all_gather(packet, CHIPS, axis=0, tiled=False).reshape(8, 8, 88, D)
    vec = gathered[..., 80:, :8].reshape(8, 8, 2, 4, 8).transpose(3, 1, 2, 0, 4)
    vec = vec.reshape(4, D).astype(f32)
    gain_one, shift_one, gain_two, shift_two = vec[0], vec[1], vec[2], vec[3]

    packed, project_t = project(order, tokens, tokens_got, first, second)
    heads_in = exchange(arrange(core_id, packed[:, :local], swap(packed[:, local:])), GROUP)
    rel = dot_tn(table_t, position_weights)
    rel = dot_tn(fold, (rel + swap(rel)).astype(bf16)).astype(bf16)
    heads_in, tokens_both = lax.optimization_barrier(
        (heads_in, jnp.concatenate([tokens, tokens_got], axis=0))
    )
    tokens_pair = swap_chips(tokens_both)
    context, kept = attend(lengths, heads_in, rel)
    context, tokens_pair = lax.optimization_barrier(
        (exchange(context, GROUP), tokens_pair)
    )
    context_got = swap(context)

    resid_own = project_back(context, tokens, gathered)
    resid_got = swap(resid_own)
    activ, slope, ffn_own, ffn_sent = ffn_forward(resid_own, resid_got, vec, gathered)
    output, blocks, grad_own, grad_sent, sums = ffn_backward(
        core_id,
        resid_own,
        resid_got,
        vec,
        ffn_own,
        swap(ffn_sent),
        cotangent,
        cotangent_got,
        activ,
        swap(activ),
        slope,
        gathered,
    )
    grad_resid1, grad_context, grad_attended, sums = first_backward(
        resid_own, resid_got, vec, grad_own, swap(grad_sent), sums, gathered
    )
    attend_blocks = make_attend_blocks(core_id, grad_attended, context, context_got, sums)

    summed = lax.psum_scatter(
        blocks.reshape(16, 4 * 64, D), ("x", "z"), scatter_dimension=0, tiled=True
    )
    attend_blocks, grad_ctx = lax.optimization_barrier(
        (attend_blocks, exchange(grad_context, GROUP))
    )
    attend_sum = exchange(attend_blocks.reshape(64, 8, D + 128), COLUMN + GROUP)

    grads, rel_grad = attend_back(heads_in, rel, grad_ctx, kept)
    grads, attend_sum = lax.optimization_barrier((grads, attend_sum))
    attend_sum = jnp.sum(attend_sum.astype(f32), axis=0)
    grad_attend = attend_sum[:, :D].T
    vectors = attend_sum[:4, D:].reshape(4, 16, 8)
    vectors = lax.dynamic_index_in_dim(vectors, 8 * core + group, axis=1, keepdims=False)
    grads = exchange(grads, GROUP)
    yl = lax.axis_index("yl")
    rel_grad = sum(dot_nn(fold, part) for part in two_parts(rel_grad))
    rel_grad = rel_grad + swap(rel_grad)
    rel_grad = two_parts(rel_grad + swap_chips(rel_grad.astype(bf16)).astype(f32))
    table_half = lax.dynamic_slice_in_dim(table_t, 256 * yl, 256, axis=0)
    weights_half = lax.dynamic_slice_in_dim(position_weights, 256 * yl, 256, axis=0)
    position_grads = sum(dot_nn(table_half, part) for part in rel_grad)
    position_grads = ring_scatter(position_grads.reshape(4, 64, 256), "x", 4)
    table_blocks = sum(dot_nt(weights_half, part) for part in rel_grad)

    def by_chip(value):
        low, high = value[:, :768], value[:, 768:]
        return jnp.where(yl == 0, low, high), jnp.where(yl == 0, high, low)

    grads, position_grads = lax.optimization_barrier((grads, position_grads))
    keep, give = split(core_id, grads)
    keep_half, keep_other = by_chip(keep)
    got = swap(give)
    got_half, got_other = by_chip(got)
    blocks = project_grad(
        keep_half,
        got_half,
        swap_chips(keep_other),
        swap_chips(got_other),
        tokens,
        tokens_got,
        tokens_pair,
        table_blocks,
    )
    blocks, got = lax.optimization_barrier((blocks, got))
    tokens_part = dot_nn(keep, project_t)
    tokens_sent = dot_nn(got, project_t).astype(bf16)
    tokens_sent, summed = lax.optimization_barrier((tokens_sent, summed))
    received, summed, tokens_back = lax.optimization_barrier(
        (
            exchange(blocks, ("x",) + GROUP),
            y_scatter(summed.reshape(4, 64, D)),
            swap(tokens_sent),
        )
    )
    grad_expand = summed[:32].T
    grad_reduce = summed[32:64].reshape(4, 8, D).transpose(1, 0, 2).reshape(8, FF).T
    received = jnp.sum(received.astype(f32), axis=0)
    grad_project = jnp.concatenate([received[:24], received[24:48]], axis=1).T
    grad_table = received[48:].T
    tokens_grad = grad_resid1 + (tokens_part + tokens_back)
    grad_key, grad_query = position_grads[:, :128], position_grads[:, 128:]

    return (
        output,
        tokens_grad.astype(bf16),
        grad_project,
        grad_attend,
        vectors[0],
        vectors[1],
        grad_expand,
        grad_reduce,
        vectors[2],
        vectors[3],
        grad_table,
        grad_query,
        grad_key,
    )


def solution(mesh):
    parts = Mesh(mesh.devices.reshape(2, 4, 2, 4, 2), EVERY)
    in_specs = (
        P(EVERY, None),
        P(None, EVERY),
        P(None, EVERY),
        P(EVERY),
        P(EVERY),
        P(None, EVERY),
        P(None, EVERY),
        P(EVERY),
        P(EVERY),
        P(None, EVERY),
        P(DP, GROUP),
        P(DP, GROUP),
        P(DP),
        P(EVERY, None),
    )
    out_specs = (
        P(EVERY, None),
        P(EVERY, None),
        P(None, EVERY),
        P(None, EVERY),
        P(EVERY),
        P(EVERY),
        P(None, EVERY),
        P(None, EVERY),
        P(EVERY),
        P(EVERY),
        P(None, EVERY),
        P(DP, GROUP),
        P(DP, GROUP),
    )
    return jax.shard_map(
        per_device, mesh=parts, in_specs=in_specs, out_specs=out_specs, check_vma=False
    )
```

```python
import math

import jax
import jax.numpy as jnp
import numpy as np
from jax import lax
from jax.experimental import pallas as pl
from jax.experimental.pallas import tpu as pltpu
from jax.sharding import Mesh
from jax.sharding import PartitionSpec as P

D = 1024
HEADS = 16
HEAD_DIM = 64
FF = 4096
SPAN = 256
SEQ = 512
BLOCK = 128
WINDOW = SEQ + BLOCK
STEP = 4

EPS = 1e-07
MASKED = -1e30

DP = ("yl", "x", "core")
GROUP = ("z", "yh")
COLUMN = ("yl", "x")
EVERY = DP + GROUP
CHIPS = ("z", "yh", "yl", "x")
DEVICES = ("core",) + CHIPS
bf16 = jnp.bfloat16
f32 = jnp.float32


def bucket_values(offset, span):
    middle = span // 2
    absolute = np.where((offset < middle) & (offset > -middle), middle - 1, np.abs(offset))
    log_place = (
        np.ceil(np.log(absolute / middle) / np.log((2 * span - 1) / middle) * (middle - 1)) + middle
    )
    buckets = np.where(absolute <= middle, offset, log_place * np.sign(offset)).astype(np.int64)
    return np.clip(buckets + span, 0, 2 * span - 1).astype(np.int32)


def normalize(value, gain, shift):
    center = value - jnp.mean(value, axis=-1, keepdims=True)
    inverse = lax.rsqrt(jnp.mean(center * center, axis=-1, keepdims=True) + EPS)
    scaled = center * inverse
    return (scaled * gain + shift, scaled, inverse)


def normalize_back(incoming, scaled, inverse, gain):
    grad_scaled = incoming * gain
    middle = (
        grad_scaled
        - jnp.mean(grad_scaled, axis=-1, keepdims=True)
        - scaled * jnp.mean(grad_scaled * scaled, axis=-1, keepdims=True)
    )
    return inverse * middle


def dot_nn(left, right):
    return lax.dot_general(left, right, (((1,), (0,)), ((), ())), preferred_element_type=f32)


def dot_nt(left, right):
    return lax.dot_general(left, right, (((1,), (1,)), ((), ())), preferred_element_type=f32)


def dot_tn(left, right):
    return lax.dot_general(left, right, (((0,), (0,)), ((), ())), preferred_element_type=f32)


def window(block):
    start = SEQ - BLOCK - BLOCK * block
    return slice(start, start + WINDOW)


def rows(block):
    return slice(BLOCK * block, BLOCK * (block + 1))


def skew(values):
    return pltpu.roll(values, SEQ + 1, 1, stride=1, stride_axis=0)[:, :SEQ]


def unskew(values):
    wide = jnp.concatenate([values, jnp.zeros((BLOCK, BLOCK), f32)], axis=1)
    return pltpu.roll(wide, 0, 1, stride=1, stride_axis=0)


def turn(mirror, values):
    upper = values.astype(bf16)
    return dot_nn(mirror, upper) + dot_nn(mirror, (values - upper.astype(f32)).astype(bf16))


def one_head(value, head):
    lane = lax.broadcasted_iota(jnp.int32, value.shape, 1)
    return jnp.where(lane // HEAD_DIM == head, value, jnp.zeros_like(value))


def query_bias(key, rel_queries, bias):
    for block in range(SEQ // BLOCK):
        by_offset = dot_nt(key[rows(block)], rel_queries[window(block)])
        bias[:, rows(block)] = skew(by_offset).T


def probabilities(query, key, rel_keys, bias, block, length):
    part = query[rows(block)]
    logits = dot_nt(part, key) + skew(dot_nt(part, rel_keys[window(block)])) + bias[rows(block)]
    logits = logits * (1.0 / math.sqrt(3 * HEAD_DIM))
    column = lax.broadcasted_iota(jnp.int32, logits.shape, 1)
    logits = jnp.where(column < length, logits, MASKED)
    exponent = jnp.exp(logits - jnp.max(logits, axis=1, keepdims=True))
    return exponent * (1.0 / jnp.sum(exponent, axis=1, keepdims=True))


def attend_kernel(lengths, heads_in, rel, context, kept, bias):
    length = lengths[pl.program_id(0)]
    query, key, values = (heads_in[:, part].reshape(SEQ, 128) for part in range(3))
    rel_keys, rel_queries = rel[:, :128], rel[:, 128:]
    total = [jnp.zeros((BLOCK, 128), f32) for _ in range(SEQ // BLOCK)]
    for head in range(2):
        query_h, key_h, values_h = (one_head(part, head) for part in (query, key, values))
        query_bias(key_h, rel_queries, bias)
        for block in range(SEQ // BLOCK):
            probs = probabilities(query_h, key, rel_keys, bias, block, length)
            kept[0, head, rows(block)] = probs
            total[block] = total[block] + dot_nn(probs.astype(bf16), values_h)
    for block in range(SEQ // BLOCK):
        context[block] = total[block].astype(bf16)


def attend_back_kernel(
    heads_in, rel, grad_context, kept, grads, grad_rel, probs_ref, grad_ref
):
    query, key, values = (heads_in[:, part].reshape(SEQ, 128) for part in range(3))
    grad_ctx = grad_context[...].reshape(SEQ, 128)
    rel_keys, rel_queries = rel[:, :128], rel[:, 128:]
    blocks = SEQ // BLOCK
    first = lax.broadcasted_iota(jnp.int32, (BLOCK, BLOCK), 0)
    second = lax.broadcasted_iota(jnp.int32, (BLOCK, BLOCK), 1)
    mirror = jnp.where(first + second == BLOCK - 1, 1.0, 0.0).astype(bf16)

    @pl.when(pl.program_id(0) == 0)
    def _():
        grad_rel[...] = jnp.zeros_like(grad_rel)

    queries, keys, ctxs = (
        [one_head(part, head) for head in range(2)] for part in (query, key, grad_ctx)
    )
    rel_keys_of = [one_head(rel_keys, head) for head in range(2)]
    rel_queries_of = [one_head(rel_queries, head) for head in range(2)]
    for block in range(blocks):
        grad_q, turned, rel_part = 0.0, 0.0, 0.0
        for head in range(2):
            probs = kept[0, head, rows(block)]
            probs_ref[head, rows(block)] = probs.astype(bf16)
            grad_probs = dot_nt(ctxs[head][rows(block)], values)
            inner = jnp.sum(probs * grad_probs, axis=1, keepdims=True)
            grad = (probs * (grad_probs - inner) * (1.0 / math.sqrt(3 * HEAD_DIM))).astype(bf16)
            grad_ref[head, rows(block)] = grad
            by_offset = unskew(dot_nn(mirror, grad)).astype(bf16)
            grad_q = grad_q + dot_nn(grad, keys[head])
            turned = turned + dot_nn(by_offset, rel_keys_of[head][window(block)])
            mirrored = dot_nn(mirror, queries[head][rows(block)]).astype(bf16)
            rel_part = rel_part + dot_tn(by_offset, mirrored)
        grad_rel[window(block), :128] += rel_part
        grads[block, 0] = (grad_q + turn(mirror, turned)).astype(bf16)
    for block in range(blocks):
        grad_k, grad_v, turned, rel_part = 0.0, 0.0, 0.0, 0.0
        for head in range(2):
            grad = grad_ref[head, :, rows(block)]
            by_offset = unskew(dot_nt(mirror, grad)).astype(bf16)
            grad_k = grad_k + dot_tn(grad, queries[head])
            turned = turned + dot_nn(by_offset, rel_queries_of[head][window(block)])
            grad_v = grad_v + dot_tn(probs_ref[head, :, rows(block)], ctxs[head])
            mirrored = dot_nn(mirror, keys[head][rows(block)]).astype(bf16)
            rel_part = rel_part + dot_tn(by_offset, mirrored)
        grad_rel[window(block), 128:] += rel_part
        grads[block, 1] = (grad_k + turn(mirror, turned)).astype(bf16)
        grads[block, 2] = grad_v.astype(bf16)


def attend(lengths, heads_in, rel):
    return pl.pallas_call(
        attend_kernel,
        grid=(2,),
        in_specs=[
            pl.BlockSpec(memory_space=pltpu.SMEM),
            pl.BlockSpec((4, 3, 128, 128), lambda row: (row, 0, 0, 0)),
            pl.BlockSpec((2 * SEQ, 256), lambda row: (0, 0)),
        ],
        out_specs=[
            pl.BlockSpec((4, 128, 128), lambda row: (row, 0, 0)),
            pl.BlockSpec((1, 2, SEQ, SEQ), lambda row: (row, 0, 0, 0)),
        ],
        out_shape=[
            jax.ShapeDtypeStruct((8, 128, 128), bf16),
            pltpu.HBM((2, 2, SEQ, SEQ), f32),
        ],
        scratch_shapes=[pltpu.VMEM((SEQ, SEQ), f32)],
        compiler_params=pltpu.CompilerParams(vmem_limit_bytes=48 * 2**20),
        name="attend",
    )(lengths, heads_in, rel)


def attend_back(heads_in, rel, grad_context, kept):
    return pl.pallas_call(
        attend_back_kernel,
        grid=(2,),
        in_specs=[
            pl.BlockSpec((4, 3, 128, 128), lambda row: (row, 0, 0, 0)),
            pl.BlockSpec((2 * SEQ, 256), lambda row: (0, 0)),
            pl.BlockSpec((4, 128, 128), lambda row: (row, 0, 0)),
            pl.BlockSpec((1, 2, SEQ, SEQ), lambda row: (row, 0, 0, 0)),
        ],
        out_specs=[
            pl.BlockSpec((4, 3, 128, 128), lambda row: (row, 0, 0, 0)),
            pl.BlockSpec((2 * SEQ, 256), lambda row: (0, 0)),
        ],
        out_shape=[
            jax.ShapeDtypeStruct((8, 3, 128, 128), bf16),
            jax.ShapeDtypeStruct((2 * SEQ, 256), f32),
        ],
        scratch_shapes=[
            pltpu.VMEM((2, SEQ, SEQ), bf16),
            pltpu.VMEM((2, SEQ, SEQ), bf16),
        ],
        compiler_params=pltpu.CompilerParams(vmem_limit_bytes=48 * 2**20),
        cost_estimate=pl.CostEstimate(
            flops=20 * 10**9, bytes_accessed=8 * 2**20, transcendentals=2**20
        ),
        name="attend_back",
    )(heads_in, rel, grad_context, kept)


def owner_rows(block):
    wide = block.astype(f32).reshape(8, STEP, 2, 8, block.shape[-1])
    return wide.transpose(1, 2, 0, 3, 4).reshape(STEP * 128, block.shape[-1]).astype(bf16)


def project_back_kernel(context, tokens, weights, resid):
    rows_in = jnp.concatenate([context[group] for group in range(8)], axis=1)
    resid[...] = tokens[...].astype(f32) + dot_nt(rows_in, owner_rows(weights[...]))


def project_back(context, tokens, gathered):
    return pl.pallas_call(
        project_back_kernel,
        grid=(8 // STEP,),
        in_specs=[
            pl.BlockSpec((8, 128, 128), lambda k: (0, 0, 0)),
            pl.BlockSpec((128, STEP * 128), lambda k: (0, k)),
            pl.BlockSpec((8, STEP, 16, D), lambda k: (0, k, 4, 0)),
        ],
        out_specs=pl.BlockSpec((128, STEP * 128), lambda k: (0, k)),
        out_shape=jax.ShapeDtypeStruct((128, D), f32),
        compiler_params=pltpu.CompilerParams(vmem_limit_bytes=48 * 2**20),
        name="project_back",
    )(context, tokens, gathered)


def ffn_kernel(mine, theirs, vec, expand, reduce, act, slope, partial, sent, low):
    phase, k = pl.program_id(0), pl.program_id(1)

    @pl.when((phase == 0) & (k == 0))
    def _():
        for half, resid in enumerate((mine, theirs)):
            first_norm, scaled, inverse = normalize(resid[...], vec[0:1], vec[1:2])
            low[128 * half : 128 * (half + 1)] = first_norm.astype(bf16)

    @pl.when(phase == 0)
    def _():
        for column in range(STEP):
            inner = dot_nt(low[...], expand[:, column].reshape(256, D))
            spread_in = 0.5 + 0.5 * lax.erf(inner * math.sqrt(0.5))
            act[STEP * k + column] = (inner * spread_in).astype(bf16)
            density = jnp.exp(-0.5 * inner * inner) * (1.0 / math.sqrt(2.0 * math.pi))
            slope[column] = spread_in + inner * density

    @pl.when(phase == 1)
    def _():
        total = jnp.zeros((256, STEP * 128), f32)
        for half in range(2):
            rows_in = jnp.concatenate([act[4 * half + part] for part in range(4)], axis=1)
            weights = owner_rows(reduce[:, :, 16 * half : 16 * (half + 1)])
            total = total + dot_nt(rows_in, weights)
        partial[...] = total
        sent[...] = total.astype(bf16)


def ffn_forward(mine, theirs, vec, gathered):
    whole = lambda phase, k: (0, 0)
    return pl.pallas_call(
        ffn_kernel,
        grid=(2, 8 // STEP),
        in_specs=[
            pl.BlockSpec((128, D), whole),
            pl.BlockSpec((128, D), whole),
            pl.BlockSpec((4, D), whole),
            pl.BlockSpec((8, STEP, 32, D), lambda phase, k: (0, jnp.where(phase == 0, k, 8 // STEP - 1), 0, 0)),
            pl.BlockSpec((8, STEP, 32, D), lambda phase, k: (0, jnp.where(phase == 0, 0, k), 1, 0)),
        ],
        out_specs=[
            pl.BlockSpec((8, 256, 256), lambda phase, k: (0, 0, 0)),
            pl.BlockSpec((STEP, 256, 256), lambda phase, k: (jnp.where(phase == 0, k, 8 // STEP - 1), 0, 0)),
            pl.BlockSpec((256, STEP * 128), lambda phase, k: (0, jnp.where(phase == 0, 0, k))),
            pl.BlockSpec((256, STEP * 128), lambda phase, k: (0, jnp.where(phase == 0, 0, k))),
        ],
        out_shape=[
            jax.ShapeDtypeStruct((8, 256, 256), bf16),
            pltpu.HBM((8, 256, 256), f32),
            pltpu.HBM((256, D), f32),
            jax.ShapeDtypeStruct((256, D), bf16),
        ],
        scratch_shapes=[pltpu.VMEM((256, D), bf16)],
        compiler_params=pltpu.CompilerParams(vmem_limit_bytes=48 * 2**20),
        name="ffn_forward",
    )(mine, theirs, vec, gathered, gathered)


def own_half(core, wide):
    return jnp.where(core[0] == 0, wide[:, :64], wide[:, 64:])


def ffn_back_kernel(
    core,
    mine,
    theirs,
    vec,
    ffn_own,
    ffn_got,
    cot_own,
    cot_got,
    act_own,
    act_got,
    slope,
    expand,
    reduce,
    output,
    blocks,
    partial,
    sent,
    sums,
    low,
    grad_ffn,
    grad_act,
    act,
):
    phase, k = pl.program_id(0), pl.program_id(1)

    @pl.when((phase == 0) & (k == 0))
    def _():
        sums[...] = jnp.zeros_like(sums)
        for half, (resid, cot) in enumerate(((mine, cot_own), (theirs, cot_got))):
            span = slice(128 * half, 128 * (half + 1))
            cross = slice(128 * (1 - half), 128 * (2 - half))
            first_norm, scaled, inverse = normalize(resid[...], vec[0:1], vec[1:2])
            low[span] = first_norm.astype(bf16)
            resid2 = first_norm + (ffn_own[span] + ffn_got[cross])
            normed, scaled, inverse = normalize(resid2, vec[2:3], vec[3:4])
            grad = cot[...].astype(f32)
            if half == 0:
                output[...] = normed.astype(bf16)
            sums[2:3] += jnp.sum(grad * scaled, axis=0, keepdims=True)
            sums[3:4] += jnp.sum(grad, axis=0, keepdims=True)
            grad = normalize_back(grad, scaled, inverse, vec[2:3])
            partial[span] = 0.5 * grad
            grad = grad.astype(bf16)
            for chunk in range(8 // STEP):
                grad_ffn[chunk, span] = grad[:, STEP * 128 * chunk : STEP * 128 * (chunk + 1)]
        grad_act[...] = jnp.zeros_like(grad_act)
        for chunk in range(8):
            own, got = act_own[chunk], act_got[chunk]
            got = jnp.concatenate([got[128:], got[:128]], axis=0)
            start = 512 * (chunk % 2)
            act[chunk // 2, :, start : start + 256] = jnp.where(core[0] == 0, own, got)
            act[chunk // 2, :, start + 256 : start + 512] = jnp.where(core[0] == 0, got, own)

    @pl.when(phase == 0)
    def _():
        grad = grad_ffn[k]
        own = [own_half(core, grad[:, 128 * column : 128 * (column + 1)]) for column in range(STEP)]
        own = jnp.concatenate(own, axis=1)
        for half in range(2):
            weights = owner_rows(reduce[:, :, 16 * half : 16 * (half + 1)])
            for part in range(4):
                grad_act[4 * half + part] += dot_nn(grad, weights[:, 256 * part : 256 * (part + 1)])
            made = [dot_tn(own, act[2 * half + part]).reshape(STEP, 8, 8, D) for part in range(2)]
            made = jnp.concatenate(made, axis=2).astype(bf16).reshape(STEP, 4, 2, 16, D)
            blocks[:, :, :, 0, 16 * half : 16 * (half + 1)] = made

    @pl.when(phase == 1)
    def _():
        for column in range(STEP):
            weights = expand[:, column].reshape(256, D)
            grad = (slope[column] * grad_act[STEP * k + column]).astype(bf16)
            made = dot_tn(grad, low[...]).astype(bf16)
            blocks[column, :, :, 0] = made.reshape(4, 2, 32, D)
            partial[...] += dot_nn(grad, weights)

    @pl.when((phase == 1) & (k == 8 // STEP - 1))
    def _():
        sent[...] = partial[...].astype(bf16)


def ffn_backward(
    core, mine, theirs, vec, ffn_own, ffn_got, cot_own, cot_got, act_own, act_got, slope, gathered
):
    whole = lambda phase, k: (0, 0)
    return pl.pallas_call(
        ffn_back_kernel,
        grid=(2, 8 // STEP),
        in_specs=[
            pl.BlockSpec(memory_space=pltpu.SMEM),
            pl.BlockSpec((128, D), whole),
            pl.BlockSpec((128, D), whole),
            pl.BlockSpec((4, D), whole),
            pl.BlockSpec((256, D), whole),
            pl.BlockSpec((256, D), whole),
            pl.BlockSpec((128, D), whole),
            pl.BlockSpec((128, D), whole),
            pl.BlockSpec((8, 256, 256), lambda phase, k: (0, 0, 0)),
            pl.BlockSpec((8, 256, 256), lambda phase, k: (0, 0, 0)),
            pl.BlockSpec((STEP, 256, 256), lambda phase, k: (jnp.where(phase == 0, 0, k), 0, 0)),
            pl.BlockSpec((8, STEP, 32, D), lambda phase, k: (0, jnp.where(phase == 0, 0, k), 0, 0)),
            pl.BlockSpec((8, STEP, 32, D), lambda phase, k: (0, jnp.where(phase == 0, k, 8 // STEP - 1), 1, 0)),
        ],
        out_specs=[
            pl.BlockSpec((128, D), whole),
            pl.BlockSpec(
                (STEP, 4, 2, 1, 32, D),
                lambda phase, k: (k % (4 // STEP), 0, 0, k // (4 // STEP), 1 - phase, 0),
            ),
            pl.BlockSpec((256, D), whole),
            pl.BlockSpec((256, D), whole),
            pl.BlockSpec((8, D), whole),
        ],
        out_shape=[
            jax.ShapeDtypeStruct((128, D), bf16),
            jax.ShapeDtypeStruct((4, 4, 2, 2, 64, D), bf16),
            jax.ShapeDtypeStruct((256, D), f32),
            jax.ShapeDtypeStruct((256, D), bf16),
            jax.ShapeDtypeStruct((8, D), f32),
        ],
        scratch_shapes=[
            pltpu.VMEM((256, D), bf16),
            pltpu.VMEM((8 // STEP, 256, STEP * 128), bf16),
            pltpu.VMEM((8, 256, 256), f32),
            pltpu.VMEM((4, 256, D), bf16),
        ],
        compiler_params=pltpu.CompilerParams(vmem_limit_bytes=56 * 2**20),
        name="ffn_backward",
    )(
        core,
        mine,
        theirs,
        vec,
        ffn_own,
        ffn_got,
        cot_own,
        cot_got,
        act_own,
        act_got,
        slope,
        gathered,
        gathered,
    )


def first_back_kernel(
    mine, theirs, vec, grad_own, grad_got, sums, weights, grad_resid, grad_context, low, found, total
):
    k = pl.program_id(0)

    @pl.when(k == 0)
    def _():
        partial = sums[...]
        place = lax.broadcasted_iota(jnp.int32, (8, D), 0)
        for half, resid in enumerate((mine, theirs)):
            span = slice(128 * half, 128 * (half + 1))
            cross = slice(128 * (1 - half), 128 * (2 - half))
            normed, scaled, inverse = normalize(resid[...], vec[0:1], vec[1:2])
            grad = grad_own[span] + grad_got[cross]
            partial += jnp.where(place == 0, jnp.sum(grad * scaled, axis=0, keepdims=True), 0.0)
            partial += jnp.where(place == 1, jnp.sum(grad, axis=0, keepdims=True), 0.0)
            grad = normalize_back(grad, scaled, inverse, vec[0:1])
            if half == 0:
                grad_resid[...] = grad
            low[span] = grad.astype(bf16)
        found[...] = partial
        total[...] = jnp.zeros_like(total)

    width = STEP * 128
    for part in range(8 // STEP):

        @pl.when(k == part)
        def _():
            grad = low[:128, width * part : width * (part + 1)]
            total[...] += dot_nn(grad, owner_rows(weights[...]))

    @pl.when(k == 8 // STEP - 1)
    def _():
        for group in range(8):
            grad_context[group] = total[:, 128 * group : 128 * (group + 1)].astype(bf16)


def first_backward(mine, theirs, vec, grad_own, grad_got, sums, gathered):
    whole = lambda k: (0, 0)
    return pl.pallas_call(
        first_back_kernel,
        grid=(8 // STEP,),
        in_specs=[
            pl.BlockSpec((128, D), whole),
            pl.BlockSpec((128, D), whole),
            pl.BlockSpec((4, D), whole),
            pl.BlockSpec((256, D), whole),
            pl.BlockSpec((256, D), whole),
            pl.BlockSpec((8, D), whole),
            pl.BlockSpec((8, STEP, 16, D), lambda k: (0, k, 4, 0)),
        ],
        out_specs=[
            pl.BlockSpec((128, D), whole),
            pl.BlockSpec((8, 128, 128), lambda k: (0, 0, 0)),
            pl.BlockSpec((256, D), whole),
            pl.BlockSpec((8, D), whole),
        ],
        out_shape=[
            jax.ShapeDtypeStruct((128, D), f32),
            jax.ShapeDtypeStruct((8, 128, 128), bf16),
            jax.ShapeDtypeStruct((256, D), bf16),
            jax.ShapeDtypeStruct((8, D), f32),
        ],
        scratch_shapes=[pltpu.VMEM((128, D), f32)],
        compiler_params=pltpu.CompilerParams(vmem_limit_bytes=56 * 2**20),
        name="first_backward",
    )(mine, theirs, vec, grad_own, grad_got, sums, gathered)


def attend_blocks_kernel(core, low, ctx_own, ctx_got, found, blocks):
    ctx = [jnp.concatenate([part[group] for group in range(8)], axis=1) for part in (ctx_own, ctx_got)]
    ctx = jnp.concatenate(ctx, axis=0)
    for half in range(2):
        columns = range(4 * half, 4 * (half + 1))
        own = [own_half(core, low[:, 128 * column : 128 * (column + 1)]) for column in columns]
        made = dot_tn(jnp.concatenate(own, axis=1), ctx).reshape(4, 8, 8, D)
        for place, column in enumerate(columns):
            row = found[:, 128 * column : 128 * (column + 1)]
            row = jnp.broadcast_to(row[None], (8, 8, 128))
            blocks[column] = jnp.concatenate([made[place], row], axis=-1).astype(bf16)


def make_attend_blocks(core, low, ctx_own, ctx_got, found):
    return pl.pallas_call(
        attend_blocks_kernel,
        in_specs=[pl.BlockSpec(memory_space=pltpu.SMEM)]
        + [pl.BlockSpec(memory_space=pltpu.VMEM)] * 4,
        out_specs=pl.BlockSpec(memory_space=pltpu.VMEM),
        out_shape=pltpu.HBM((8, 8, 8, D + 128), bf16),
        compiler_params=pltpu.CompilerParams(vmem_limit_bytes=32 * 2**20),
        name="attend_blocks",
    )(core, low, ctx_own, ctx_got, found)


def two_parts(value):
    upper = value.astype(bf16)
    return upper, (value - upper.astype(f32)).astype(bf16)


def swap(value):
    return lax.ppermute(value, "core", [(0, 1), (1, 0)])


def swap_chips(value):
    return lax.ppermute(value, "yl", [(0, 1), (1, 0)])


def exchange(value, axes):
    return lax.all_to_all(value, axes, 0, 0, tiled=True)


def shifted(value, axis, size, step):
    return lax.ppermute(value, axis, [(i, (i + step) % size) for i in range(size)])


def stacked(value, axis):
    size = lax.axis_size(axis)
    return jnp.stack([value] + [shifted(value, axis, size, step) for step in range(1, size)])


def places_back(axis):
    size = lax.axis_size(axis)
    return (lax.axis_index(axis) - jnp.arange(size)) % size


def pick(blocks, index):
    return blocks.at[index.reshape(-1)].get(mode="promise_in_bounds")


def spread(value, axes):
    return exchange(jnp.broadcast_to(value[None], (8,) + value.shape), axes)


def gather_projection(rows_t, table_rows, position_rows):
    first = spread(jnp.concatenate([rows_t[:, :512], table_rows], axis=0), GROUP)
    first, second = lax.optimization_barrier((first, rows_t[:, 512:]))
    second = stacked(stacked(second, "x"), "yl").reshape(8 * 24, 512)
    first = jnp.concatenate([first.reshape(256, 512), position_rows], axis=0)
    first, second = lax.optimization_barrier((stacked(first, "yl"), second))
    first = first.reshape(2, 9, 32, 512)
    table = jnp.concatenate([first[:, :8, 24:].reshape(2, 64, 512), first[:, 8]], axis=1)
    first = stacked(first[:, :8, :24], "x").reshape(8, 8, 24, 512)
    second = spread(second, GROUP).reshape(8, 8, 24, 512)
    table = stacked(table, "x").reshape(8, 96, 512)
    x, yl = places_back("x")[None], places_back("yl")[:, None]
    order = jnp.stack([(yl + 2 * x).reshape(-1), (x + 4 * yl).reshape(-1)])
    table = table.at[order[0]].get(mode="promise_in_bounds")
    return first, second, order, table[:, :64].reshape(512, 512), table[:, 64:]


def pack_kernel(core, expand, reduce, attend, vectors, got, packet):
    first = core[0] == 0
    packet[:32] = expand[...]
    inner = []
    for source in (reduce, got):
        spans = [source[:, 512 * k : 512 * (k + 1)].astype(f32) for k in range(8)]
        inner.append([jnp.where(first, span[:, :256], span[:, 256:]) for span in spans])
    for half in range(2):
        parts = [jnp.concatenate(rows_in[4 * half : 4 * half + 4], axis=1) for rows_in in inner]
        low, high = jnp.where(first, *parts), jnp.where(first, *reversed(parts))
        joined = jnp.concatenate([low, high], axis=0).astype(bf16)
        packet[32 + 16 * half : 48 + 16 * half] = joined
    own, other = attend[...].astype(f32), got[:, FF : FF + D].astype(f32)
    joined = jnp.concatenate([jnp.where(first, own, other), jnp.where(first, other, own)], axis=0)
    packet[64:80] = joined.astype(bf16)
    own, other = vectors[:4].astype(f32), got[:4, FF + D :].astype(f32)
    joined = jnp.concatenate([jnp.where(first, own, other), jnp.where(first, other, own)], axis=0)
    packet[80:] = jnp.concatenate([joined, jnp.zeros((8, D - 128), f32)], axis=1).astype(bf16)


def pack(core, expand, reduce, attend, vectors, got):
    return pl.pallas_call(
        pack_kernel,
        in_specs=[pl.BlockSpec(memory_space=pltpu.SMEM)]
        + [pl.BlockSpec(memory_space=pltpu.VMEM)] * 5,
        out_specs=pl.BlockSpec(memory_space=pltpu.VMEM),
        out_shape=jax.ShapeDtypeStruct((88, D), bf16),
        compiler_params=pltpu.CompilerParams(vmem_limit_bytes=60 * 2**20),
        name="pack",
    )(core, expand, reduce, attend, vectors, got)


def project_kernel(order, mine, theirs, first, second, packed, rows_out):
    tokens = jnp.concatenate([mine[...], theirs[...]], axis=0)
    low = first[0].astype(f32).reshape(192, 512).astype(bf16)
    high = second[:, 0].astype(f32).reshape(192, 512).astype(bf16)
    made = dot_nt(tokens[:, :512], low) + dot_nt(tokens[:, 512:], high)
    packed[0] = made.astype(bf16)
    rows_out[:, :512] = low
    rows_out[:, 512:] = high


def project(order, mine, theirs, first, second):
    return pl.pallas_call(
        project_kernel,
        grid_spec=pltpu.PrefetchScalarGridSpec(
            num_scalar_prefetch=1,
            grid=(8,),
            in_specs=[
                pl.BlockSpec((128, D), lambda k, order: (0, 0)),
                pl.BlockSpec((128, D), lambda k, order: (0, 0)),
                pl.BlockSpec((1, 8, 24, 512), lambda k, order: (order[0, k], 0, 0, 0)),
                pl.BlockSpec((8, 1, 24, 512), lambda k, order: (0, order[1, k], 0, 0)),
            ],
            out_specs=[
                pl.BlockSpec((1, 256, 192), lambda k, order: (k, 0, 0)),
                pl.BlockSpec((192, D), lambda k, order: (k, 0)),
            ],
        ),
        out_shape=[
            jax.ShapeDtypeStruct((8, 256, 192), bf16),
            pltpu.HBM((1536, D), bf16),
        ],
        compiler_params=pltpu.CompilerParams(vmem_limit_bytes=32 * 2**20),
        name="project",
    )(order, mine, theirs, first, second)


def arrange_kernel(core, mine, theirs, heads):
    for column in range(8):
        own, other = mine[column].astype(f32), theirs[column].astype(f32)
        first = core[0] == 0
        joined = jnp.concatenate(
            [jnp.where(first, own, other), jnp.where(first, other, own)], axis=1
        )
        for place in range(3):
            chunk = 3 * column + place
            heads[chunk % 8, chunk // 8] = joined[:, 128 * place : 128 * (place + 1)].astype(bf16)


def arrange(core, mine, theirs):
    return pl.pallas_call(
        arrange_kernel,
        in_specs=[
            pl.BlockSpec(memory_space=pltpu.SMEM),
            pl.BlockSpec(memory_space=pltpu.VMEM),
            pl.BlockSpec(memory_space=pltpu.VMEM),
        ],
        out_specs=pl.BlockSpec(memory_space=pltpu.VMEM),
        out_shape=jax.ShapeDtypeStruct((8, 3, 128, 128), bf16),
        compiler_params=pltpu.CompilerParams(vmem_limit_bytes=32 * 2**20),
        name="arrange",
    )(core, mine, theirs)


def project_grad_kernel(
    keep, got, keep_pair, got_pair, tokens_own, tokens_got, tokens_pair, table, blocks
):
    tokens = jnp.concatenate([tokens_own[...], tokens_got[...], tokens_pair[...]], axis=0)
    for step in range(2):
        span = slice(384 * step, 384 * (step + 1))
        parts = [part[:, span] for part in (keep, got, keep_pair, got_pair)]
        made = dot_tn(jnp.concatenate(parts, axis=0), tokens).reshape(16, 24, D)
        rest = table[128 * step : 128 * (step + 1)].reshape(16, 8, 512)
        made = jnp.concatenate([made[..., :512], made[..., 512:], rest], axis=1)
        blocks[16 * step : 16 * (step + 1)] = made.astype(bf16)


def project_grad(keep, got, keep_pair, got_pair, tokens_own, tokens_got, tokens_pair, table):
    return pl.pallas_call(
        project_grad_kernel,
        in_specs=[pl.BlockSpec(memory_space=pltpu.VMEM)] * 8,
        out_specs=pl.BlockSpec(memory_space=pltpu.VMEM),
        out_shape=jax.ShapeDtypeStruct((32, 56, 512), bf16),
        compiler_params=pltpu.CompilerParams(vmem_limit_bytes=48 * 2**20),
        name="project_grad",
    )(keep, got, keep_pair, got_pair, tokens_own, tokens_got, tokens_pair, table)


def ring_scatter(blocks, axis, size, dtype=f32):
    place = lax.axis_index(axis)
    total = lax.dynamic_index_in_dim(blocks, place, 0, keepdims=False).astype(f32)
    for step in range(1, size):
        sent = lax.dynamic_index_in_dim(blocks, (place + step) % size, 0, keepdims=False)
        total = total + shifted(sent, axis, size, step).astype(f32)
    return total.astype(dtype)


def y_scatter(blocks):
    place = 2 * lax.axis_index("yh") + lax.axis_index("yl")
    total = lax.dynamic_index_in_dim(blocks, place, 0, keepdims=False).astype(f32)

    def on_mesh(y):
        return 2 * (y % 2) + y // 2

    for step in range(1, 4):
        sent = lax.dynamic_index_in_dim(blocks, (place + step) % 4, 0, keepdims=False)
        ring = [(on_mesh(y), on_mesh((y + step) % 4)) for y in range(4)]
        total = total + lax.ppermute(sent, ("yl", "yh"), ring).astype(f32)
    return total


def split_kernel(core, heads, keep, give):
    for column in range(8):
        chunks = [3 * column + place for place in range(3)]
        joined = jnp.concatenate(
            [heads[chunk % 8, chunk // 8].astype(f32) for chunk in chunks], axis=1
        )
        first = core[0] == 0
        zero, one = joined[:, :192], joined[:, 192:]
        span = slice(192 * column, 192 * (column + 1))
        keep[:, span] = jnp.where(first, zero, one).astype(bf16)
        give[:, span] = jnp.where(first, one, zero).astype(bf16)


def split(core, heads):
    return pl.pallas_call(
        split_kernel,
        in_specs=[
            pl.BlockSpec(memory_space=pltpu.SMEM),
            pl.BlockSpec(memory_space=pltpu.VMEM),
        ],
        out_specs=[pl.BlockSpec(memory_space=pltpu.VMEM)] * 2,
        out_shape=[jax.ShapeDtypeStruct((128, 1536), bf16)] * 2,
        compiler_params=pltpu.CompilerParams(vmem_limit_bytes=32 * 2**20),
        name="split",
    )(core, heads)


def per_device(
    tokens,
    w_project,
    w_attend,
    first_gain,
    first_shift,
    w_expand,
    w_reduce,
    second_gain,
    second_shift,
    position_table,
    w_query,
    w_key,
    lengths,
    cotangent,
):
    core = lax.axis_index("core")
    group = lax.axis_index(GROUP)
    local = tokens.shape[0]
    core_id = core.reshape(1)
    pair = 2 * local
    column_bucket = bucket_values(SEQ - 1 - np.arange(2 * SEQ - 1), SPAN)
    fold = np.append(column_bucket, -1)[None, :] == np.arange(2 * SPAN)[:, None]
    fold = jnp.asarray(fold.astype(np.float32)).astype(bf16)

    def by_core(zero, one):
        return jnp.where(core == 0, zero, one)

    def in_order(mine, theirs):
        return by_core(mine, theirs), by_core(theirs, mine)

    cotangent_got = swap(cotangent)
    tokens_got = swap(tokens)
    weights_own = jnp.concatenate([w_key, w_query], axis=1)
    first, second, order, table_t, position_rows = gather_projection(
        w_project.T,
        position_table.T,
        jnp.concatenate([weights_own[:32], weights_own[32:]], axis=1),
    )
    position_weights = jnp.stack([position_rows[..., :256], position_rows[..., 256:]], axis=1)
    position_weights = position_weights.reshape(512, 256)

    vectors = jnp.stack([first_gain, first_shift, second_gain, second_shift])
    vectors = jnp.pad(vectors, ((0, 4), (0, 128 - 8)))
    reduce_rows = w_reduce.T
    got = swap(jnp.concatenate([reduce_rows, w_attend.T, vectors], axis=1))
    packet = pack(core_id, w_expand.T, reduce_rows, w_attend.T, vectors, got)
    gathered = lax.all_gather(packet, CHIPS, axis=0, tiled=False).reshape(8, 8, 88, D)
    vec = gathered[..., 80:, :8].reshape(8, 8, 2, 4, 8).transpose(3, 1, 2, 0, 4)
    vec = vec.reshape(4, D).astype(f32)
    gain_one, shift_one, gain_two, shift_two = vec[0], vec[1], vec[2], vec[3]

    packed, project_t = project(order, tokens, tokens_got, first, second)
    heads_in = exchange(arrange(core_id, packed[:, :local], swap(packed[:, local:])), GROUP)
    rel = dot_tn(table_t, position_weights)
    rel = dot_tn(fold, (rel + swap(rel)).astype(bf16)).astype(bf16)
    heads_in, tokens_both = lax.optimization_barrier(
        (heads_in, jnp.concatenate([tokens, tokens_got], axis=0))
    )
    tokens_pair = swap_chips(tokens_both)
    context, kept = attend(lengths, heads_in, rel)
    context, tokens_pair = lax.optimization_barrier(
        (exchange(context, GROUP), tokens_pair)
    )
    context_got = swap(context)

    resid_own = project_back(context, tokens, gathered)
    resid_got = swap(resid_own)
    activ, slope, ffn_own, ffn_sent = ffn_forward(resid_own, resid_got, vec, gathered)
    output, blocks, grad_own, grad_sent, sums = ffn_backward(
        core_id,
        resid_own,
        resid_got,
        vec,
        ffn_own,
        swap(ffn_sent),
        cotangent,
        cotangent_got,
        activ,
        swap(activ),
        slope,
        gathered,
    )
    grad_resid1, grad_context, grad_attended, sums = first_backward(
        resid_own, resid_got, vec, grad_own, swap(grad_sent), sums, gathered
    )
    attend_blocks = make_attend_blocks(core_id, grad_attended, context, context_got, sums)

    summed = lax.psum_scatter(
        blocks.reshape(16, 4 * 64, D), ("x", "z"), scatter_dimension=0, tiled=True
    )
    attend_blocks, grad_ctx = lax.optimization_barrier(
        (attend_blocks, exchange(grad_context, GROUP))
    )
    attend_sum = exchange(attend_blocks.reshape(64, 8, D + 128), COLUMN + GROUP)

    grads, rel_grad = attend_back(heads_in, rel, grad_ctx, kept)
    grads, attend_sum = lax.optimization_barrier((grads, attend_sum))
    attend_sum = jnp.sum(attend_sum.astype(f32), axis=0)
    grad_attend = attend_sum[:, :D].T
    vectors = attend_sum[:4, D:].reshape(4, 16, 8)
    vectors = lax.dynamic_index_in_dim(vectors, 8 * core + group, axis=1, keepdims=False)
    grads = exchange(grads, GROUP)
    yl = lax.axis_index("yl")
    rel_grad = sum(dot_nn(fold, part) for part in two_parts(rel_grad))
    rel_grad = rel_grad + swap(rel_grad)
    rel_grad = two_parts(rel_grad + swap_chips(rel_grad.astype(bf16)).astype(f32))
    table_half = lax.dynamic_slice_in_dim(table_t, 256 * yl, 256, axis=0)
    weights_half = lax.dynamic_slice_in_dim(position_weights, 256 * yl, 256, axis=0)
    position_grads = sum(dot_nn(table_half, part) for part in rel_grad)
    position_grads = ring_scatter(position_grads.reshape(4, 64, 256), "x", 4)
    table_blocks = sum(dot_nt(weights_half, part) for part in rel_grad)

    def by_chip(value):
        low, high = value[:, :768], value[:, 768:]
        return jnp.where(yl == 0, low, high), jnp.where(yl == 0, high, low)

    grads, position_grads = lax.optimization_barrier((grads, position_grads))
    keep, give = split(core_id, grads)
    keep_half, keep_other = by_chip(keep)
    got = swap(give)
    got_half, got_other = by_chip(got)
    blocks = project_grad(
        keep_half,
        got_half,
        swap_chips(keep_other),
        swap_chips(got_other),
        tokens,
        tokens_got,
        tokens_pair,
        table_blocks,
    )
    blocks, got = lax.optimization_barrier((blocks, got))
    tokens_part = dot_nn(keep, project_t)
    tokens_sent = dot_nn(got, project_t).astype(bf16)
    tokens_sent, tokens_part, summed = lax.optimization_barrier(
        (tokens_sent, grad_resid1 + tokens_part, summed)
    )
    received, summed, tokens_back = lax.optimization_barrier(
        (
            exchange(blocks, ("x",) + GROUP),
            y_scatter(summed.reshape(4, 64, D)),
            swap(tokens_sent),
        )
    )
    grad_expand = summed[:32].T
    grad_reduce = summed[32:64].reshape(4, 8, D).transpose(1, 0, 2).reshape(8, FF).T
    received = jnp.sum(received.astype(f32), axis=0)
    grad_project = jnp.concatenate([received[:24], received[24:48]], axis=1).T
    grad_table = received[48:].T
    tokens_grad = tokens_part + tokens_back
    grad_key, grad_query = position_grads[:, :128], position_grads[:, 128:]

    return (
        output,
        tokens_grad.astype(bf16),
        grad_project,
        grad_attend,
        vectors[0],
        vectors[1],
        grad_expand,
        grad_reduce,
        vectors[2],
        vectors[3],
        grad_table,
        grad_query,
        grad_key,
    )


def solution(mesh):
    parts = Mesh(mesh.devices.reshape(2, 4, 2, 4, 2), EVERY)
    in_specs = (
        P(EVERY, None),
        P(None, EVERY),
        P(None, EVERY),
        P(EVERY),
        P(EVERY),
        P(None, EVERY),
        P(None, EVERY),
        P(EVERY),
        P(EVERY),
        P(None, EVERY),
        P(DP, GROUP),
        P(DP, GROUP),
        P(DP),
        P(EVERY, None),
    )
    out_specs = (
        P(EVERY, None),
        P(EVERY, None),
        P(None, EVERY),
        P(None, EVERY),
        P(EVERY),
        P(EVERY),
        P(None, EVERY),
        P(None, EVERY),
        P(EVERY),
        P(EVERY),
        P(None, EVERY),
        P(DP, GROUP),
        P(DP, GROUP),
    )
    return jax.shard_map(
        per_device, mesh=parts, in_specs=in_specs, out_specs=out_specs, check_vma=False
    )
```

```python
import math

import jax
import jax.numpy as jnp
import numpy as np
from jax import lax
from jax.experimental import pallas as pl
from jax.experimental.pallas import tpu as pltpu
from jax.sharding import Mesh
from jax.sharding import PartitionSpec as P

D = 1024
HEADS = 16
HEAD_DIM = 64
FF = 4096
SPAN = 256
SEQ = 512
BLOCK = 128
WINDOW = SEQ + BLOCK
STEP = 4

EPS = 1e-07
MASKED = -1e30

DP = ("yl", "x", "core")
GROUP = ("z", "yh")
COLUMN = ("yl", "x")
EVERY = DP + GROUP
CHIPS = ("z", "yh", "yl", "x")
DEVICES = ("core",) + CHIPS
bf16 = jnp.bfloat16
f32 = jnp.float32


def bucket_values(offset, span):
    middle = span // 2
    absolute = np.where((offset < middle) & (offset > -middle), middle - 1, np.abs(offset))
    log_place = (
        np.ceil(np.log(absolute / middle) / np.log((2 * span - 1) / middle) * (middle - 1)) + middle
    )
    buckets = np.where(absolute <= middle, offset, log_place * np.sign(offset)).astype(np.int64)
    return np.clip(buckets + span, 0, 2 * span - 1).astype(np.int32)


def normalize(value, gain, shift):
    center = value - jnp.mean(value, axis=-1, keepdims=True)
    inverse = lax.rsqrt(jnp.mean(center * center, axis=-1, keepdims=True) + EPS)
    scaled = center * inverse
    return (scaled * gain + shift, scaled, inverse)


def normalize_back(incoming, scaled, inverse, gain):
    grad_scaled = incoming * gain
    middle = (
        grad_scaled
        - jnp.mean(grad_scaled, axis=-1, keepdims=True)
        - scaled * jnp.mean(grad_scaled * scaled, axis=-1, keepdims=True)
    )
    return inverse * middle


def dot_nn(left, right):
    return lax.dot_general(left, right, (((1,), (0,)), ((), ())), preferred_element_type=f32)


def dot_nt(left, right):
    return lax.dot_general(left, right, (((1,), (1,)), ((), ())), preferred_element_type=f32)


def dot_tn(left, right):
    return lax.dot_general(left, right, (((0,), (0,)), ((), ())), preferred_element_type=f32)


def window(block):
    start = SEQ - BLOCK - BLOCK * block
    return slice(start, start + WINDOW)


def rows(block):
    return slice(BLOCK * block, BLOCK * (block + 1))


def skew(values):
    return pltpu.roll(values, SEQ + 1, 1, stride=1, stride_axis=0)[:, :SEQ]


def unskew(values):
    wide = jnp.concatenate([values, jnp.zeros((BLOCK, BLOCK), f32)], axis=1)
    return pltpu.roll(wide, 0, 1, stride=1, stride_axis=0)


def turn(mirror, values):
    upper = values.astype(bf16)
    return dot_nn(mirror, upper) + dot_nn(mirror, (values - upper.astype(f32)).astype(bf16))


def one_head(value, head):
    lane = lax.broadcasted_iota(jnp.int32, value.shape, 1)
    return jnp.where(lane // HEAD_DIM == head, value, jnp.zeros_like(value))


def query_bias(key, rel_queries, bias):
    for block in range(SEQ // BLOCK):
        by_offset = dot_nt(key[rows(block)], rel_queries[window(block)])
        bias[:, rows(block)] = skew(by_offset).T


def probabilities(query, key, rel_keys, bias, block, length):
    part = query[rows(block)]
    logits = dot_nt(part, key) + skew(dot_nt(part, rel_keys[window(block)])) + bias[rows(block)]
    logits = logits * (1.0 / math.sqrt(3 * HEAD_DIM))
    column = lax.broadcasted_iota(jnp.int32, logits.shape, 1)
    logits = jnp.where(column < length, logits, MASKED)
    exponent = jnp.exp(logits - jnp.max(logits, axis=1, keepdims=True))
    return exponent * (1.0 / jnp.sum(exponent, axis=1, keepdims=True))


def attend_kernel(lengths, heads_in, rel, context, kept, bias):
    length = lengths[pl.program_id(0)]
    query, key, values = (heads_in[:, part].reshape(SEQ, 128) for part in range(3))
    rel_keys, rel_queries = rel[:, :128], rel[:, 128:]
    total = [jnp.zeros((BLOCK, 128), f32) for _ in range(SEQ // BLOCK)]
    for head in range(2):
        query_h, key_h, values_h = (one_head(part, head) for part in (query, key, values))
        query_bias(key_h, rel_queries, bias)
        for block in range(SEQ // BLOCK):
            probs = probabilities(query_h, key, rel_keys, bias, block, length)
            kept[0, head, rows(block)] = probs
            total[block] = total[block] + dot_nn(probs.astype(bf16), values_h)
    for block in range(SEQ // BLOCK):
        context[block] = total[block].astype(bf16)


def attend_back_kernel(
    heads_in, rel, grad_context, kept, grads, grad_rel, probs_ref, grad_ref
):
    query, key, values = (heads_in[:, part].reshape(SEQ, 128) for part in range(3))
    grad_ctx = grad_context[...].reshape(SEQ, 128)
    rel_keys, rel_queries = rel[:, :128], rel[:, 128:]
    blocks = SEQ // BLOCK
    first = lax.broadcasted_iota(jnp.int32, (BLOCK, BLOCK), 0)
    second = lax.broadcasted_iota(jnp.int32, (BLOCK, BLOCK), 1)
    mirror = jnp.where(first + second == BLOCK - 1, 1.0, 0.0).astype(bf16)

    @pl.when(pl.program_id(0) == 0)
    def _():
        grad_rel[...] = jnp.zeros_like(grad_rel)

    queries, keys, ctxs = (
        [one_head(part, head) for head in range(2)] for part in (query, key, grad_ctx)
    )
    rel_keys_of = [one_head(rel_keys, head) for head in range(2)]
    rel_queries_of = [one_head(rel_queries, head) for head in range(2)]
    for block in range(blocks):
        grad_q, turned, rel_part = 0.0, 0.0, 0.0
        for head in range(2):
            probs = kept[0, head, rows(block)]
            probs_ref[head, rows(block)] = probs.astype(bf16)
            grad_probs = dot_nt(ctxs[head][rows(block)], values)
            inner = jnp.sum(probs * grad_probs, axis=1, keepdims=True)
            grad = (probs * (grad_probs - inner) * (1.0 / math.sqrt(3 * HEAD_DIM))).astype(bf16)
            grad_ref[head, rows(block)] = grad
            by_offset = unskew(dot_nn(mirror, grad)).astype(bf16)
            grad_q = grad_q + dot_nn(grad, keys[head])
            turned = turned + dot_nn(by_offset, rel_keys_of[head][window(block)])
            mirrored = dot_nn(mirror, queries[head][rows(block)]).astype(bf16)
            rel_part = rel_part + dot_tn(by_offset, mirrored)
        grad_rel[window(block), :128] += rel_part
        grads[block, 0] = (grad_q + turn(mirror, turned)).astype(bf16)
    for block in range(blocks):
        grad_k, grad_v, turned, rel_part = 0.0, 0.0, 0.0, 0.0
        for head in range(2):
            grad = grad_ref[head, :, rows(block)]
            by_offset = unskew(dot_nt(mirror, grad)).astype(bf16)
            grad_k = grad_k + dot_tn(grad, queries[head])
            turned = turned + dot_nn(by_offset, rel_queries_of[head][window(block)])
            grad_v = grad_v + dot_tn(probs_ref[head, :, rows(block)], ctxs[head])
            mirrored = dot_nn(mirror, keys[head][rows(block)]).astype(bf16)
            rel_part = rel_part + dot_tn(by_offset, mirrored)
        grad_rel[window(block), 128:] += rel_part
        grads[block, 1] = (grad_k + turn(mirror, turned)).astype(bf16)
        grads[block, 2] = grad_v.astype(bf16)


def attend(lengths, heads_in, rel):
    return pl.pallas_call(
        attend_kernel,
        grid=(2,),
        in_specs=[
            pl.BlockSpec(memory_space=pltpu.SMEM),
            pl.BlockSpec((4, 3, 128, 128), lambda row: (row, 0, 0, 0)),
            pl.BlockSpec((2 * SEQ, 256), lambda row: (0, 0)),
        ],
        out_specs=[
            pl.BlockSpec((4, 128, 128), lambda row: (row, 0, 0)),
            pl.BlockSpec((1, 2, SEQ, SEQ), lambda row: (row, 0, 0, 0)),
        ],
        out_shape=[
            jax.ShapeDtypeStruct((8, 128, 128), bf16),
            pltpu.HBM((2, 2, SEQ, SEQ), f32),
        ],
        scratch_shapes=[pltpu.VMEM((SEQ, SEQ), f32)],
        compiler_params=pltpu.CompilerParams(vmem_limit_bytes=48 * 2**20),
        name="attend",
    )(lengths, heads_in, rel)


def attend_back(heads_in, rel, grad_context, kept):
    return pl.pallas_call(
        attend_back_kernel,
        grid=(2,),
        in_specs=[
            pl.BlockSpec((4, 3, 128, 128), lambda row: (row, 0, 0, 0)),
            pl.BlockSpec((2 * SEQ, 256), lambda row: (0, 0)),
            pl.BlockSpec((4, 128, 128), lambda row: (row, 0, 0)),
            pl.BlockSpec((1, 2, SEQ, SEQ), lambda row: (row, 0, 0, 0)),
        ],
        out_specs=[
            pl.BlockSpec((4, 3, 128, 128), lambda row: (row, 0, 0, 0)),
            pl.BlockSpec((2 * SEQ, 256), lambda row: (0, 0)),
        ],
        out_shape=[
            jax.ShapeDtypeStruct((8, 3, 128, 128), bf16),
            jax.ShapeDtypeStruct((2 * SEQ, 256), f32),
        ],
        scratch_shapes=[
            pltpu.VMEM((2, SEQ, SEQ), bf16),
            pltpu.VMEM((2, SEQ, SEQ), bf16),
        ],
        compiler_params=pltpu.CompilerParams(vmem_limit_bytes=48 * 2**20),
        cost_estimate=pl.CostEstimate(
            flops=20 * 10**9, bytes_accessed=8 * 2**20, transcendentals=2**20
        ),
        name="attend_back",
    )(heads_in, rel, grad_context, kept)


def owner_rows(block):
    wide = block.astype(f32).reshape(8, STEP, 2, 8, block.shape[-1])
    return wide.transpose(1, 2, 0, 3, 4).reshape(STEP * 128, block.shape[-1]).astype(bf16)


def project_back_kernel(context, tokens, weights, resid):
    rows_in = jnp.concatenate([context[group] for group in range(8)], axis=1)
    resid[...] = tokens[...].astype(f32) + dot_nt(rows_in, owner_rows(weights[...]))


def project_back(context, tokens, gathered):
    return pl.pallas_call(
        project_back_kernel,
        grid=(8 // STEP,),
        in_specs=[
            pl.BlockSpec((8, 128, 128), lambda k: (0, 0, 0)),
            pl.BlockSpec((128, STEP * 128), lambda k: (0, k)),
            pl.BlockSpec((8, STEP, 16, D), lambda k: (0, k, 4, 0)),
        ],
        out_specs=pl.BlockSpec((128, STEP * 128), lambda k: (0, k)),
        out_shape=jax.ShapeDtypeStruct((128, D), f32),
        compiler_params=pltpu.CompilerParams(vmem_limit_bytes=48 * 2**20),
        name="project_back",
    )(context, tokens, gathered)


def ffn_kernel(mine, theirs, vec, expand, reduce, act, slope, partial, sent, low):
    phase, k = pl.program_id(0), pl.program_id(1)

    @pl.when((phase == 0) & (k == 0))
    def _():
        for half, resid in enumerate((mine, theirs)):
            first_norm, scaled, inverse = normalize(resid[...], vec[0:1], vec[1:2])
            low[128 * half : 128 * (half + 1)] = first_norm.astype(bf16)

    @pl.when(phase == 0)
    def _():
        for column in range(STEP):
            inner = dot_nt(low[...], expand[:, column].reshape(256, D))
            spread_in = 0.5 + 0.5 * lax.erf(inner * math.sqrt(0.5))
            act[STEP * k + column] = (inner * spread_in).astype(bf16)
            density = jnp.exp(-0.5 * inner * inner) * (1.0 / math.sqrt(2.0 * math.pi))
            slope[column] = spread_in + inner * density

    @pl.when(phase == 1)
    def _():
        total = jnp.zeros((256, STEP * 128), f32)
        for half in range(2):
            rows_in = jnp.concatenate([act[4 * half + part] for part in range(4)], axis=1)
            weights = owner_rows(reduce[:, :, 16 * half : 16 * (half + 1)])
            total = total + dot_nt(rows_in, weights)
        partial[...] = total
        sent[...] = total.astype(bf16)


def ffn_forward(mine, theirs, vec, gathered):
    whole = lambda phase, k: (0, 0)
    return pl.pallas_call(
        ffn_kernel,
        grid=(2, 8 // STEP),
        in_specs=[
            pl.BlockSpec((128, D), whole),
            pl.BlockSpec((128, D), whole),
            pl.BlockSpec((4, D), whole),
            pl.BlockSpec((8, STEP, 32, D), lambda phase, k: (0, jnp.where(phase == 0, k, 8 // STEP - 1), 0, 0)),
            pl.BlockSpec((8, STEP, 32, D), lambda phase, k: (0, jnp.where(phase == 0, 0, k), 1, 0)),
        ],
        out_specs=[
            pl.BlockSpec((8, 256, 256), lambda phase, k: (0, 0, 0)),
            pl.BlockSpec((STEP, 256, 256), lambda phase, k: (jnp.where(phase == 0, k, 8 // STEP - 1), 0, 0)),
            pl.BlockSpec((256, STEP * 128), lambda phase, k: (0, jnp.where(phase == 0, 0, k))),
            pl.BlockSpec((256, STEP * 128), lambda phase, k: (0, jnp.where(phase == 0, 0, k))),
        ],
        out_shape=[
            jax.ShapeDtypeStruct((8, 256, 256), bf16),
            pltpu.HBM((8, 256, 256), f32),
            pltpu.HBM((256, D), f32),
            jax.ShapeDtypeStruct((256, D), bf16),
        ],
        scratch_shapes=[pltpu.VMEM((256, D), bf16)],
        compiler_params=pltpu.CompilerParams(vmem_limit_bytes=48 * 2**20),
        name="ffn_forward",
    )(mine, theirs, vec, gathered, gathered)


def own_half(core, wide):
    return jnp.where(core[0] == 0, wide[:, :64], wide[:, 64:])


def ffn_back_kernel(
    core,
    mine,
    theirs,
    vec,
    ffn_own,
    ffn_got,
    cot_own,
    cot_got,
    act_own,
    act_got,
    slope,
    expand,
    reduce,
    output,
    blocks,
    partial,
    sent,
    sums,
    low,
    grad_ffn,
    grad_act,
    act,
):
    phase, k = pl.program_id(0), pl.program_id(1)

    @pl.when((phase == 0) & (k == 0))
    def _():
        sums[...] = jnp.zeros_like(sums)
        for half, (resid, cot) in enumerate(((mine, cot_own), (theirs, cot_got))):
            span = slice(128 * half, 128 * (half + 1))
            cross = slice(128 * (1 - half), 128 * (2 - half))
            first_norm, scaled, inverse = normalize(resid[...], vec[0:1], vec[1:2])
            low[span] = first_norm.astype(bf16)
            resid2 = first_norm + (ffn_own[span] + ffn_got[cross])
            normed, scaled, inverse = normalize(resid2, vec[2:3], vec[3:4])
            grad = cot[...].astype(f32)
            if half == 0:
                output[...] = normed.astype(bf16)
            sums[2:3] += jnp.sum(grad * scaled, axis=0, keepdims=True)
            sums[3:4] += jnp.sum(grad, axis=0, keepdims=True)
            grad = normalize_back(grad, scaled, inverse, vec[2:3])
            partial[span] = 0.5 * grad
            grad = grad.astype(bf16)
            for chunk in range(8 // STEP):
                grad_ffn[chunk, span] = grad[:, STEP * 128 * chunk : STEP * 128 * (chunk + 1)]
        grad_act[...] = jnp.zeros_like(grad_act)
        for chunk in range(8):
            own, got = act_own[chunk], act_got[chunk]
            got = jnp.concatenate([got[128:], got[:128]], axis=0)
            start = 512 * (chunk % 2)
            act[chunk // 2, :, start : start + 256] = jnp.where(core[0] == 0, own, got)
            act[chunk // 2, :, start + 256 : start + 512] = jnp.where(core[0] == 0, got, own)

    @pl.when(phase == 0)
    def _():
        grad = grad_ffn[k]
        own = [own_half(core, grad[:, 128 * column : 128 * (column + 1)]) for column in range(STEP)]
        own = jnp.concatenate(own, axis=1)
        for half in range(2):
            weights = owner_rows(reduce[:, :, 16 * half : 16 * (half + 1)])
            for part in range(4):
                grad_act[4 * half + part] += dot_nn(grad, weights[:, 256 * part : 256 * (part + 1)])
            made = [dot_tn(own, act[2 * half + part]).reshape(STEP, 8, 8, D) for part in range(2)]
            made = jnp.concatenate(made, axis=2).astype(bf16).reshape(STEP, 4, 2, 16, D)
            blocks[:, :, :, 0, 16 * half : 16 * (half + 1)] = made

    @pl.when(phase == 1)
    def _():
        for column in range(STEP):
            weights = expand[:, column].reshape(256, D)
            grad = (slope[column] * grad_act[STEP * k + column]).astype(bf16)
            made = dot_tn(grad, low[...]).astype(bf16)
            blocks[column, :, :, 0] = made.reshape(4, 2, 32, D)
            partial[...] += dot_nn(grad, weights)

    @pl.when((phase == 1) & (k == 8 // STEP - 1))
    def _():
        sent[...] = partial[...].astype(bf16)


def ffn_backward(
    core, mine, theirs, vec, ffn_own, ffn_got, cot_own, cot_got, act_own, act_got, slope, gathered
):
    whole = lambda phase, k: (0, 0)
    return pl.pallas_call(
        ffn_back_kernel,
        grid=(2, 8 // STEP),
        in_specs=[
            pl.BlockSpec(memory_space=pltpu.SMEM),
            pl.BlockSpec((128, D), whole),
            pl.BlockSpec((128, D), whole),
            pl.BlockSpec((4, D), whole),
            pl.BlockSpec((256, D), whole),
            pl.BlockSpec((256, D), whole),
            pl.BlockSpec((128, D), whole),
            pl.BlockSpec((128, D), whole),
            pl.BlockSpec((8, 256, 256), lambda phase, k: (0, 0, 0)),
            pl.BlockSpec((8, 256, 256), lambda phase, k: (0, 0, 0)),
            pl.BlockSpec((STEP, 256, 256), lambda phase, k: (jnp.where(phase == 0, 0, k), 0, 0)),
            pl.BlockSpec((8, STEP, 32, D), lambda phase, k: (0, jnp.where(phase == 0, 0, k), 0, 0)),
            pl.BlockSpec((8, STEP, 32, D), lambda phase, k: (0, jnp.where(phase == 0, k, 8 // STEP - 1), 1, 0)),
        ],
        out_specs=[
            pl.BlockSpec((128, D), whole),
            pl.BlockSpec(
                (STEP, 4, 2, 1, 32, D),
                lambda phase, k: (k % (4 // STEP), 0, 0, k // (4 // STEP), 1 - phase, 0),
            ),
            pl.BlockSpec((256, D), whole),
            pl.BlockSpec((256, D), whole),
            pl.BlockSpec((8, D), whole),
        ],
        out_shape=[
            jax.ShapeDtypeStruct((128, D), bf16),
            jax.ShapeDtypeStruct((4, 4, 2, 2, 64, D), bf16),
            jax.ShapeDtypeStruct((256, D), f32),
            jax.ShapeDtypeStruct((256, D), bf16),
            jax.ShapeDtypeStruct((8, D), f32),
        ],
        scratch_shapes=[
            pltpu.VMEM((256, D), bf16),
            pltpu.VMEM((8 // STEP, 256, STEP * 128), bf16),
            pltpu.VMEM((8, 256, 256), f32),
            pltpu.VMEM((4, 256, D), bf16),
        ],
        compiler_params=pltpu.CompilerParams(vmem_limit_bytes=56 * 2**20),
        name="ffn_backward",
    )(
        core,
        mine,
        theirs,
        vec,
        ffn_own,
        ffn_got,
        cot_own,
        cot_got,
        act_own,
        act_got,
        slope,
        gathered,
        gathered,
    )


def first_back_kernel(
    mine, theirs, vec, grad_own, grad_got, sums, weights, grad_resid, grad_context, low, found, total
):
    k = pl.program_id(0)

    @pl.when(k == 0)
    def _():
        partial = sums[...]
        place = lax.broadcasted_iota(jnp.int32, (8, D), 0)
        for half, resid in enumerate((mine, theirs)):
            span = slice(128 * half, 128 * (half + 1))
            cross = slice(128 * (1 - half), 128 * (2 - half))
            normed, scaled, inverse = normalize(resid[...], vec[0:1], vec[1:2])
            grad = grad_own[span] + grad_got[cross]
            partial += jnp.where(place == 0, jnp.sum(grad * scaled, axis=0, keepdims=True), 0.0)
            partial += jnp.where(place == 1, jnp.sum(grad, axis=0, keepdims=True), 0.0)
            grad = normalize_back(grad, scaled, inverse, vec[0:1])
            if half == 0:
                grad_resid[...] = grad
            low[span] = grad.astype(bf16)
        found[...] = partial
        total[...] = jnp.zeros_like(total)

    width = STEP * 128
    for part in range(8 // STEP):

        @pl.when(k == part)
        def _():
            grad = low[:128, width * part : width * (part + 1)]
            total[...] += dot_nn(grad, owner_rows(weights[...]))

    @pl.when(k == 8 // STEP - 1)
    def _():
        for group in range(8):
            grad_context[group] = total[:, 128 * group : 128 * (group + 1)].astype(bf16)


def first_backward(mine, theirs, vec, grad_own, grad_got, sums, gathered):
    whole = lambda k: (0, 0)
    return pl.pallas_call(
        first_back_kernel,
        grid=(8 // STEP,),
        in_specs=[
            pl.BlockSpec((128, D), whole),
            pl.BlockSpec((128, D), whole),
            pl.BlockSpec((4, D), whole),
            pl.BlockSpec((256, D), whole),
            pl.BlockSpec((256, D), whole),
            pl.BlockSpec((8, D), whole),
            pl.BlockSpec((8, STEP, 16, D), lambda k: (0, k, 4, 0)),
        ],
        out_specs=[
            pl.BlockSpec((128, D), whole),
            pl.BlockSpec((8, 128, 128), lambda k: (0, 0, 0)),
            pl.BlockSpec((256, D), whole),
            pl.BlockSpec((8, D), whole),
        ],
        out_shape=[
            jax.ShapeDtypeStruct((128, D), f32),
            jax.ShapeDtypeStruct((8, 128, 128), bf16),
            jax.ShapeDtypeStruct((256, D), bf16),
            jax.ShapeDtypeStruct((8, D), f32),
        ],
        scratch_shapes=[pltpu.VMEM((128, D), f32)],
        compiler_params=pltpu.CompilerParams(vmem_limit_bytes=56 * 2**20),
        name="first_backward",
    )(mine, theirs, vec, grad_own, grad_got, sums, gathered)


def attend_blocks_kernel(core, low, ctx_own, ctx_got, found, blocks):
    ctx = [jnp.concatenate([part[group] for group in range(8)], axis=1) for part in (ctx_own, ctx_got)]
    ctx = jnp.concatenate(ctx, axis=0)
    for half in range(2):
        columns = range(4 * half, 4 * (half + 1))
        own = [own_half(core, low[:, 128 * column : 128 * (column + 1)]) for column in columns]
        made = dot_tn(jnp.concatenate(own, axis=1), ctx).reshape(4, 8, 8, D)
        for place, column in enumerate(columns):
            row = found[:, 128 * column : 128 * (column + 1)]
            row = jnp.broadcast_to(row[None], (8, 8, 128))
            blocks[column] = jnp.concatenate([made[place], row], axis=-1).astype(bf16)


def make_attend_blocks(core, low, ctx_own, ctx_got, found):
    return pl.pallas_call(
        attend_blocks_kernel,
        in_specs=[pl.BlockSpec(memory_space=pltpu.SMEM)]
        + [pl.BlockSpec(memory_space=pltpu.VMEM)] * 4,
        out_specs=pl.BlockSpec(memory_space=pltpu.VMEM),
        out_shape=pltpu.HBM((8, 8, 8, D + 128), bf16),
        compiler_params=pltpu.CompilerParams(vmem_limit_bytes=32 * 2**20),
        name="attend_blocks",
    )(core, low, ctx_own, ctx_got, found)


def two_parts(value):
    upper = value.astype(bf16)
    return upper, (value - upper.astype(f32)).astype(bf16)


def swap(value):
    return lax.ppermute(value, "core", [(0, 1), (1, 0)])


def swap_chips(value):
    return lax.ppermute(value, "yl", [(0, 1), (1, 0)])


def exchange(value, axes):
    return lax.all_to_all(value, axes, 0, 0, tiled=True)


def shifted(value, axis, size, step):
    return lax.ppermute(value, axis, [(i, (i + step) % size) for i in range(size)])


def stacked(value, axis):
    size = lax.axis_size(axis)
    return jnp.stack([value] + [shifted(value, axis, size, step) for step in range(1, size)])


def places_back(axis):
    size = lax.axis_size(axis)
    return (lax.axis_index(axis) - jnp.arange(size)) % size


def pick(blocks, index):
    return blocks.at[index.reshape(-1)].get(mode="promise_in_bounds")


def spread(value, axes):
    return exchange(jnp.broadcast_to(value[None], (8,) + value.shape), axes)


def gather_projection(rows_t, table_rows, position_rows):
    first = spread(jnp.concatenate([rows_t[:, :512], table_rows], axis=0), GROUP)
    first, second = lax.optimization_barrier((first, rows_t[:, 512:]))
    second = stacked(stacked(second, "x"), "yl").reshape(8 * 24, 512)
    first = jnp.concatenate([first.reshape(256, 512), position_rows], axis=0)
    first, second = lax.optimization_barrier((stacked(first, "yl"), second))
    first = first.reshape(2, 9, 32, 512)
    table = jnp.concatenate([first[:, :8, 24:].reshape(2, 64, 512), first[:, 8]], axis=1)
    first = stacked(first[:, :8, :24], "x").reshape(8, 8, 24, 512)
    second = spread(second, GROUP).reshape(8, 8, 24, 512)
    table = stacked(table, "x").reshape(8, 96, 512)
    x, yl = places_back("x")[None], places_back("yl")[:, None]
    order = jnp.stack([(yl + 2 * x).reshape(-1), (x + 4 * yl).reshape(-1)])
    table = table.at[order[0]].get(mode="promise_in_bounds")
    return first, second, order, table[:, :64].reshape(512, 512), table[:, 64:]


def pack_kernel(core, expand, reduce, attend, vectors, got, packet):
    first = core[0] == 0
    packet[:32] = expand[...]
    inner = []
    for source in (reduce, got):
        spans = [source[:, 512 * k : 512 * (k + 1)].astype(f32) for k in range(8)]
        inner.append([jnp.where(first, span[:, :256], span[:, 256:]) for span in spans])
    for half in range(2):
        parts = [jnp.concatenate(rows_in[4 * half : 4 * half + 4], axis=1) for rows_in in inner]
        low, high = jnp.where(first, *parts), jnp.where(first, *reversed(parts))
        joined = jnp.concatenate([low, high], axis=0).astype(bf16)
        packet[32 + 16 * half : 48 + 16 * half] = joined
    own, other = attend[...].astype(f32), got[:, FF : FF + D].astype(f32)
    joined = jnp.concatenate([jnp.where(first, own, other), jnp.where(first, other, own)], axis=0)
    packet[64:80] = joined.astype(bf16)
    own, other = vectors[:4].astype(f32), got[:4, FF + D :].astype(f32)
    joined = jnp.concatenate([jnp.where(first, own, other), jnp.where(first, other, own)], axis=0)
    packet[80:] = jnp.concatenate([joined, jnp.zeros((8, D - 128), f32)], axis=1).astype(bf16)


def pack(core, expand, reduce, attend, vectors, got):
    return pl.pallas_call(
        pack_kernel,
        in_specs=[pl.BlockSpec(memory_space=pltpu.SMEM)]
        + [pl.BlockSpec(memory_space=pltpu.VMEM)] * 5,
        out_specs=pl.BlockSpec(memory_space=pltpu.VMEM),
        out_shape=jax.ShapeDtypeStruct((88, D), bf16),
        compiler_params=pltpu.CompilerParams(vmem_limit_bytes=60 * 2**20),
        name="pack",
    )(core, expand, reduce, attend, vectors, got)


def project_kernel(order, mine, theirs, first, second, packed, rows_out):
    tokens = jnp.concatenate([mine[...], theirs[...]], axis=0)
    low = first[0].astype(f32).reshape(192, 512).astype(bf16)
    high = second[:, 0].astype(f32).reshape(192, 512).astype(bf16)
    made = dot_nt(tokens[:, :512], low) + dot_nt(tokens[:, 512:], high)
    packed[0] = made.astype(bf16)
    rows_out[:, :512] = low
    rows_out[:, 512:] = high


def project(order, mine, theirs, first, second):
    return pl.pallas_call(
        project_kernel,
        grid_spec=pltpu.PrefetchScalarGridSpec(
            num_scalar_prefetch=1,
            grid=(8,),
            in_specs=[
                pl.BlockSpec((128, D), lambda k, order: (0, 0)),
                pl.BlockSpec((128, D), lambda k, order: (0, 0)),
                pl.BlockSpec((1, 8, 24, 512), lambda k, order: (order[0, k], 0, 0, 0)),
                pl.BlockSpec((8, 1, 24, 512), lambda k, order: (0, order[1, k], 0, 0)),
            ],
            out_specs=[
                pl.BlockSpec((1, 256, 192), lambda k, order: (k, 0, 0)),
                pl.BlockSpec((192, D), lambda k, order: (k, 0)),
            ],
        ),
        out_shape=[
            jax.ShapeDtypeStruct((8, 256, 192), bf16),
            pltpu.HBM((1536, D), bf16),
        ],
        compiler_params=pltpu.CompilerParams(vmem_limit_bytes=32 * 2**20),
        name="project",
    )(order, mine, theirs, first, second)


def arrange_kernel(core, mine, theirs, heads):
    for column in range(8):
        own, other = mine[column].astype(f32), theirs[column].astype(f32)
        first = core[0] == 0
        joined = jnp.concatenate(
            [jnp.where(first, own, other), jnp.where(first, other, own)], axis=1
        )
        for place in range(3):
            chunk = 3 * column + place
            heads[chunk % 8, chunk // 8] = joined[:, 128 * place : 128 * (place + 1)].astype(bf16)


def arrange(core, mine, theirs):
    return pl.pallas_call(
        arrange_kernel,
        in_specs=[
            pl.BlockSpec(memory_space=pltpu.SMEM),
            pl.BlockSpec(memory_space=pltpu.VMEM),
            pl.BlockSpec(memory_space=pltpu.VMEM),
        ],
        out_specs=pl.BlockSpec(memory_space=pltpu.VMEM),
        out_shape=jax.ShapeDtypeStruct((8, 3, 128, 128), bf16),
        compiler_params=pltpu.CompilerParams(vmem_limit_bytes=32 * 2**20),
        name="arrange",
    )(core, mine, theirs)


def project_grad_kernel(
    keep, got, keep_pair, got_pair, tokens_own, tokens_got, tokens_pair, table, blocks
):
    tokens = jnp.concatenate([tokens_own[...], tokens_got[...], tokens_pair[...]], axis=0)
    for step in range(2):
        span = slice(384 * step, 384 * (step + 1))
        parts = [part[:, span] for part in (keep, got, keep_pair, got_pair)]
        made = dot_tn(jnp.concatenate(parts, axis=0), tokens).reshape(16, 24, D)
        rest = table[128 * step : 128 * (step + 1)].reshape(16, 8, 512)
        made = jnp.concatenate([made[..., :512], made[..., 512:], rest], axis=1)
        blocks[16 * step : 16 * (step + 1)] = made.astype(bf16)


def project_grad(keep, got, keep_pair, got_pair, tokens_own, tokens_got, tokens_pair, table):
    return pl.pallas_call(
        project_grad_kernel,
        in_specs=[pl.BlockSpec(memory_space=pltpu.VMEM)] * 8,
        out_specs=pl.BlockSpec(memory_space=pltpu.VMEM),
        out_shape=jax.ShapeDtypeStruct((32, 56, 512), bf16),
        compiler_params=pltpu.CompilerParams(vmem_limit_bytes=48 * 2**20),
        name="project_grad",
    )(keep, got, keep_pair, got_pair, tokens_own, tokens_got, tokens_pair, table)


def ring_scatter(blocks, axis, size, dtype=f32):
    place = lax.axis_index(axis)
    total = lax.dynamic_index_in_dim(blocks, place, 0, keepdims=False).astype(f32)
    for step in range(1, size):
        sent = lax.dynamic_index_in_dim(blocks, (place + step) % size, 0, keepdims=False)
        total = total + shifted(sent, axis, size, step).astype(f32)
    return total.astype(dtype)


def y_scatter(blocks):
    place = 2 * lax.axis_index("yh") + lax.axis_index("yl")
    total = lax.dynamic_index_in_dim(blocks, place, 0, keepdims=False).astype(f32)

    def on_mesh(y):
        return 2 * (y % 2) + y // 2

    for step in range(1, 4):
        sent = lax.dynamic_index_in_dim(blocks, (place + step) % 4, 0, keepdims=False)
        ring = [(on_mesh(y), on_mesh((y + step) % 4)) for y in range(4)]
        total = total + lax.ppermute(sent, ("yl", "yh"), ring).astype(f32)
    return total


def split_kernel(core, heads, keep, give):
    for column in range(8):
        chunks = [3 * column + place for place in range(3)]
        joined = jnp.concatenate(
            [heads[chunk % 8, chunk // 8].astype(f32) for chunk in chunks], axis=1
        )
        first = core[0] == 0
        zero, one = joined[:, :192], joined[:, 192:]
        span = slice(192 * column, 192 * (column + 1))
        keep[:, span] = jnp.where(first, zero, one).astype(bf16)
        give[:, span] = jnp.where(first, one, zero).astype(bf16)


def split(core, heads):
    return pl.pallas_call(
        split_kernel,
        in_specs=[
            pl.BlockSpec(memory_space=pltpu.SMEM),
            pl.BlockSpec(memory_space=pltpu.VMEM),
        ],
        out_specs=[pl.BlockSpec(memory_space=pltpu.VMEM)] * 2,
        out_shape=[jax.ShapeDtypeStruct((128, 1536), bf16)] * 2,
        compiler_params=pltpu.CompilerParams(vmem_limit_bytes=32 * 2**20),
        name="split",
    )(core, heads)


def per_device(
    tokens,
    w_project,
    w_attend,
    first_gain,
    first_shift,
    w_expand,
    w_reduce,
    second_gain,
    second_shift,
    position_table,
    w_query,
    w_key,
    lengths,
    cotangent,
):
    core = lax.axis_index("core")
    group = lax.axis_index(GROUP)
    local = tokens.shape[0]
    core_id = core.reshape(1)
    pair = 2 * local
    column_bucket = bucket_values(SEQ - 1 - np.arange(2 * SEQ - 1), SPAN)
    fold = np.append(column_bucket, -1)[None, :] == np.arange(2 * SPAN)[:, None]
    fold = jnp.asarray(fold.astype(np.float32)).astype(bf16)

    def by_core(zero, one):
        return jnp.where(core == 0, zero, one)

    def in_order(mine, theirs):
        return by_core(mine, theirs), by_core(theirs, mine)

    cotangent_got = swap(cotangent)
    tokens_got = swap(tokens)
    weights_own = jnp.concatenate([w_key, w_query], axis=1)
    first, second, order, table_t, position_rows = gather_projection(
        w_project.T,
        position_table.T,
        jnp.concatenate([weights_own[:32], weights_own[32:]], axis=1),
    )
    position_weights = jnp.stack([position_rows[..., :256], position_rows[..., 256:]], axis=1)
    position_weights = position_weights.reshape(512, 256)

    vectors = jnp.stack([first_gain, first_shift, second_gain, second_shift])
    vectors = jnp.pad(vectors, ((0, 4), (0, 128 - 8)))
    reduce_rows = w_reduce.T
    got = swap(jnp.concatenate([reduce_rows, w_attend.T, vectors], axis=1))
    packet = pack(core_id, w_expand.T, reduce_rows, w_attend.T, vectors, got)
    gathered = lax.all_gather(packet, CHIPS, axis=0, tiled=False).reshape(8, 8, 88, D)
    vec = gathered[..., 80:, :8].reshape(8, 8, 2, 4, 8).transpose(3, 1, 2, 0, 4)
    vec = vec.reshape(4, D).astype(f32)
    gain_one, shift_one, gain_two, shift_two = vec[0], vec[1], vec[2], vec[3]

    packed, project_t = project(order, tokens, tokens_got, first, second)
    heads_in = exchange(arrange(core_id, packed[:, :local], swap(packed[:, local:])), GROUP)
    rel = dot_tn(table_t, position_weights)
    rel = dot_tn(fold, (rel + swap(rel)).astype(bf16)).astype(bf16)
    heads_in, tokens_both = lax.optimization_barrier(
        (heads_in, jnp.concatenate([tokens, tokens_got], axis=0))
    )
    tokens_pair = swap_chips(tokens_both)
    context, kept = attend(lengths, heads_in, rel)
    context, tokens_pair = lax.optimization_barrier(
        (exchange(context, GROUP), tokens_pair)
    )
    context_got = swap(context)

    resid_own = project_back(context, tokens, gathered)
    resid_got = swap(resid_own)
    activ, slope, ffn_own, ffn_sent = ffn_forward(resid_own, resid_got, vec, gathered)
    output, blocks, grad_own, grad_sent, sums = ffn_backward(
        core_id,
        resid_own,
        resid_got,
        vec,
        ffn_own,
        swap(ffn_sent),
        cotangent,
        cotangent_got,
        activ,
        swap(activ),
        slope,
        gathered,
    )
    grad_resid1, grad_context, grad_attended, sums = first_backward(
        resid_own, resid_got, vec, grad_own, swap(grad_sent), sums, gathered
    )
    attend_blocks = make_attend_blocks(core_id, grad_attended, context, context_got, sums)

    summed = lax.psum_scatter(
        blocks.reshape(16, 4 * 64, D), ("x", "z"), scatter_dimension=0, tiled=True
    )
    attend_blocks, grad_ctx = lax.optimization_barrier(
        (attend_blocks, exchange(grad_context, GROUP))
    )
    attend_sum = exchange(attend_blocks.reshape(64, 8, D + 128), COLUMN + GROUP)

    grads, rel_grad = attend_back(heads_in, rel, grad_ctx, kept)
    grads, attend_sum = lax.optimization_barrier((grads, attend_sum))
    attend_sum = jnp.sum(attend_sum.astype(f32), axis=0)
    grad_attend = attend_sum[:, :D].T
    vectors = attend_sum[:4, D:].reshape(4, 16, 8)
    vectors = lax.dynamic_index_in_dim(vectors, 8 * core + group, axis=1, keepdims=False)
    grads = exchange(grads, GROUP)
    yl = lax.axis_index("yl")
    rel_grad = sum(dot_nn(fold, part) for part in two_parts(rel_grad))
    rel_grad = rel_grad + swap(rel_grad.astype(bf16)).astype(f32)
    rel_grad = two_parts(rel_grad + swap_chips(rel_grad.astype(bf16)).astype(f32))
    table_half = lax.dynamic_slice_in_dim(table_t, 256 * yl, 256, axis=0)
    weights_half = lax.dynamic_slice_in_dim(position_weights, 256 * yl, 256, axis=0)
    position_grads = sum(dot_nn(table_half, part) for part in rel_grad)
    position_grads = ring_scatter(position_grads.reshape(4, 64, 256), "x", 4)
    table_blocks = sum(dot_nt(weights_half, part) for part in rel_grad)

    def by_chip(value):
        low, high = value[:, :768], value[:, 768:]
        return jnp.where(yl == 0, low, high), jnp.where(yl == 0, high, low)

    grads, position_grads = lax.optimization_barrier((grads, position_grads))
    keep, give = split(core_id, grads)
    keep_half, keep_other = by_chip(keep)
    got = swap(give)
    got_half, got_other = by_chip(got)
    blocks = project_grad(
        keep_half,
        got_half,
        swap_chips(keep_other),
        swap_chips(got_other),
        tokens,
        tokens_got,
        tokens_pair,
        table_blocks,
    )
    blocks, got = lax.optimization_barrier((blocks, got))
    tokens_part = dot_nn(keep, project_t)
    tokens_sent = dot_nn(got, project_t).astype(bf16)
    tokens_sent, tokens_part, summed = lax.optimization_barrier(
        (tokens_sent, grad_resid1 + tokens_part, summed)
    )
    received, summed, tokens_back = lax.optimization_barrier(
        (
            exchange(blocks, ("x",) + GROUP),
            y_scatter(summed.reshape(4, 64, D)),
            swap(tokens_sent),
        )
    )
    grad_expand = summed[:32].T
    grad_reduce = summed[32:64].reshape(4, 8, D).transpose(1, 0, 2).reshape(8, FF).T
    received = jnp.sum(received.astype(f32), axis=0)
    grad_project = jnp.concatenate([received[:24], received[24:48]], axis=1).T
    grad_table = received[48:].T
    tokens_grad = tokens_part + tokens_back
    grad_key, grad_query = position_grads[:, :128], position_grads[:, 128:]

    return (
        output,
        tokens_grad.astype(bf16),
        grad_project,
        grad_attend,
        vectors[0],
        vectors[1],
        grad_expand,
        grad_reduce,
        vectors[2],
        vectors[3],
        grad_table,
        grad_query,
        grad_key,
    )


def solution(mesh):
    parts = Mesh(mesh.devices.reshape(2, 4, 2, 4, 2), EVERY)
    in_specs = (
        P(EVERY, None),
        P(None, EVERY),
        P(None, EVERY),
        P(EVERY),
        P(EVERY),
        P(None, EVERY),
        P(None, EVERY),
        P(EVERY),
        P(EVERY),
        P(None, EVERY),
        P(DP, GROUP),
        P(DP, GROUP),
        P(DP),
        P(EVERY, None),
    )
    out_specs = (
        P(EVERY, None),
        P(EVERY, None),
        P(None, EVERY),
        P(None, EVERY),
        P(EVERY),
        P(EVERY),
        P(None, EVERY),
        P(None, EVERY),
        P(EVERY),
        P(EVERY),
        P(None, EVERY),
        P(DP, GROUP),
        P(DP, GROUP),
    )
    return jax.shard_map(
        per_device, mesh=parts, in_specs=in_specs, out_specs=out_specs, check_vma=False
    )
```
